32 devices in a mesh: group: 2 (over y), chan: 4 (over z), tm: 2 (over x), beam: 2 (over core).
Axes of the slice: x: 2, y: 2, z: 4, core: 2. Of those that a mesh axis runs over, the one named last changes fastest.
Arguments:
- samples: bfloat16 [1024, 2, 1024, 16], P(('group', 'chan', 'beam'), None, None, 'tm'), parts along dimension 0, may hold values from -6 to 6
- window_taps: float32 [4, 1024], replicated, may hold values from -1 to 1
- sky_model: bfloat16 [1024, 2, 512, 512], P(('group', 'chan', 'tm'), None, 'beam'), parts along dimension 0, may hold values from -0.0234375 to 0.0234375
- prior_gains: float32 [1024, 2, 512], P(('group', 'chan', 'tm')), parts along dimension 0, may hold values from -4.2 to 4.2
- beam_steering: int32 [2, 1024], P(None, ('group', 'beam')), parts along dimension 1, may hold values from 0 to 255
- input_flags: int32 [1024, 512], P(('group', 'chan', 'tm')), parts along dimension 0, may hold values 0 or 1
Outputs:
- visibilities: bfloat16 [1024, 2, 512, 512], P(('group', 'chan', 'tm'), None, 'beam'), parts along dimension 0
- new_gains: float32 [1024, 2, 512], P(('group', 'chan', 'tm'), None, 'beam'), parts along dimension 0
- beam_power: float32 [1024, 512, 16], P(('group', 'chan', 'tm'), 'beam'), parts along dimension 0
The draws below stay inside these ranges and needn't reach their ends.
There are 2 independent parts, one for each index of `group`. The reference program is written for one: setup_inputs(seed, part) draws one part's arguments, and reference() takes and returns one part's arrays. A program takes and returns all parts, laid end to end along the dimension named above; an argument that names none is the same for every part. Nothing has to cross between parts.
All inputs are finite; a program needn't handle non-finite values. No bound on the sum of `input_flags` on one device may be relied on, other than what follows from the above.
Results may differ from the reference program's by a relative error of at most 0.0076.
Values may be sent and summed in bfloat16 or wider, within the bound.
No kernel may reach another device: no remote copies, remote signals or barrier semaphores. Data moves between devices by JAX's collectives and lax.ppermute only.
A program may use at most 384 MiB of HBM per device.

```python
import math
import jax
import jax.numpy as jnp
from jax import lax

NIN = 512
NFFT = 1024
NCH = 512
PT = 4
NBEAM = 512
ITERS = 2
FRAMES = 16


def touch_ends(drawn, key, smallest, top_value):
    index_at = [jax.random.randint(jax.random.fold_in(key, axis), (), 0, length) for axis, length in enumerate(drawn.shape)]
    widest = drawn.shape.index(max(drawn.shape))
    next_to = index_at[:widest] + [(index_at[widest] + 1) % drawn.shape[widest]] + index_at[widest + 1:]
    return drawn.at[tuple(index_at)].set(smallest).at[tuple(next_to)].set(top_value)


def shard_levels(own_key, dims, pieces, low, top_value):
    def one(dim, blocks):
        steps = jax.random.uniform(jax.random.fold_in(jax.random.fold_in(own_key, 6), dim), (blocks,), jnp.float32, low / len(pieces), top_value / len(pieces))
        return jnp.repeat(jnp.exp(steps), dims[dim] // blocks).reshape((-1,) + (1,) * (len(dims) - dim - 1))

    level = one(*pieces[0])
    for cut in pieces[1:]:
        level = level * one(*cut)
    return level


def noise(stream_key, dims, spread, bound, cuts=(), kind=jnp.bfloat16):
    array = spread * jax.random.normal(stream_key, dims, jnp.float32)
    if cuts:
        array = array * shard_levels(stream_key, dims, cuts, -0.22, 0.18)
    return jnp.clip(array, -bound, bound).astype(kind)


def setup_inputs(seed: int = 0, part: int = 0) -> dict:
    arg_keys = jax.random.split(jax.random.key(seed), 7)
    part_splits = jax.random.split(jax.random.fold_in(arg_keys[6], part), 7)
    return {
        "samples": noise(part_splits[0], (NIN, 2, NFFT, FRAMES), 1.0, 6.0, ((0, 8), (3, 2))),
        "window_taps": jnp.clip(jax.random.uniform(arg_keys[1], (PT, NFFT), jnp.float32, -1.0, 1.0), -1.0, 1.0),
        "sky_model": noise(part_splits[2], (NCH, 2, NIN, NIN), (NIN * NIN // 4) ** -0.5, 0.0234375, ((0, 8), (2, 2))),
        "prior_gains": noise(part_splits[3], (NCH, 2, NIN), 0.7, 4.2, ((0, 8),), jnp.float32),
        "beam_steering": touch_ends(jax.random.randint(part_splits[4], (2, NBEAM), 0, 256), jax.random.fold_in(part_splits[4], 1), 0, 255).astype(jnp.int32),
        "input_flags": touch_ends((jax.random.randint(part_splits[5], (NCH, NIN), 0, 16) < 15).astype(jnp.int32), jax.random.fold_in(part_splits[5], 1), 0, 1),
    }


damping = 0.5
epsilon = 1e-06

def pfb_table(window_taps, kept_count):
    transform_count = window_taps.shape[1]
    kept = jnp.arange(kept_count, dtype=jnp.int32)
    indices = jnp.arange(transform_count, dtype=jnp.int32)
    phases = (kept[:, None] * indices[None, :] % transform_count).astype(jnp.float32) * (2.0 * math.pi / transform_count)
    cosine = jnp.cos(phases)
    sine_part = jnp.sin(phases)
    real_row = jnp.concatenate([cosine, sine_part], axis=1)
    imag_row = jnp.concatenate([-sine_part, cosine], axis=1)
    base_matrix = jnp.stack([real_row, imag_row], axis=1).reshape(2 * kept_count, 2 * transform_count)
    doubled = jnp.concatenate([window_taps, window_taps], axis=1)
    return (base_matrix[None] * doubled[:, None, :] / math.sqrt(transform_count)).astype(jnp.bfloat16)

def steering_angles(beam_steering, channels, input_count, chan_total):
    positions = jnp.arange(input_count, dtype=jnp.int32)
    column = positions // (input_count // 4)
    within = positions % (input_count // 4)
    phase_index = (beam_steering[0][:, None] * column[None, :] * 64 + beam_steering[1][:, None] * within[None, :]) % 256
    scaled = phase_index[None] * (chan_total + channels)[:, None, None]
    return scaled.astype(jnp.float32) * (2.0 * math.pi / (512 * chan_total))

def reference(samples, window_taps, sky_model, prior_gains, beam_steering, input_flags):
    coeff_table = pfb_table(window_taps, NCH).astype(jnp.float32)
    stacked = samples.reshape(NIN, 2 * NFFT, FRAMES)
    group_size = math.gcd(NIN, 32)
    grouped = stacked.reshape(NIN // group_size, group_size, 2 * NFFT, FRAMES)

    def filter_group(group_block):
        values = jnp.pad(group_block.astype(jnp.float32), ((0, 0), (0, 0), (PT - 1, 0)))
        running = jnp.zeros((group_size, 2 * NCH, FRAMES), jnp.float32)
        for tap_index in range(PT):
            running = running + jnp.einsum('ab,ibf->iaf', coeff_table[tap_index], values[:, :, tap_index:tap_index + FRAMES], precision=lax.Precision.HIGHEST)
        return running.astype(jnp.bfloat16)
    spectra = lax.map(filter_group, grouped).reshape(NIN, NCH, 2, FRAMES)
    by_channel = jnp.transpose(spectra, (1, 0, 2, 3))
    channels = jnp.arange(NCH, dtype=jnp.int32)
    highest = lax.Precision.HIGHEST

    def one_channel(channel_items):
        channel_spectrum, model_part, gains_part, flags_part, channel = channel_items
        values = channel_spectrum.astype(jnp.float32)
        paired = values.reshape(NIN, 2 * FRAMES)
        rotated = jnp.stack([values[:, 1], -values[:, 0]], axis=1).reshape(NIN, 2 * FRAMES)
        vis_real = jnp.dot(paired, paired.T, precision=highest) / FRAMES
        vis_imag = jnp.dot(rotated, paired.T, precision=highest) / FRAMES
        vis_stored = jnp.stack([vis_real, vis_imag]).astype(jnp.bfloat16)
        vis_used = lax.optimization_barrier(vis_stored).astype(jnp.float32)
        model_values = model_part.astype(jnp.float32)
        weighted_real = vis_used[0] * model_values[0] + vis_used[1] * model_values[1]
        weighted_imag = vis_used[1] * model_values[0] - vis_used[0] * model_values[1]
        model_power = model_values[0] * model_values[0] + model_values[1] * model_values[1]
        weights = flags_part.astype(jnp.float32)
        current = gains_part
        for step_index in range(ITERS):
            masked_real = current[0] * weights
            masked_imag = current[1] * weights
            numer_real = jnp.dot(weighted_real, masked_real, precision=highest) - jnp.dot(weighted_imag, masked_imag, precision=highest)
            numer_imag = jnp.dot(weighted_real, masked_imag, precision=highest) + jnp.dot(weighted_imag, masked_real, precision=highest)
            denom = jnp.dot(model_power, weights * (current[0] * current[0] + current[1] * current[1]), precision=highest) + epsilon
            current = damping * current + (1.0 - damping) * jnp.stack([numer_real / denom, numer_imag / denom])
        angles = steering_angles(beam_steering, channel[None], NIN, NCH)[0]
        cosine = jnp.cos(angles)
        sine_part = jnp.sin(angles)
        scale_factor = 1.0 / math.sqrt(NIN)
        gain_real = (gains_part[0] * weights)[None, :]
        gain_imaginary = (gains_part[1] * weights)[None, :]
        steering_real = ((gain_real * cosine - gain_imaginary * sine_part) * scale_factor).astype(jnp.bfloat16).astype(jnp.float32)
        steering_imaginary = ((gain_real * sine_part + gain_imaginary * cosine) * scale_factor).astype(jnp.bfloat16).astype(jnp.float32)
        volt_real = jnp.dot(steering_real, values[:, 0], precision=highest) - jnp.dot(steering_imaginary, values[:, 1], precision=highest)
        volt_imag = jnp.dot(steering_real, values[:, 1], precision=highest) + jnp.dot(steering_imaginary, values[:, 0], precision=highest)
        power = volt_real * volt_real + volt_imag * volt_imag
        return (vis_stored, current, power)
    results = lax.map(one_channel, (by_channel, sky_model, prior_gains, input_flags, channels))
    return (results[0], results[1], results[2])
```

```python
import functools
import math

import jax
import jax.numpy as jnp
import numpy as np
from jax import lax
from jax.experimental import pallas as pl
from jax.experimental.pallas import tpu as pltpu
from jax.sharding import PartitionSpec as P

NCH = 512
ITERS = 2


damping = 0.5
epsilon = 1e-06


def from_behind(block, axis, distance):
    devices = range(lax.axis_size(axis))
    route = [(i - distance, i) for i in devices if i - distance in devices]
    return lax.ppermute(block, axis, route)


def filter_bank(extended, window_taps, kept_count, frames):
    transform_count = window_taps.shape[1]
    tap_count = window_taps.shape[0]
    local_inputs = extended.shape[0]
    kept = jnp.arange(kept_count, dtype=jnp.int32)
    indices = jnp.arange(transform_count, dtype=jnp.int32)
    phases = (kept[:, None] * indices[None, :] % transform_count).astype(jnp.float32) * (
        2.0 * math.pi / transform_count
    )
    cosine = jnp.cos(phases)
    sine_part = jnp.sin(phases)
    real_in = extended[:, :transform_count]
    imag_in = extended[:, transform_count:]
    real_sum = jnp.zeros((local_inputs, kept_count, frames), jnp.float32)
    imag_sum = jnp.zeros((local_inputs, kept_count, frames), jnp.float32)
    for tap_index in range(tap_count):
        tap_row = window_taps[tap_index][None, :]
        cos_block = (cosine * tap_row / math.sqrt(transform_count)).astype(jnp.bfloat16)
        sin_block = (sine_part * tap_row / math.sqrt(transform_count)).astype(jnp.bfloat16)
        part_real = real_in[:, :, tap_index : tap_index + frames]
        part_imag = imag_in[:, :, tap_index : tap_index + frames]
        real_sum = (
            real_sum
            + jnp.einsum("kn,inf->ikf", cos_block, part_real, preferred_element_type=jnp.float32)
            + jnp.einsum("kn,inf->ikf", sin_block, part_imag, preferred_element_type=jnp.float32)
        )
        imag_sum = (
            imag_sum
            + jnp.einsum("kn,inf->ikf", cos_block, part_imag, preferred_element_type=jnp.float32)
            - jnp.einsum("kn,inf->ikf", sin_block, part_real, preferred_element_type=jnp.float32)
        )
    return jnp.stack([real_sum, imag_sum], axis=2).astype(jnp.bfloat16)


def steering_angles(beam_steering, channels, input_count, chan_total):
    positions = jnp.arange(input_count, dtype=jnp.int32)
    column = positions // (input_count // 4)
    within = positions % (input_count // 4)
    phase_index = (
        beam_steering[0][:, None] * column[None, :] * 64
        + beam_steering[1][:, None] * within[None, :]
    ) % 256
    scaled = phase_index[None] * (chan_total + channels)[:, None, None]
    return scaled.astype(jnp.float32) * (2.0 * math.pi / (512 * chan_total))


def cross_rows(owned_rows, all_rows):
    paired = owned_rows.reshape(owned_rows.shape[0], owned_rows.shape[1], -1)
    rotated = jnp.stack([owned_rows[:, :, 1], -owned_rows[:, :, 0]], axis=2).reshape(paired.shape)
    left = jnp.stack([paired, rotated], axis=1)
    columns = all_rows.reshape(all_rows.shape[0], all_rows.shape[1], -1)
    return jnp.einsum("isck,jck->csij", left, columns, preferred_element_type=jnp.float32)


def form_beams(whole_set, gains_part, weights, beam_steering, channels, chan_total):
    input_count = whole_set.shape[0]
    angles = steering_angles(beam_steering, channels, input_count, chan_total)
    cosine = jnp.cos(angles)
    sine_part = jnp.sin(angles)
    scale_factor = 1.0 / math.sqrt(input_count)
    gain_real = (gains_part[:, 0] * weights)[:, None, :]
    gain_imaginary = (gains_part[:, 1] * weights)[:, None, :]
    steering_real = ((gain_real * cosine - gain_imaginary * sine_part) * scale_factor).astype(
        jnp.bfloat16
    )
    steering_imaginary = ((gain_real * sine_part + gain_imaginary * cosine) * scale_factor).astype(
        jnp.bfloat16
    )
    spectrum_real = whole_set[:, :, 0]
    spectrum_imaginary = whole_set[:, :, 1]
    volt_real = jnp.einsum(
        "jan,njg->jag", steering_real, spectrum_real, preferred_element_type=jnp.float32
    ) - jnp.einsum(
        "jan,njg->jag", steering_imaginary, spectrum_imaginary, preferred_element_type=jnp.float32
    )
    volt_imag = jnp.einsum(
        "jan,njg->jag", steering_real, spectrum_imaginary, preferred_element_type=jnp.float32
    ) + jnp.einsum(
        "jan,njg->jag", steering_imaginary, spectrum_real, preferred_element_type=jnp.float32
    )
    return volt_real * volt_real + volt_imag * volt_imag


def matvec(matrix, vector):
    return jnp.einsum("crj,cj->cr", matrix, vector, precision=lax.Precision.HIGHEST)


def general_shards(samples, window_taps, sky_model, prior_gains, beam_steering, input_flags):
    local_inputs = samples.shape[0]
    transform_count = samples.shape[2]
    frames = samples.shape[3]
    tap_count = window_taps.shape[0]
    kept_count = NCH
    time_count = lax.axis_size("tm")
    beam_count = lax.axis_size("beam")
    time_index = lax.axis_index("tm")
    beam_index = lax.axis_index("beam")
    chan_index = lax.axis_index("chan")
    weights = input_flags.astype(jnp.float32)
    stacked = samples.reshape(local_inputs, 2 * transform_count, frames)
    previous = from_behind(stacked[:, :, frames - tap_count + 1 :], "tm", 1)
    extended = jnp.concatenate([previous, stacked], axis=2)
    spectra = filter_bank(extended, window_taps, kept_count, frames).reshape(
        1, local_inputs, kept_count, 2, 1, frames
    )
    mixed = lax.all_to_all(spectra, ("chan", "tm"), split_axis=2, concat_axis=0, tiled=True)
    blocks = mixed.reshape(
        mixed.shape[0] // time_count, time_count, local_inputs, mixed.shape[2], 2, frames
    )
    turned = jnp.transpose(blocks, (0, 2, 3, 4, 1, 5))
    joined = lax.all_gather(turned, "beam", axis=1, tiled=True)
    input_count = joined.shape[0] * joined.shape[1]
    chan_local = joined.shape[2]
    whole_set = joined.reshape(input_count, chan_local, 2, joined.shape[4] * frames)
    half_rows = input_count // beam_count
    owned_rows = lax.dynamic_slice_in_dim(whole_set, beam_index * half_rows, half_rows, 0)
    terms = cross_rows(owned_rows, whole_set)
    visibilities = (terms / whole_set.shape[3]).astype(jnp.bfloat16)
    channels = (chan_index * time_count + time_index) * chan_local + jnp.arange(
        chan_local, dtype=jnp.int32
    )
    beam_power = form_beams(whole_set, prior_gains, weights, beam_steering, channels, kept_count)
    vis_used = lax.optimization_barrier(visibilities).astype(jnp.float32)
    model_values = sky_model.astype(jnp.float32)
    weighted = jnp.stack(
        [
            vis_used[:, 0] * model_values[:, 0] + vis_used[:, 1] * model_values[:, 1],
            vis_used[:, 1] * model_values[:, 0] - vis_used[:, 0] * model_values[:, 1],
        ],
        axis=1,
    )
    model_power = model_values[:, 0] * model_values[:, 0] + model_values[:, 1] * model_values[:, 1]
    row_start = beam_index * half_rows
    current = prior_gains
    updated = lax.dynamic_slice_in_dim(current, row_start, half_rows, 2)
    for step_index in range(ITERS):
        masked_real = current[:, 0] * weights
        masked_imag = current[:, 1] * weights
        vectors = jnp.stack([masked_real, masked_imag], axis=2)
        products = jnp.einsum("csrj,cjv->csrv", weighted, vectors, precision=lax.Precision.HIGHEST)
        numer_real = products[:, 0, :, 0] - products[:, 1, :, 1]
        numer_imag = products[:, 0, :, 1] + products[:, 1, :, 0]
        denom = (
            matvec(
                model_power,
                weights * (current[:, 0] * current[:, 0] + current[:, 1] * current[:, 1]),
            )
            + epsilon
        )
        older = lax.dynamic_slice_in_dim(current, row_start, half_rows, 2)
        updated = damping * older + (1.0 - damping) * jnp.stack(
            [numer_real / denom, numer_imag / denom], axis=1
        )
        if step_index + 1 < ITERS:
            current = lax.all_gather(updated, "beam", axis=2, tiled=True)
    return (visibilities, updated, beam_power)


LANES = 128
SUBLANES = 8
NEXT_ROWS = 4
MIB = 2**20
NT = (((1,), (1,)), ((), ()))
TN = (((0,), (0,)), ((), ()))
NN = (((1,), (0,)), ((), ()))


def mxu(left, right, dims):
    return lax.dot_general(left, right, dims, preferred_element_type=jnp.float32)


def transform_rows(kept_count, transform_count, owners, chunks):
    kept = np.arange(kept_count).reshape(owners, chunks, -1).transpose(1, 0, 2).reshape(-1)
    phases = (kept[:, None] * np.arange(transform_count)[None, :] % transform_count) * (
        2.0 * math.pi / transform_count
    )
    table = np.concatenate([np.cos(phases), np.sin(phases)], axis=1) / math.sqrt(transform_count)
    return jnp.asarray(table.astype(jnp.bfloat16))


def filter_kernel(owners, x_ref, taps_ref, table_ref, *refs):
    *out_refs, here_ref, next_ref, windowed_ref, turned_ref, spill_ref = refs
    inputs, _, frames, points = x_ref.shape
    taps = taps_ref.shape[0]
    width = 2 * inputs
    frame_of = lax.broadcasted_iota(jnp.int32, (frames, points), 0)
    here_weights = []
    next_weights = []
    for tap in range(taps):
        shift = taps - 1 - tap
        row = jnp.broadcast_to(taps_ref[tap : tap + 1, :], (frames, points))
        here_weights.append(jnp.where(frame_of >= shift, row, 0.0))
        next_weights.append(jnp.where(frame_of < shift, row, 0.0))

    def window(i, carry):
        for part in range(2):
            block = x_ref[i, part].astype(jnp.float32)
            here = block * here_weights[taps - 1]
            later = jnp.zeros_like(block)
            for tap in range(taps - 1):
                rolled = pltpu.roll(block, taps - 1 - tap, 0)
                here = here + rolled * here_weights[tap]
                later = later + rolled * next_weights[tap]
            for piece in range(points // LANES):
                lanes = slice(piece * LANES, (piece + 1) * LANES)
                here_ref[part, piece, pl.ds(i * frames, frames), :] = here[:, lanes]
                next_ref[part, piece, pl.ds(i * frames, frames), :] = later[:, lanes]
        return carry

    lax.fori_loop(0, inputs, window, 0)
    for frame in range(frames + taps - 1):
        source = here_ref if frame < frames else next_ref
        first = frame % frames
        for piece in range(points // LANES):
            lanes = slice(piece * LANES, (piece + 1) * LANES)
            upper = slice(points + piece * LANES, points + (piece + 1) * LANES)
            real = source[0, piece, pl.ds(first, inputs, stride=frames), :].astype(jnp.bfloat16)
            imag = source[1, piece, pl.ds(first, inputs, stride=frames), :].astype(jnp.bfloat16)
            base = frame * width
            windowed_ref[base : base + inputs, lanes] = real
            windowed_ref[base : base + inputs, upper] = imag
            windowed_ref[base + inputs : base + width, lanes] = imag
            windowed_ref[base + inputs : base + width, upper] = -real
    rows = table_ref.shape[0] // len(out_refs)
    share = rows // owners
    for chunk, out_ref in enumerate(out_refs):
        block = mxu(table_ref[chunk * rows : (chunk + 1) * rows, :], windowed_ref[...], NT)
        for frame in range(frames):
            turned_ref[pl.ds(frame, rows, stride=frames), :] = block[
                :, frame * width : (frame + 1) * width
            ]
        for frame in range(NEXT_ROWS):
            at = (frames + frame) * width
            if frame < taps - 1:
                part = block[:, at : at + width]
            else:
                part = jnp.zeros((rows, width), jnp.float32)
            spill_ref[pl.ds(frame, rows, stride=NEXT_ROWS), :] = part
        main = share * frames
        for owner in range(owners):
            out_ref[owner, :main, :] = turned_ref[owner * main : (owner + 1) * main, :].astype(
                jnp.bfloat16
            )
            extra = share * NEXT_ROWS
            out_ref[owner, main : main + extra, :] = spill_ref[
                owner * extra : (owner + 1) * extra, :
            ].astype(jnp.bfloat16)


def filtered(samples, window_taps, kept_count, owners, chunks):
    inputs, _, points, frames = samples.shape
    taps = window_taps.shape[0]
    width = 2 * inputs
    rows = kept_count // chunks
    table = transform_rows(kept_count, points, owners, chunks)
    by_frame = jnp.transpose(samples, (0, 1, 3, 2))
    out = jax.ShapeDtypeStruct(
        (owners, rows // owners * (frames + NEXT_ROWS), width), jnp.bfloat16
    )
    pieces = points // LANES
    return pl.pallas_call(
        functools.partial(filter_kernel, owners),
        out_shape=[out] * chunks,
        in_specs=[pl.BlockSpec(memory_space=pltpu.VMEM)] * 3,
        out_specs=[pl.BlockSpec(memory_space=pltpu.VMEM)] * chunks,
        scratch_shapes=[
            pltpu.VMEM((2, pieces, inputs * frames, LANES), jnp.float32),
            pltpu.VMEM((2, pieces, inputs * frames, LANES), jnp.float32),
            pltpu.VMEM(((frames + taps - 1) * width, 2 * points), jnp.bfloat16),
            pltpu.VMEM((rows * frames, width), jnp.float32),
            pltpu.VMEM((rows * NEXT_ROWS, width), jnp.float32),
        ],
        compiler_params=pltpu.CompilerParams(vmem_limit_bytes=48 * MIB),
        name="filter",
    )(by_frame, window_taps, table)


def gain_terms(real, imag, gains, flags):
    weights = flags.astype(jnp.float32)
    gain_real = gains[0:1] * weights
    gain_imag = gains[1:2] * weights
    turned_real = real * gain_real + imag * gain_imag
    turned_imag = imag * gain_real - real * gain_imag
    power = weights * (gains[0:1] * gains[0:1] + gains[1:2] * gains[1:2])
    return turned_real, turned_imag, power


def updated_gains(real, imag, own_real, own_imag, model_real, model_imag, gains, flags, older):
    turned_real, turned_imag, power = gain_terms(real, imag, gains, flags)
    straight = jnp.concatenate([turned_real, turned_imag], axis=0).astype(jnp.bfloat16)
    crossed = jnp.concatenate([-turned_imag, turned_real], axis=0).astype(jnp.bfloat16)
    modelled = mxu(straight, model_real, NT) + mxu(crossed, model_imag, NT)
    model_power = model_real * model_real + model_imag * model_imag
    power_rows = jnp.broadcast_to(power, (SUBLANES, power.shape[1])).astype(jnp.bfloat16)
    denom = mxu(power_rows, model_power, NT)[0:1] + epsilon
    frames = real.shape[0]
    modelled_real = modelled[:frames]
    modelled_imag = modelled[frames:]
    numer_real = jnp.sum(own_real * modelled_real + own_imag * modelled_imag, axis=0, keepdims=True)
    numer_imag = jnp.sum(own_imag * modelled_real - own_real * modelled_imag, axis=0, keepdims=True)
    numer = jnp.concatenate([numer_real, numer_imag], axis=0) / frames
    return damping * older + (1.0 - damping) * (numer / denom)


def own_half(values, core):
    half = values.shape[1] // 2
    return jnp.where(core == 0, values[:, :half], values[:, half:])


def first_kernel(
    times,
    core_ref,
    own_ref,
    own_next_ref,
    other_ref,
    other_next_ref,
    model_ref,
    gains_ref,
    flags_ref,
    spectra_ref,
    updated_ref,
):
    core = core_ref[0]
    count = gains_ref.shape[0]
    sources = own_ref.shape[0]
    frames = own_ref.shape[1] // count
    width = own_ref.shape[2]
    columns = sources // times
    lane = lax.broadcasted_iota(jnp.int32, (frames, width), 1)
    row = lax.broadcasted_iota(jnp.int32, (frames, width), 0)
    low = lane < width // 2

    def loaded(ref, next_ref, column, time, c):
        source = column * times + time
        block = ref[source, c * frames : (c + 1) * frames, :].astype(jnp.float32)
        if time > 0:
            pair = c // 2 * 2 * NEXT_ROWS
            extra = next_ref[source - 1, pair : pair + 2 * NEXT_ROWS, :].astype(jnp.float32)
            if c % 2:
                extra = pltpu.roll(extra, NEXT_ROWS, 0)
            block = block + jnp.where(row < NEXT_ROWS - 1, extra, 0.0)
        return block

    for c in range(count):
        real_rows = []
        imag_rows = []
        for time in range(times):
            reals = []
            imags = []
            for column in range(columns):
                own = loaded(own_ref, own_next_ref, column, time, c)
                other = loaded(other_ref, other_next_ref, column, time, c)
                first = jnp.where(core == 0, own, other)
                second = jnp.where(core == 0, other, own)
                reals.append(jnp.where(low, first, pltpu.roll(second, width // 2, 1)))
                imags.append(jnp.where(low, pltpu.roll(first, width // 2, 1), second))
            real_rows.append(jnp.concatenate(reals, axis=1))
            imag_rows.append(jnp.concatenate(imags, axis=1))
        spectra = jnp.concatenate(real_rows + imag_rows, axis=0).astype(jnp.bfloat16)
        spectra_ref[c] = spectra
        values = spectra.astype(jnp.float32)
        half = values.shape[0] // 2
        real = values[:half]
        imag = values[half:]
        updated_ref[c] = updated_gains(
            real,
            imag,
            own_half(real, core),
            own_half(imag, core),
            model_ref[c, 0],
            model_ref[c, 1],
            gains_ref[c],
            flags_ref[c : c + 1],
            own_half(gains_ref[c], core),
        )


def second_kernel(
    core_ref, spectra_ref, model_ref, own_ref, other_ref, flags_ref, *refs
):
    visibilities_ref, updated_ref = refs[-2:]
    core = core_ref[0]
    for c in range(spectra_ref.shape[0]):
        spectra = spectra_ref[c]
        half = spectra.shape[0] // 2
        values = spectra.astype(jnp.float32)
        real = values[:half]
        imag = values[half:]
        own_real = own_half(real, core)
        own_imag = own_half(imag, core)
        paired = (jnp.concatenate([own_real, own_imag], axis=0) / half).astype(jnp.bfloat16)
        rotated = (jnp.concatenate([own_imag, -own_real], axis=0) / half).astype(jnp.bfloat16)
        visibilities_ref[c, 0] = mxu(paired, spectra, TN).astype(jnp.bfloat16)
        visibilities_ref[c, 1] = mxu(rotated, spectra, TN).astype(jnp.bfloat16)
        own = own_ref[c]
        other = other_ref[c]
        first = jnp.where(core == 0, own, other)
        second = jnp.where(core == 0, other, own)
        gains = jnp.concatenate([first, second], axis=1)
        updated_ref[c] = updated_gains(
            real,
            imag,
            own_real,
            own_imag,
            model_ref[c, 0],
            model_ref[c, 1],
            gains,
            flags_ref[c : c + 1],
            own,
        )


def series_length(reach):
    terms = 1
    while reach**terms / math.factorial(terms) >= 2.0**-22:
        terms += 1
    return terms


def steering_kernel(terms, reach, step, centre_ref, steering_ref, table_ref):
    inputs = table_ref.shape[1] // 2
    beams = table_ref.shape[2] // 2
    position = lax.broadcasted_iota(jnp.int32, (inputs, beams), 0)
    column = position // (inputs // 4)
    within = position % (inputs // 4)
    phase_index = (steering_ref[0:1, :] * column * 64 + steering_ref[1:2, :] * within) % 256
    angle = (phase_index * centre_ref[0]).astype(jnp.float32) * (0.5 * step)
    cosine = jnp.cos(angle)
    sine_part = jnp.sin(angle)
    offset = (phase_index - 128).astype(jnp.float32) * (reach * step)
    factor = jnp.ones_like(offset)
    for term in range(terms):
        if term:
            factor = factor * offset / term
        real, imag = (
            (cosine, sine_part),
            (-sine_part, cosine),
            (-cosine, -sine_part),
            (sine_part, -cosine),
        )[term % 4]
        real = (factor * real).astype(jnp.bfloat16)
        imag = (factor * imag).astype(jnp.bfloat16)
        table_ref[term, :inputs, :beams] = real
        table_ref[term, :inputs, beams:] = imag
        table_ref[term, inputs:, :beams] = -imag
        table_ref[term, inputs:, beams:] = real


def beams_kernel(spectra_ref, gains_ref, flags_ref, table_ref, *refs):
    power_ref, left_ref = refs[-2:]
    count, doubled, inputs = spectra_ref.shape
    frames = doubled // 2
    scale = 1.0 / math.sqrt(inputs)
    middle = 0.5 * (count - 1)
    terms = table_ref.shape[0]
    for c in range(count):
        values = spectra_ref[c].astype(jnp.float32)
        real = values[:frames]
        imag = values[frames:]
        weights = flags_ref[c : c + 1].astype(jnp.float32) * scale
        gain_real = gains_ref[c, 0:1] * weights
        gain_imag = gains_ref[c, 1:2] * weights
        lit_real = real * gain_real - imag * gain_imag
        lit_imag = real * gain_imag + imag * gain_real
        rows = slice(c * frames, (c + 1) * frames)
        for term in range(terms):
            power = ((c - middle) / max(middle, 0.5)) ** term
            left_ref[term, rows, :inputs] = (lit_real * power).astype(jnp.bfloat16)
            left_ref[term, rows, inputs:] = (lit_imag * power).astype(jnp.bfloat16)
    total = mxu(left_ref[0], table_ref[0], NN)
    for term in range(1, terms):
        total = total + mxu(left_ref[term], table_ref[term], NN)
    beams = total.shape[1] // 2
    real = total[:, :beams]
    imag = total[:, beams:]
    power_ref[...] = (real * real + imag * imag).reshape(count, frames, beams)


def chunk_shards(samples, window_taps, sky_model, prior_gains, beam_steering, input_flags):
    frames = samples.shape[3]
    chan_local, _, half_rows, input_count = sky_model.shape
    times = lax.axis_size("tm")
    owners = lax.axis_size("chan") * times
    core = lax.axis_index("beam")
    kept_count = chan_local * owners
    frame_count = frames * times
    beams = beam_steering.shape[1]
    chunks = CHUNKS
    share = chan_local // chunks
    block = BLOCK
    steps = share // block
    sent = filtered(samples, window_taps, kept_count, owners, chunks)
    core_word = core.astype(jnp.int32).reshape(1)
    swap = [(0, 1), (1, 0)]
    smem = pl.BlockSpec(memory_space=pltpu.SMEM)
    vmem = pl.BlockSpec(memory_space=pltpu.VMEM)
    anywhere = pl.BlockSpec(memory_space=pl.ANY)
    first_channel = (lax.axis_index("chan") * times + lax.axis_index("tm")) * chan_local
    step = 2.0 * math.pi / (512 * kept_count)
    reach = max(0.5 * (share - 1), 0.5)
    terms = series_length(128 * reach * step)
    visibilities = None
    beam_power = None
    gain_parts = []
    for chunk in range(chunks):
        base = chunk * steps
        own = lax.all_to_all(sent[chunk], ("chan", "tm"), 0, 0, tiled=True)
        other = lax.ppermute(own, "beam", swap)
        width = own.shape[2]
        next_base = frames * steps // NEXT_ROWS
        main_spec = pl.BlockSpec((owners, block * frames, width), lambda i: (0, i, 0))
        next_spec = pl.BlockSpec(
            (owners, block * NEXT_ROWS, width), lambda i, at=next_base: (0, at + i, 0)
        )
        model_spec = pl.BlockSpec(
            (block, 2, half_rows, input_count), lambda i, at=base: (at + i, 0, 0, 0)
        )
        gains_spec = pl.BlockSpec((block, 2, input_count), lambda i, at=base: (at + i, 0, 0))
        flags_spec = pl.BlockSpec((block, input_count), lambda i, at=base: (at + i, 0))
        spectra_spec = pl.BlockSpec((block, 2 * frame_count, input_count), lambda i: (i, 0, 0))
        half_spec = pl.BlockSpec((block, 2, half_rows), lambda i: (i, 0, 0))
        half_shape = jax.ShapeDtypeStruct((share, 2, half_rows), jnp.float32)
        spectra, gains_own = pl.pallas_call(
            functools.partial(first_kernel, times),
            grid=(steps,),
            in_specs=[
                smem,
                main_spec,
                next_spec,
                main_spec,
                next_spec,
                model_spec,
                gains_spec,
                flags_spec,
            ],
            out_specs=[spectra_spec, half_spec],
            out_shape=[
                jax.ShapeDtypeStruct((share, 2 * frame_count, input_count), jnp.bfloat16),
                half_shape,
            ],
            compiler_params=pltpu.CompilerParams(vmem_limit_bytes=40 * MIB),
            name="first_update",
        )(core_word, own, own, other, other, sky_model, prior_gains, input_flags)
        gains_other = lax.ppermute(gains_own, "beam", swap)
        centre = 2 * (kept_count + first_channel + chunk * share) + share - 1
        table = pl.pallas_call(
            functools.partial(steering_kernel, terms, reach, step),
            in_specs=[smem, vmem],
            out_specs=vmem,
            out_shape=jax.ShapeDtypeStruct((terms, 2 * input_count, 2 * beams), jnp.bfloat16),
            compiler_params=pltpu.CompilerParams(vmem_limit_bytes=32 * MIB),
            name="steering",
        )(centre.astype(jnp.int32).reshape(1), beam_steering)
        power_spec = pl.BlockSpec(
            (share, frame_count, beams), lambda i, at=chunk: (at, 0, 0)
        )
        earlier = [] if beam_power is None else [beam_power]
        beam_power = pl.pallas_call(
            beams_kernel,
            grid=(1,),
            in_specs=[
                pl.BlockSpec((share, 2 * frame_count, input_count), lambda i: (0, 0, 0)),
                pl.BlockSpec((share, 2, input_count), lambda i, at=chunk: (at, 0, 0)),
                pl.BlockSpec((share, input_count), lambda i, at=chunk: (at, 0)),
                pl.BlockSpec((terms, 2 * input_count, 2 * beams), lambda i: (0, 0, 0)),
            ]
            + [anywhere] * len(earlier),
            out_specs=power_spec,
            out_shape=jax.ShapeDtypeStruct((chan_local, frame_count, beams), jnp.float32),
            input_output_aliases={4: 0} if earlier else {},
            scratch_shapes=[
                pltpu.VMEM((terms, share * frame_count, 2 * input_count), jnp.bfloat16)
            ],
            compiler_params=pltpu.CompilerParams(vmem_limit_bytes=40 * MIB),
            name="beams",
        )(spectra, prior_gains, input_flags, table, *earlier)
        earlier = [] if visibilities is None else [visibilities]
        visibilities, gains_new = pl.pallas_call(
            second_kernel,
            grid=(steps,),
            in_specs=[smem, spectra_spec, model_spec, half_spec, half_spec, flags_spec]
            + [anywhere] * len(earlier),
            out_specs=[model_spec, half_spec],
            out_shape=[
                jax.ShapeDtypeStruct((chan_local, 2, half_rows, input_count), jnp.bfloat16),
                half_shape,
            ],
            input_output_aliases={6: 0} if earlier else {},
            compiler_params=pltpu.CompilerParams(vmem_limit_bytes=40 * MIB),
            name="second_update",
        )(core_word, spectra, sky_model, gains_own, gains_other, input_flags, *earlier)
        gain_parts.append(gains_new)
    return (
        visibilities,
        jnp.concatenate(gain_parts, axis=0),
        jnp.transpose(beam_power, (0, 2, 1)),
    )


CHUNKS = 2
BLOCK = 8


def shards(samples, window_taps, sky_model, prior_gains, beam_steering, input_flags):
    inputs, _, points, frames = samples.shape
    chan_local, _, half_rows, input_count = sky_model.shape
    frame_count = frames * lax.axis_size("tm")
    fits = (
        ITERS == 2
        and 2 * inputs == LANES
        and points % LANES == 0
        and frames == SUBLANES
        and window_taps.shape[0] == NEXT_ROWS
        and lax.axis_size("beam") == 2
        and chan_local % (CHUNKS * BLOCK) == 0
        and half_rows % LANES == 0
        and frame_count & (frame_count - 1) == 0
        and beam_steering.shape[1] % LANES == 0
    )
    form = chunk_shards if fits else general_shards
    return form(samples, window_taps, sky_model, prior_gains, beam_steering, input_flags)


def solution(mesh):
    return jax.shard_map(
        shards,
        mesh=mesh,
        in_specs=(
            P(("group", "chan", "beam"), None, None, "tm"),
            P(),
            P(("group", "chan", "tm"), None, "beam", None),
            P(("group", "chan", "tm"), None, None),
            P(None, ("group", "beam")),
            P(("group", "chan", "tm"), None),
        ),
        out_specs=(
            P(("group", "chan", "tm"), None, "beam", None),
            P(("group", "chan", "tm"), None, "beam"),
            P(("group", "chan", "tm"), "beam", None),
        ),
        check_vma=False,
    )
```

```python
import functools
import math

import jax
import jax.numpy as jnp
import numpy as np
from jax import lax
from jax.experimental import pallas as pl
from jax.experimental.pallas import tpu as pltpu
from jax.sharding import PartitionSpec as P

NCH = 512
ITERS = 2


damping = 0.5
epsilon = 1e-06


def from_behind(block, axis, distance):
    devices = range(lax.axis_size(axis))
    route = [(i - distance, i) for i in devices if i - distance in devices]
    return lax.ppermute(block, axis, route)


def filter_bank(extended, window_taps, kept_count, frames):
    transform_count = window_taps.shape[1]
    tap_count = window_taps.shape[0]
    local_inputs = extended.shape[0]
    kept = jnp.arange(kept_count, dtype=jnp.int32)
    indices = jnp.arange(transform_count, dtype=jnp.int32)
    phases = (kept[:, None] * indices[None, :] % transform_count).astype(jnp.float32) * (
        2.0 * math.pi / transform_count
    )
    cosine = jnp.cos(phases)
    sine_part = jnp.sin(phases)
    real_in = extended[:, :transform_count]
    imag_in = extended[:, transform_count:]
    real_sum = jnp.zeros((local_inputs, kept_count, frames), jnp.float32)
    imag_sum = jnp.zeros((local_inputs, kept_count, frames), jnp.float32)
    for tap_index in range(tap_count):
        tap_row = window_taps[tap_index][None, :]
        cos_block = (cosine * tap_row / math.sqrt(transform_count)).astype(jnp.bfloat16)
        sin_block = (sine_part * tap_row / math.sqrt(transform_count)).astype(jnp.bfloat16)
        part_real = real_in[:, :, tap_index : tap_index + frames]
        part_imag = imag_in[:, :, tap_index : tap_index + frames]
        real_sum = (
            real_sum
            + jnp.einsum("kn,inf->ikf", cos_block, part_real, preferred_element_type=jnp.float32)
            + jnp.einsum("kn,inf->ikf", sin_block, part_imag, preferred_element_type=jnp.float32)
        )
        imag_sum = (
            imag_sum
            + jnp.einsum("kn,inf->ikf", cos_block, part_imag, preferred_element_type=jnp.float32)
            - jnp.einsum("kn,inf->ikf", sin_block, part_real, preferred_element_type=jnp.float32)
        )
    return jnp.stack([real_sum, imag_sum], axis=2).astype(jnp.bfloat16)


def steering_angles(beam_steering, channels, input_count, chan_total):
    positions = jnp.arange(input_count, dtype=jnp.int32)
    column = positions // (input_count // 4)
    within = positions % (input_count // 4)
    phase_index = (
        beam_steering[0][:, None] * column[None, :] * 64
        + beam_steering[1][:, None] * within[None, :]
    ) % 256
    scaled = phase_index[None] * (chan_total + channels)[:, None, None]
    return scaled.astype(jnp.float32) * (2.0 * math.pi / (512 * chan_total))


def cross_rows(owned_rows, all_rows):
    paired = owned_rows.reshape(owned_rows.shape[0], owned_rows.shape[1], -1)
    rotated = jnp.stack([owned_rows[:, :, 1], -owned_rows[:, :, 0]], axis=2).reshape(paired.shape)
    left = jnp.stack([paired, rotated], axis=1)
    columns = all_rows.reshape(all_rows.shape[0], all_rows.shape[1], -1)
    return jnp.einsum("isck,jck->csij", left, columns, preferred_element_type=jnp.float32)


def form_beams(whole_set, gains_part, weights, beam_steering, channels, chan_total):
    input_count = whole_set.shape[0]
    angles = steering_angles(beam_steering, channels, input_count, chan_total)
    cosine = jnp.cos(angles)
    sine_part = jnp.sin(angles)
    scale_factor = 1.0 / math.sqrt(input_count)
    gain_real = (gains_part[:, 0] * weights)[:, None, :]
    gain_imaginary = (gains_part[:, 1] * weights)[:, None, :]
    steering_real = ((gain_real * cosine - gain_imaginary * sine_part) * scale_factor).astype(
        jnp.bfloat16
    )
    steering_imaginary = ((gain_real * sine_part + gain_imaginary * cosine) * scale_factor).astype(
        jnp.bfloat16
    )
    spectrum_real = whole_set[:, :, 0]
    spectrum_imaginary = whole_set[:, :, 1]
    volt_real = jnp.einsum(
        "jan,njg->jag", steering_real, spectrum_real, preferred_element_type=jnp.float32
    ) - jnp.einsum(
        "jan,njg->jag", steering_imaginary, spectrum_imaginary, preferred_element_type=jnp.float32
    )
    volt_imag = jnp.einsum(
        "jan,njg->jag", steering_real, spectrum_imaginary, preferred_element_type=jnp.float32
    ) + jnp.einsum(
        "jan,njg->jag", steering_imaginary, spectrum_real, preferred_element_type=jnp.float32
    )
    return volt_real * volt_real + volt_imag * volt_imag


def matvec(matrix, vector):
    return jnp.einsum("crj,cj->cr", matrix, vector, precision=lax.Precision.HIGHEST)


def general_shards(samples, window_taps, sky_model, prior_gains, beam_steering, input_flags):
    local_inputs = samples.shape[0]
    transform_count = samples.shape[2]
    frames = samples.shape[3]
    tap_count = window_taps.shape[0]
    kept_count = NCH
    time_count = lax.axis_size("tm")
    beam_count = lax.axis_size("beam")
    time_index = lax.axis_index("tm")
    beam_index = lax.axis_index("beam")
    chan_index = lax.axis_index("chan")
    weights = input_flags.astype(jnp.float32)
    stacked = samples.reshape(local_inputs, 2 * transform_count, frames)
    previous = from_behind(stacked[:, :, frames - tap_count + 1 :], "tm", 1)
    extended = jnp.concatenate([previous, stacked], axis=2)
    spectra = filter_bank(extended, window_taps, kept_count, frames).reshape(
        1, local_inputs, kept_count, 2, 1, frames
    )
    mixed = lax.all_to_all(spectra, ("chan", "tm"), split_axis=2, concat_axis=0, tiled=True)
    blocks = mixed.reshape(
        mixed.shape[0] // time_count, time_count, local_inputs, mixed.shape[2], 2, frames
    )
    turned = jnp.transpose(blocks, (0, 2, 3, 4, 1, 5))
    joined = lax.all_gather(turned, "beam", axis=1, tiled=True)
    input_count = joined.shape[0] * joined.shape[1]
    chan_local = joined.shape[2]
    whole_set = joined.reshape(input_count, chan_local, 2, joined.shape[4] * frames)
    half_rows = input_count // beam_count
    owned_rows = lax.dynamic_slice_in_dim(whole_set, beam_index * half_rows, half_rows, 0)
    terms = cross_rows(owned_rows, whole_set)
    visibilities = (terms / whole_set.shape[3]).astype(jnp.bfloat16)
    channels = (chan_index * time_count + time_index) * chan_local + jnp.arange(
        chan_local, dtype=jnp.int32
    )
    beam_power = form_beams(whole_set, prior_gains, weights, beam_steering, channels, kept_count)
    vis_used = lax.optimization_barrier(visibilities).astype(jnp.float32)
    model_values = sky_model.astype(jnp.float32)
    weighted = jnp.stack(
        [
            vis_used[:, 0] * model_values[:, 0] + vis_used[:, 1] * model_values[:, 1],
            vis_used[:, 1] * model_values[:, 0] - vis_used[:, 0] * model_values[:, 1],
        ],
        axis=1,
    )
    model_power = model_values[:, 0] * model_values[:, 0] + model_values[:, 1] * model_values[:, 1]
    row_start = beam_index * half_rows
    current = prior_gains
    updated = lax.dynamic_slice_in_dim(current, row_start, half_rows, 2)
    for step_index in range(ITERS):
        masked_real = current[:, 0] * weights
        masked_imag = current[:, 1] * weights
        vectors = jnp.stack([masked_real, masked_imag], axis=2)
        products = jnp.einsum("csrj,cjv->csrv", weighted, vectors, precision=lax.Precision.HIGHEST)
        numer_real = products[:, 0, :, 0] - products[:, 1, :, 1]
        numer_imag = products[:, 0, :, 1] + products[:, 1, :, 0]
        denom = (
            matvec(
                model_power,
                weights * (current[:, 0] * current[:, 0] + current[:, 1] * current[:, 1]),
            )
            + epsilon
        )
        older = lax.dynamic_slice_in_dim(current, row_start, half_rows, 2)
        updated = damping * older + (1.0 - damping) * jnp.stack(
            [numer_real / denom, numer_imag / denom], axis=1
        )
        if step_index + 1 < ITERS:
            current = lax.all_gather(updated, "beam", axis=2, tiled=True)
    return (visibilities, updated, beam_power)


LANES = 128
SUBLANES = 8
NEXT_ROWS = 4
MIB = 2**20
NT = (((1,), (1,)), ((), ()))
TN = (((0,), (0,)), ((), ()))
NN = (((1,), (0,)), ((), ()))


def mxu(left, right, dims):
    return lax.dot_general(left, right, dims, preferred_element_type=jnp.float32)


def transform_rows(kept_count, transform_count, owners, shares):
    by_owner = np.arange(kept_count).reshape(owners, -1)
    ends = np.cumsum(shares)
    kept = np.concatenate(
        [by_owner[:, end - share : end].reshape(-1) for share, end in zip(shares, ends)]
    )
    phases = (kept[:, None] * np.arange(transform_count)[None, :] % transform_count) * (
        2.0 * math.pi / transform_count
    )
    table = np.concatenate([np.cos(phases), np.sin(phases)], axis=1) / math.sqrt(transform_count)
    return jnp.asarray(table.astype(jnp.bfloat16))


def transformed(owners, frames, taps, table, windowed, out_ref, turned_ref, spill_ref):
    rows = table.shape[0]
    width = out_ref.shape[2]
    share = rows // owners
    block = mxu(table, windowed, NT)
    for frame in range(frames):
        turned_ref[pl.ds(frame, rows, stride=frames), :] = block[
            :, frame * width : (frame + 1) * width
        ]
    for frame in range(NEXT_ROWS):
        at = (frames + frame) * width
        if frame < taps - 1:
            part = block[:, at : at + width]
        else:
            part = jnp.zeros((rows, width), jnp.float32)
        spill_ref[pl.ds(frame, rows, stride=NEXT_ROWS), :] = part
    main = share * frames
    extra = share * NEXT_ROWS
    for owner in range(owners):
        out_ref[owner, :main, :] = turned_ref[owner * main : (owner + 1) * main, :].astype(
            jnp.bfloat16
        )
        out_ref[owner, main : main + extra, :] = spill_ref[
            owner * extra : (owner + 1) * extra, :
        ].astype(jnp.bfloat16)


def filter_kernel(
    owners,
    x_hbm,
    taps_ref,
    table_hbm,
    windowed_hbm,
    out_ref,
    x_ref,
    table_ref,
    here_ref,
    next_ref,
    windowed_ref,
    turned_ref,
    spill_ref,
    sems,
):
    inputs, _, frames, points = x_ref.shape
    taps = taps_ref.shape[0]
    width = 2 * inputs
    pieces = sems.shape[0] - 2
    group = inputs // pieces
    table_copy = pltpu.make_async_copy(
        table_hbm.at[pl.ds(0, table_ref.shape[0])], table_ref, sems.at[pieces]
    )
    copies = [
        pltpu.make_async_copy(
            x_hbm.at[pl.ds(i * group, group)], x_ref.at[pl.ds(i * group, group)], sems.at[i]
        )
        for i in range(pieces)
    ]
    for copy in copies:
        copy.start()
    table_copy.start()
    frame_of = lax.broadcasted_iota(jnp.int32, (frames, points), 0)
    here_weights = []
    next_weights = []
    for tap in range(taps):
        shift = taps - 1 - tap
        row = jnp.broadcast_to(taps_ref[tap : tap + 1, :], (frames, points))
        here_weights.append(jnp.where(frame_of >= shift, row, 0.0))
        next_weights.append(jnp.where(frame_of < shift, row, 0.0))

    def window(i, carry):
        for part in range(2):
            block = x_ref[i, part].astype(jnp.float32)
            here = block * here_weights[taps - 1]
            later = jnp.zeros_like(block)
            for tap in range(taps - 1):
                rolled = pltpu.roll(block, taps - 1 - tap, 0)
                here = here + rolled * here_weights[tap]
                later = later + rolled * next_weights[tap]
            for piece in range(points // LANES):
                lanes = slice(piece * LANES, (piece + 1) * LANES)
                here_ref[part, piece, pl.ds(i * frames, frames), :] = here[:, lanes]
                next_ref[part, piece, pl.ds(i * frames, frames), :] = later[:, lanes]
        return carry

    for i, copy in enumerate(copies):
        copy.wait()
        lax.fori_loop(i * group, (i + 1) * group, window, 0)
    for frame in range(frames + taps - 1):
        source = here_ref if frame < frames else next_ref
        first = frame % frames
        for piece in range(points // LANES):
            lanes = slice(piece * LANES, (piece + 1) * LANES)
            upper = slice(points + piece * LANES, points + (piece + 1) * LANES)
            real = source[0, piece, pl.ds(first, inputs, stride=frames), :].astype(jnp.bfloat16)
            imag = source[1, piece, pl.ds(first, inputs, stride=frames), :].astype(jnp.bfloat16)
            base = frame * width
            windowed_ref[base : base + inputs, lanes] = real
            windowed_ref[base : base + inputs, upper] = imag
            windowed_ref[base + inputs : base + width, lanes] = imag
            windowed_ref[base + inputs : base + width, upper] = -real
    keep = pltpu.make_async_copy(windowed_ref, windowed_hbm, sems.at[pieces + 1])
    keep.start()
    table_copy.wait()
    transformed(
        owners, frames, taps, table_ref[...], windowed_ref[...], out_ref, turned_ref, spill_ref
    )
    keep.wait()


def filter_more_kernel(
    owners,
    frames,
    taps,
    start,
    windowed_hbm,
    table_hbm,
    out_ref,
    windowed_ref,
    table_ref,
    turned_ref,
    spill_ref,
    sems,
):
    copies = [
        pltpu.make_async_copy(windowed_hbm, windowed_ref, sems.at[0]),
        pltpu.make_async_copy(
            table_hbm.at[pl.ds(start, table_ref.shape[0])], table_ref, sems.at[1]
        ),
    ]
    for copy in copies:
        copy.start()
    for copy in copies:
        copy.wait()
    transformed(
        owners, frames, taps, table_ref[...], windowed_ref[...], out_ref, turned_ref, spill_ref
    )


def filtered(samples, window_taps, kept_count, owners, shares):
    inputs, _, points, frames = samples.shape
    taps = window_taps.shape[0]
    width = 2 * inputs
    table = transform_rows(kept_count, points, owners, shares)
    by_frame = jnp.transpose(samples, (0, 1, 3, 2))
    by_frame = pltpu.with_memory_space_constraint(by_frame, pltpu.HBM)
    table = pltpu.with_memory_space_constraint(table, pltpu.HBM)
    pieces = points // LANES
    anywhere = pl.BlockSpec(memory_space=pl.ANY)
    vmem = pl.BlockSpec(memory_space=pltpu.VMEM)
    windowed_shape = ((frames + taps - 1) * width, 2 * points)

    def out_shape(share):
        return jax.ShapeDtypeStruct((owners, share * (frames + NEXT_ROWS), width), jnp.bfloat16)

    def scratch(share):
        rows = owners * share
        return [
            pltpu.VMEM((rows * frames, width), jnp.float32),
            pltpu.VMEM((rows * NEXT_ROWS, width), jnp.float32),
        ]

    windowed, first = pl.pallas_call(
        functools.partial(filter_kernel, owners),
        out_shape=[pltpu.HBM(windowed_shape, jnp.bfloat16), out_shape(shares[0])],
        in_specs=[anywhere, vmem, anywhere],
        out_specs=[anywhere, vmem],
        scratch_shapes=[
            pltpu.VMEM(by_frame.shape, jnp.bfloat16),
            pltpu.VMEM((owners * shares[0], 2 * points), jnp.bfloat16),
            pltpu.VMEM((2, pieces, inputs * frames, LANES), jnp.float32),
            pltpu.VMEM((2, pieces, inputs * frames, LANES), jnp.float32),
            pltpu.VMEM(windowed_shape, jnp.bfloat16),
            *scratch(shares[0]),
            pltpu.SemaphoreType.DMA((6,)),
        ],
        compiler_params=pltpu.CompilerParams(vmem_limit_bytes=32 * MIB),
        name="filter",
    )(by_frame, window_taps, table)
    windowed = pltpu.with_memory_space_constraint(windowed, pltpu.HBM)
    sent = [first]
    start = owners * shares[0]
    for share in shares[1:]:
        rows = owners * share
        sent.append(
            pl.pallas_call(
                functools.partial(filter_more_kernel, owners, frames, taps, start),
                out_shape=out_shape(share),
                in_specs=[anywhere, anywhere],
                out_specs=vmem,
                scratch_shapes=[
                    pltpu.VMEM(windowed_shape, jnp.bfloat16),
                    pltpu.VMEM((rows, 2 * points), jnp.bfloat16),
                    *scratch(share),
                    pltpu.SemaphoreType.DMA((2,)),
                ],
                compiler_params=pltpu.CompilerParams(vmem_limit_bytes=24 * MIB),
                name="filter_more",
            )(windowed, table)
        )
        start += rows
    return sent


def gain_terms(real, imag, gains, flags):
    weights = flags.astype(jnp.float32)
    gain_real = gains[0:1] * weights
    gain_imag = gains[1:2] * weights
    turned_real = real * gain_real + imag * gain_imag
    turned_imag = imag * gain_real - real * gain_imag
    power = weights * (gains[0:1] * gains[0:1] + gains[1:2] * gains[1:2])
    return turned_real, turned_imag, power


def denominators(power, model_real, model_imag):
    model_power = model_real * model_real + model_imag * model_imag
    rows = jnp.broadcast_to(power, (SUBLANES, power.shape[1])).astype(jnp.bfloat16)
    return mxu(rows, model_power, NT)[0:1] + epsilon


def updated_gains(own, turned, model_real, model_imag, denom, older):
    real, imag = turned
    straight = jnp.concatenate([real, imag], axis=0).astype(jnp.bfloat16)
    crossed = jnp.concatenate([-imag, real], axis=0).astype(jnp.bfloat16)
    modelled = mxu(straight, model_real, NT) + mxu(crossed, model_imag, NT)
    frames = real.shape[0]
    modelled_real = modelled[:frames]
    modelled_imag = modelled[frames:]
    own_real, own_imag = own
    numer_real = jnp.sum(own_real * modelled_real + own_imag * modelled_imag, axis=0, keepdims=True)
    numer_imag = jnp.sum(own_imag * modelled_real - own_real * modelled_imag, axis=0, keepdims=True)
    numer = jnp.concatenate([numer_real, numer_imag], axis=0) / frames
    return damping * older + (1.0 - damping) * (numer / denom)


def own_half(values, core):
    half = values.shape[1] // 2
    return jnp.where(core == 0, values[:, :half], values[:, half:])


def denominators_kernel(model_ref, gains_ref, flags_ref, denom_ref):
    flags = flags_ref[...].astype(jnp.float32)
    for c in range(model_ref.shape[0]):
        gains = gains_ref[c]
        power = flags[c : c + 1] * (gains[0:1] * gains[0:1] + gains[1:2] * gains[1:2])
        denom_ref[c] = denominators(power, model_ref[c, 0], model_ref[c, 1])


def first_kernel(times, base, core_ref, own_ref, other_ref, model_hbm, gains_ref, flags_ref, *refs):
    denom_ref = refs[0] if len(refs) == 5 else None
    spectra_ref, updated_ref, model_ref, sems = refs[-4:]
    core = core_ref[0]
    share = spectra_ref.shape[0]
    sources, rows, width = own_ref.shape
    frames = rows // share - NEXT_ROWS
    columns = sources // times
    lane = lax.broadcasted_iota(jnp.int32, (frames, width), 1)
    row = lax.broadcasted_iota(jnp.int32, (frames, width), 0)
    low = lane < width // 2
    count = BLOCK

    def copy(i):
        here = pl.ds(i * count, count)
        there = pl.ds(base + i * count, count)
        return pltpu.make_async_copy(model_hbm.at[there], model_ref.at[here], sems.at[i])

    for i in range(share // count):
        copy(i).start()

    def step(i, carry):
        main_rows = pl.ds(pl.multiple_of(i * (count * frames), count * frames), count * frames)
        next_rows = pl.ds(
            pl.multiple_of(share * frames + i * (count * NEXT_ROWS), count * NEXT_ROWS),
            count * NEXT_ROWS,
        )
        flags = flags_ref[pl.ds(pl.multiple_of(base + i * count, count), count), :]

        def loaded(ref, column, time):
            source = column * times + time
            block = ref[source, main_rows, :].astype(jnp.float32)
            extra = None
            if time > 0:
                extra = ref[source - 1, next_rows, :].astype(jnp.float32)
            return block, extra

        def one(value, c):
            block, extra = value
            block = block[c * frames : (c + 1) * frames]
            if extra is not None:
                pair = c // 2 * 2 * NEXT_ROWS
                extra = extra[pair : pair + 2 * NEXT_ROWS]
                if c % 2:
                    extra = pltpu.roll(extra, NEXT_ROWS, 0)
                block = block + jnp.where(row < NEXT_ROWS - 1, extra, 0.0)
            return block

        blocks = {
            (column, time): (loaded(own_ref, column, time), loaded(other_ref, column, time))
            for column in range(columns)
            for time in range(times)
        }
        for c in range(count):
            real_rows = []
            imag_rows = []
            for time in range(times):
                reals = []
                imags = []
                for column in range(columns):
                    own, other = blocks[column, time]
                    own = one(own, c)
                    other = one(other, c)
                    first = jnp.where(core == 0, own, other)
                    second = jnp.where(core == 0, other, own)
                    reals.append(jnp.where(low, first, pltpu.roll(second, width // 2, 1)))
                    imags.append(jnp.where(low, pltpu.roll(first, width // 2, 1), second))
                real_rows.append(jnp.concatenate(reals, axis=1))
                imag_rows.append(jnp.concatenate(imags, axis=1))
            spectra = jnp.concatenate(real_rows + imag_rows, axis=0)
            spectra_ref[i * count + c] = spectra.astype(jnp.bfloat16)
        copy(i).wait()
        for c in range(count):
            here = i * count + c
            values = spectra_ref[here].astype(jnp.float32)
            half = values.shape[0] // 2
            real = values[:half]
            imag = values[half:]
            gains = gains_ref[base + here]
            model_real = model_ref[here, 0]
            model_imag = model_ref[here, 1]
            turned_real, turned_imag, power = gain_terms(real, imag, gains, flags[c : c + 1])
            if denom_ref is None:
                denom = denominators(power, model_real, model_imag)
            else:
                denom = denom_ref[base + here]
            updated_ref[here] = updated_gains(
                (own_half(real, core), own_half(imag, core)),
                (turned_real, turned_imag),
                model_real,
                model_imag,
                denom,
                own_half(gains, core),
            )
        return carry

    lax.fori_loop(0, share // count, step, 0)


def second_kernel(
    base, core_ref, spectra_ref, model_ref, own_ref, other_ref, flags_ref, *refs
):
    visibilities_ref, updated_ref = refs[-2:]
    core = core_ref[0]
    count = visibilities_ref.shape[0]
    start = pl.program_id(0) * count
    for c in range(count):
        here = start + c
        spectra = spectra_ref[here]
        half = spectra.shape[0] // 2
        values = spectra.astype(jnp.float32)
        real = values[:half]
        imag = values[half:]
        own_real = own_half(real, core)
        own_imag = own_half(imag, core)
        paired = (jnp.concatenate([own_real, own_imag], axis=0) / half).astype(jnp.bfloat16)
        rotated = (jnp.concatenate([own_imag, -own_real], axis=0) / half).astype(jnp.bfloat16)
        visibilities_ref[c, 0] = mxu(paired, spectra, TN).astype(jnp.bfloat16)
        visibilities_ref[c, 1] = mxu(rotated, spectra, TN).astype(jnp.bfloat16)
        own = own_ref[here]
        other = other_ref[here]
        first = jnp.where(core == 0, own, other)
        second = jnp.where(core == 0, other, own)
        gains = jnp.concatenate([first, second], axis=1)
        turned_real, turned_imag, power = gain_terms(real, imag, gains, flags_ref[base + here])
        model_real = model_ref[here, 0]
        model_imag = model_ref[here, 1]
        updated_ref[here] = updated_gains(
            (own_real, own_imag),
            (turned_real, turned_imag),
            model_real,
            model_imag,
            denominators(power, model_real, model_imag),
            own,
        )


def series_length(reach):
    terms = 1
    while reach**terms / math.factorial(terms) >= 2.0**-22:
        terms += 1
    return terms


def steering_kernel(terms, reach, step, centre_ref, steering_ref, table_ref):
    inputs = table_ref.shape[1] // 2
    beams = table_ref.shape[2] // 2
    position = lax.broadcasted_iota(jnp.int32, (inputs, beams), 0)
    column = position // (inputs // 4)
    within = position % (inputs // 4)
    phase_index = (steering_ref[0:1, :] * column * 64 + steering_ref[1:2, :] * within) % 256
    angle = (phase_index * centre_ref[0]).astype(jnp.float32) * (0.5 * step)
    cosine = jnp.cos(angle)
    sine_part = jnp.sin(angle)
    offset = (phase_index - 128).astype(jnp.float32) * (reach * step)
    factor = jnp.ones_like(offset)
    for term in range(terms):
        if term:
            factor = factor * offset / term
        real, imag = (
            (cosine, sine_part),
            (-sine_part, cosine),
            (-cosine, -sine_part),
            (sine_part, -cosine),
        )[term % 4]
        real = (factor * real).astype(jnp.bfloat16)
        imag = (factor * imag).astype(jnp.bfloat16)
        table_ref[term, :inputs, :beams] = real
        table_ref[term, :inputs, beams:] = imag
        table_ref[term, inputs:, :beams] = -imag
        table_ref[term, inputs:, beams:] = real


def beams_kernel(spectra_ref, gains_ref, flags_ref, table_ref, *refs):
    power_ref, left_ref = refs[-2:]
    count, doubled, inputs = spectra_ref.shape
    frames = doubled // 2
    scale = 1.0 / math.sqrt(inputs)
    middle = 0.5 * (count - 1)
    terms = table_ref.shape[0]
    for c in range(count):
        values = spectra_ref[c].astype(jnp.float32)
        real = values[:frames]
        imag = values[frames:]
        weights = flags_ref[c : c + 1].astype(jnp.float32) * scale
        gain_real = gains_ref[c, 0:1] * weights
        gain_imag = gains_ref[c, 1:2] * weights
        lit_real = real * gain_real - imag * gain_imag
        lit_imag = real * gain_imag + imag * gain_real
        rows = slice(c * frames, (c + 1) * frames)
        for term in range(terms):
            power = ((c - middle) / max(middle, 0.5)) ** term
            left_ref[term, rows, :inputs] = (lit_real * power).astype(jnp.bfloat16)
            left_ref[term, rows, inputs:] = (lit_imag * power).astype(jnp.bfloat16)
    total = mxu(left_ref[0], table_ref[0], NN)
    for term in range(1, terms):
        total = total + mxu(left_ref[term], table_ref[term], NN)
    beams = total.shape[1] // 2
    real = total[:, :beams]
    imag = total[:, beams:]
    power_ref[...] = (real * real + imag * imag).reshape(count, frames, beams)


def formed_beams(chunk, gains, flags, earlier):
    base, spectra, table = chunk
    share, doubled, input_count = spectra.shape
    frame_count = doubled // 2
    beams = table.shape[2] // 2
    at = base // share
    earlier = [] if earlier is None else [earlier]
    return pl.pallas_call(
        beams_kernel,
        grid=(1,),
        in_specs=[
            pl.BlockSpec((share, doubled, input_count), lambda i: (0, 0, 0)),
            pl.BlockSpec((share, 2, input_count), lambda i: (at, 0, 0)),
            pl.BlockSpec((share, input_count), lambda i: (at, 0)),
            pl.BlockSpec(memory_space=pltpu.VMEM),
        ]
        + [pl.BlockSpec(memory_space=pl.ANY)] * len(earlier),
        out_specs=pl.BlockSpec((share, frame_count, beams), lambda i: (at, 0, 0)),
        out_shape=jax.ShapeDtypeStruct((gains.shape[0], frame_count, beams), jnp.float32),
        input_output_aliases={4: 0} if earlier else {},
        scratch_shapes=[
            pltpu.VMEM((table.shape[0], share * frame_count, 2 * input_count), jnp.bfloat16)
        ],
        compiler_params=pltpu.CompilerParams(vmem_limit_bytes=12 * MIB),
        name="beams",
    )(spectra, gains, flags, table, *earlier)


def chunk_shards(samples, window_taps, sky_model, prior_gains, beam_steering, input_flags):
    frames = samples.shape[3]
    chan_local, _, half_rows, input_count = sky_model.shape
    times = lax.axis_size("tm")
    owners = lax.axis_size("chan") * times
    core = lax.axis_index("beam").astype(jnp.int32).reshape(1)
    first_channel = (lax.axis_index("chan") * times + lax.axis_index("tm")) * chan_local
    kept_count = chan_local * owners
    frame_count = frames * times
    beams = beam_steering.shape[1]
    shares = [chan_local // CHUNKS] * CHUNKS
    bases = [sum(shares[:chunk]) for chunk in range(CHUNKS)]
    centres = [
        (2 * (kept_count + first_channel + base) + share - 1).astype(jnp.int32).reshape(1)
        for base, share in zip(bases, shares)
    ]
    flag_rows = input_flags.reshape(chan_local, 1, input_count)
    sent = filtered(samples, window_taps, kept_count, owners, shares)
    swap = [(0, 1), (1, 0)]
    smem = pl.BlockSpec(memory_space=pltpu.SMEM)
    vmem = pl.BlockSpec(memory_space=pltpu.VMEM)
    anywhere = pl.BlockSpec(memory_space=pl.ANY)
    step = 2.0 * math.pi / (512 * kept_count)

    sent[0], gains, flags, steering, flag_rows, core, centres = lax.optimization_barrier(
        (sent[0], prior_gains, input_flags, beam_steering, flag_rows, core, centres)
    )
    denom = pl.pallas_call(
        denominators_kernel,
        grid=(shares[0] // BLOCK,),
        in_specs=[
            pl.BlockSpec((BLOCK, 2, half_rows, input_count), lambda i: (i, 0, 0, 0)),
            pl.BlockSpec((BLOCK, 2, input_count), lambda i: (i, 0, 0)),
            pl.BlockSpec((BLOCK, input_count), lambda i: (i, 0)),
        ],
        out_specs=pl.BlockSpec((BLOCK, 1, half_rows), lambda i: (i, 0, 0)),
        out_shape=jax.ShapeDtypeStruct((shares[0], 1, half_rows), jnp.float32),
        compiler_params=pltpu.CompilerParams(vmem_limit_bytes=24 * MIB),
        name="denominators",
    )(sky_model, gains, flags)
    tables = []
    for centre, share in zip(centres, shares):
        reach = max(0.5 * (share - 1), 0.5)
        terms = series_length(128 * reach * step)
        tables.append(
            pl.pallas_call(
                functools.partial(steering_kernel, terms, reach, step),
                in_specs=[smem, vmem],
                out_specs=vmem,
                out_shape=jax.ShapeDtypeStruct((terms, 2 * input_count, 2 * beams), jnp.bfloat16),
                compiler_params=pltpu.CompilerParams(vmem_limit_bytes=8 * MIB),
                name="steering",
            )(centre, steering)
        )
    denom, *rest = lax.optimization_barrier((denom, *tables, *sent[1:]))
    tables = rest[:CHUNKS]
    sent[1:] = rest[CHUNKS:]
    visibilities = None
    beam_power = None
    gain_parts = []
    before = None
    for chunk, (base, share) in enumerate(zip(bases, shares)):
        own = lax.all_to_all(sent[chunk], ("chan", "tm"), 0, 0, tiled=True)
        if before is not None:
            own, gain_parts[-1], spectra = lax.optimization_barrier((own, gain_parts[-1], spectra))
            before = (before[0], spectra, before[2])
        other = lax.ppermute(own, "beam", swap)
        if before is not None:
            beam_power = formed_beams(before, gains, flags, beam_power)
            other, beam_power = lax.optimization_barrier((other, beam_power))
        half_shape = jax.ShapeDtypeStruct((share, 2, half_rows), jnp.float32)
        known = [denom] if chunk == 0 else []
        spectra, gains_own, model = pl.pallas_call(
            functools.partial(first_kernel, times, base),
            in_specs=[smem, vmem, vmem, anywhere, vmem, vmem] + [vmem] * len(known),
            out_specs=[vmem, vmem, vmem],
            out_shape=[
                jax.ShapeDtypeStruct((share, 2 * frame_count, input_count), jnp.bfloat16),
                half_shape,
                pltpu.VMEM((share, *sky_model.shape[1:]), sky_model.dtype),
            ],
            scratch_shapes=[pltpu.SemaphoreType.DMA((share // BLOCK,))],
            compiler_params=pltpu.CompilerParams(vmem_limit_bytes=12 * MIB),
            name="first_update",
        )(core, own, other, sky_model, gains, flags, *known)
        model = pltpu.with_memory_space_constraint(model, pltpu.VMEM)
        gains_other = lax.ppermute(gains_own, "beam", swap)
        before = (base, spectra, tables[chunk])
        if chunk == CHUNKS - 1:
            beam_power = formed_beams(before, gains, flags, beam_power)
        earlier = [] if visibilities is None else [visibilities]
        block = VIS_BLOCK
        block_spec = pl.BlockSpec(
            (block, 2, half_rows, input_count), lambda i, at=base // block: (at + i, 0, 0, 0)
        )
        visibilities, gains_new = pl.pallas_call(
            functools.partial(second_kernel, base),
            grid=(share // block,),
            in_specs=[smem, vmem, vmem, vmem, vmem, vmem] + [anywhere] * len(earlier),
            out_specs=[block_spec, vmem],
            out_shape=[
                jax.ShapeDtypeStruct((chan_local, 2, half_rows, input_count), jnp.bfloat16),
                half_shape,
            ],
            input_output_aliases={6: 0} if earlier else {},
            compiler_params=pltpu.CompilerParams(vmem_limit_bytes=12 * MIB),
            name="second_update",
        )(core, spectra, model, gains_own, gains_other, flag_rows, *earlier)
        gain_parts.append(gains_new)
    return (
        visibilities,
        jnp.concatenate(gain_parts, axis=0),
        jnp.transpose(beam_power, (0, 2, 1)),
    )


CHUNKS = 2
BLOCK = 8
VIS_BLOCK = 4


def shards(samples, window_taps, sky_model, prior_gains, beam_steering, input_flags):
    inputs, _, points, frames = samples.shape
    chan_local, _, half_rows, input_count = sky_model.shape
    frame_count = frames * lax.axis_size("tm")
    fits = (
        ITERS == 2
        and 2 * inputs == LANES
        and points % LANES == 0
        and frames == SUBLANES
        and window_taps.shape[0] == NEXT_ROWS
        and lax.axis_size("beam") == 2
        and chan_local % (CHUNKS * BLOCK) == 0
        and half_rows % LANES == 0
        and frame_count & (frame_count - 1) == 0
        and beam_steering.shape[1] % LANES == 0
    )
    form = chunk_shards if fits else general_shards
    return form(samples, window_taps, sky_model, prior_gains, beam_steering, input_flags)


def solution(mesh):
    return jax.shard_map(
        shards,
        mesh=mesh,
        in_specs=(
            P(("group", "chan", "beam"), None, None, "tm"),
            P(),
            P(("group", "chan", "tm"), None, "beam", None),
            P(("group", "chan", "tm"), None, None),
            P(None, ("group", "beam")),
            P(("group", "chan", "tm"), None),
        ),
        out_specs=(
            P(("group", "chan", "tm"), None, "beam", None),
            P(("group", "chan", "tm"), None, "beam"),
            P(("group", "chan", "tm"), "beam", None),
        ),
        check_vma=False,
    )
```

```python
import functools
import math

import jax
import jax.numpy as jnp
import numpy as np
from jax import lax
from jax.experimental import pallas as pl
from jax.experimental.pallas import tpu as pltpu
from jax.sharding import PartitionSpec as P

NCH = 512
ITERS = 2


damping = 0.5
epsilon = 1e-06


def from_behind(block, axis, distance):
    devices = range(lax.axis_size(axis))
    route = [(i - distance, i) for i in devices if i - distance in devices]
    return lax.ppermute(block, axis, route)


def filter_bank(extended, window_taps, kept_count, frames):
    transform_count = window_taps.shape[1]
    tap_count = window_taps.shape[0]
    local_inputs = extended.shape[0]
    kept = jnp.arange(kept_count, dtype=jnp.int32)
    indices = jnp.arange(transform_count, dtype=jnp.int32)
    phases = (kept[:, None] * indices[None, :] % transform_count).astype(jnp.float32) * (
        2.0 * math.pi / transform_count
    )
    cosine = jnp.cos(phases)
    sine_part = jnp.sin(phases)
    real_in = extended[:, :transform_count]
    imag_in = extended[:, transform_count:]
    real_sum = jnp.zeros((local_inputs, kept_count, frames), jnp.float32)
    imag_sum = jnp.zeros((local_inputs, kept_count, frames), jnp.float32)
    for tap_index in range(tap_count):
        tap_row = window_taps[tap_index][None, :]
        cos_block = (cosine * tap_row / math.sqrt(transform_count)).astype(jnp.bfloat16)
        sin_block = (sine_part * tap_row / math.sqrt(transform_count)).astype(jnp.bfloat16)
        part_real = real_in[:, :, tap_index : tap_index + frames]
        part_imag = imag_in[:, :, tap_index : tap_index + frames]
        real_sum = (
            real_sum
            + jnp.einsum("kn,inf->ikf", cos_block, part_real, preferred_element_type=jnp.float32)
            + jnp.einsum("kn,inf->ikf", sin_block, part_imag, preferred_element_type=jnp.float32)
        )
        imag_sum = (
            imag_sum
            + jnp.einsum("kn,inf->ikf", cos_block, part_imag, preferred_element_type=jnp.float32)
            - jnp.einsum("kn,inf->ikf", sin_block, part_real, preferred_element_type=jnp.float32)
        )
    return jnp.stack([real_sum, imag_sum], axis=2).astype(jnp.bfloat16)


def steering_angles(beam_steering, channels, input_count, chan_total):
    positions = jnp.arange(input_count, dtype=jnp.int32)
    column = positions // (input_count // 4)
    within = positions % (input_count // 4)
    phase_index = (
        beam_steering[0][:, None] * column[None, :] * 64
        + beam_steering[1][:, None] * within[None, :]
    ) % 256
    scaled = phase_index[None] * (chan_total + channels)[:, None, None]
    return scaled.astype(jnp.float32) * (2.0 * math.pi / (512 * chan_total))


def cross_rows(owned_rows, all_rows):
    paired = owned_rows.reshape(owned_rows.shape[0], owned_rows.shape[1], -1)
    rotated = jnp.stack([owned_rows[:, :, 1], -owned_rows[:, :, 0]], axis=2).reshape(paired.shape)
    left = jnp.stack([paired, rotated], axis=1)
    columns = all_rows.reshape(all_rows.shape[0], all_rows.shape[1], -1)
    return jnp.einsum("isck,jck->csij", left, columns, preferred_element_type=jnp.float32)


def form_beams(whole_set, gains_part, weights, beam_steering, channels, chan_total):
    input_count = whole_set.shape[0]
    angles = steering_angles(beam_steering, channels, input_count, chan_total)
    cosine = jnp.cos(angles)
    sine_part = jnp.sin(angles)
    scale_factor = 1.0 / math.sqrt(input_count)
    gain_real = (gains_part[:, 0] * weights)[:, None, :]
    gain_imaginary = (gains_part[:, 1] * weights)[:, None, :]
    steering_real = ((gain_real * cosine - gain_imaginary * sine_part) * scale_factor).astype(
        jnp.bfloat16
    )
    steering_imaginary = ((gain_real * sine_part + gain_imaginary * cosine) * scale_factor).astype(
        jnp.bfloat16
    )
    spectrum_real = whole_set[:, :, 0]
    spectrum_imaginary = whole_set[:, :, 1]
    volt_real = jnp.einsum(
        "jan,njg->jag", steering_real, spectrum_real, preferred_element_type=jnp.float32
    ) - jnp.einsum(
        "jan,njg->jag", steering_imaginary, spectrum_imaginary, preferred_element_type=jnp.float32
    )
    volt_imag = jnp.einsum(
        "jan,njg->jag", steering_real, spectrum_imaginary, preferred_element_type=jnp.float32
    ) + jnp.einsum(
        "jan,njg->jag", steering_imaginary, spectrum_real, preferred_element_type=jnp.float32
    )
    return volt_real * volt_real + volt_imag * volt_imag


def matvec(matrix, vector):
    return jnp.einsum("crj,cj->cr", matrix, vector, precision=lax.Precision.HIGHEST)


def general_shards(samples, window_taps, sky_model, prior_gains, beam_steering, input_flags):
    local_inputs = samples.shape[0]
    transform_count = samples.shape[2]
    frames = samples.shape[3]
    tap_count = window_taps.shape[0]
    kept_count = NCH
    time_count = lax.axis_size("tm")
    beam_count = lax.axis_size("beam")
    time_index = lax.axis_index("tm")
    beam_index = lax.axis_index("beam")
    chan_index = lax.axis_index("chan")
    weights = input_flags.astype(jnp.float32)
    stacked = samples.reshape(local_inputs, 2 * transform_count, frames)
    previous = from_behind(stacked[:, :, frames - tap_count + 1 :], "tm", 1)
    extended = jnp.concatenate([previous, stacked], axis=2)
    spectra = filter_bank(extended, window_taps, kept_count, frames).reshape(
        1, local_inputs, kept_count, 2, 1, frames
    )
    mixed = lax.all_to_all(spectra, ("chan", "tm"), split_axis=2, concat_axis=0, tiled=True)
    blocks = mixed.reshape(
        mixed.shape[0] // time_count, time_count, local_inputs, mixed.shape[2], 2, frames
    )
    turned = jnp.transpose(blocks, (0, 2, 3, 4, 1, 5))
    joined = lax.all_gather(turned, "beam", axis=1, tiled=True)
    input_count = joined.shape[0] * joined.shape[1]
    chan_local = joined.shape[2]
    whole_set = joined.reshape(input_count, chan_local, 2, joined.shape[4] * frames)
    half_rows = input_count // beam_count
    owned_rows = lax.dynamic_slice_in_dim(whole_set, beam_index * half_rows, half_rows, 0)
    terms = cross_rows(owned_rows, whole_set)
    visibilities = (terms / whole_set.shape[3]).astype(jnp.bfloat16)
    channels = (chan_index * time_count + time_index) * chan_local + jnp.arange(
        chan_local, dtype=jnp.int32
    )
    beam_power = form_beams(whole_set, prior_gains, weights, beam_steering, channels, kept_count)
    vis_used = lax.optimization_barrier(visibilities).astype(jnp.float32)
    model_values = sky_model.astype(jnp.float32)
    weighted = jnp.stack(
        [
            vis_used[:, 0] * model_values[:, 0] + vis_used[:, 1] * model_values[:, 1],
            vis_used[:, 1] * model_values[:, 0] - vis_used[:, 0] * model_values[:, 1],
        ],
        axis=1,
    )
    model_power = model_values[:, 0] * model_values[:, 0] + model_values[:, 1] * model_values[:, 1]
    row_start = beam_index * half_rows
    current = prior_gains
    updated = lax.dynamic_slice_in_dim(current, row_start, half_rows, 2)
    for step_index in range(ITERS):
        masked_real = current[:, 0] * weights
        masked_imag = current[:, 1] * weights
        vectors = jnp.stack([masked_real, masked_imag], axis=2)
        products = jnp.einsum("csrj,cjv->csrv", weighted, vectors, precision=lax.Precision.HIGHEST)
        numer_real = products[:, 0, :, 0] - products[:, 1, :, 1]
        numer_imag = products[:, 0, :, 1] + products[:, 1, :, 0]
        denom = (
            matvec(
                model_power,
                weights * (current[:, 0] * current[:, 0] + current[:, 1] * current[:, 1]),
            )
            + epsilon
        )
        older = lax.dynamic_slice_in_dim(current, row_start, half_rows, 2)
        updated = damping * older + (1.0 - damping) * jnp.stack(
            [numer_real / denom, numer_imag / denom], axis=1
        )
        if step_index + 1 < ITERS:
            current = lax.all_gather(updated, "beam", axis=2, tiled=True)
    return (visibilities, updated, beam_power)


LANES = 128
SUBLANES = 8
NEXT_ROWS = 4
MIB = 2**20
UPDATE_LIMIT = 14 * MIB
NT = (((1,), (1,)), ((), ()))
TN = (((0,), (0,)), ((), ()))
NN = (((1,), (0,)), ((), ()))


def mxu(left, right, dims):
    return lax.dot_general(left, right, dims, preferred_element_type=jnp.float32)


def transform_rows(kept_count, transform_count, owners, shares):
    by_owner = np.arange(kept_count).reshape(owners, -1)
    ends = np.cumsum(shares)
    kept = np.concatenate(
        [by_owner[:, end - share : end].reshape(-1) for share, end in zip(shares, ends)]
    )
    phases = (kept[:, None] * np.arange(transform_count)[None, :] % transform_count) * (
        2.0 * math.pi / transform_count
    )
    table = np.concatenate([np.cos(phases), np.sin(phases)], axis=1) / math.sqrt(transform_count)
    return jnp.asarray(table.astype(jnp.bfloat16))


def transformed(owners, frames, table, windowed_ref, turned_ref, copies=()):
    rows = table.shape[0]
    width = turned_ref.shape[1]
    share = rows // owners
    total = windowed_ref.shape[0] // width
    step = 4
    for frame in range(0, total, step):
        some = min(step, total - frame)
        for copy in copies[frame : frame + some]:
            copy.wait()
        block = mxu(table, windowed_ref[frame * width : (frame + some) * width, :], NT)
        for i in range(some):
            at = frame + i
            part = block[:, i * width : (i + 1) * width]
            if at < frames:
                turned_ref[pl.ds(at, rows, stride=frames), :] = part
            else:
                first = rows * frames + (at - frames) * share
                for owner in range(owners):
                    turned_ref[pl.ds(first + owner * (total - frames) * share, share), :] = part[
                        owner * share : (owner + 1) * share
                    ]


def filter_kernel(
    owners,
    x_hbm,
    taps_hbm,
    table_hbm,
    windowed_hbm,
    out_ref,
    x_ref,
    table_ref,
    taps_ref,
    frames_ref,
    windowed_ref,
    turned_ref,
    sems,
):
    inputs, _, frames, points = x_ref.shape
    taps = taps_ref.shape[0]
    width = 2 * inputs
    pieces = sems.shape[0] - 3
    group = inputs // pieces
    table_copy = pltpu.make_async_copy(
        table_hbm.at[pl.ds(0, table_ref.shape[0])], table_ref, sems.at[pieces]
    )
    copies = [
        pltpu.make_async_copy(
            x_hbm.at[pl.ds(i * group, group)], x_ref.at[pl.ds(i * group, group)], sems.at[i]
        )
        for i in range(pieces)
    ]
    taps_copy = pltpu.make_async_copy(taps_hbm, taps_ref, sems.at[pieces + 2])
    taps_copy.start()
    for copy in copies:
        copy.start()
    taps_copy.wait()

    def spread(i, carry):
        for part in range(2):
            block = x_ref[i, part].astype(jnp.float32)
            for piece in range(points // LANES):
                here = pl.ds(pl.multiple_of(i * frames, frames), frames)
                frames_ref[part, piece, here, :] = block[:, piece * LANES : (piece + 1) * LANES]
        return carry

    for i, copy in enumerate(copies):
        copy.wait()
        lax.fori_loop(i * group, (i + 1) * group, spread, 0, unroll=4)

    table_copy.start()

    def window(piece, carry):
        lanes = pl.ds(pl.multiple_of(piece * LANES, LANES), LANES)
        upper = pl.ds(pl.multiple_of(points + piece * LANES, LANES), LANES)
        weights = taps_ref[:, lanes]
        weights = [
            jnp.broadcast_to(weights[tap : tap + 1], (2 * SUBLANES, LANES)) for tap in range(taps)
        ]
        for first in range(0, inputs, 2 * SUBLANES):
            for part in range(2):
                values = [
                    frames_ref[
                        part, piece, pl.ds(first * frames + frame, 2 * SUBLANES, stride=frames), :
                    ]
                    for frame in range(frames)
                ]
                for frame in range(frames + taps - 1):
                    total = None
                    for tap in range(taps):
                        source = frame + tap - (taps - 1)
                        if 0 <= source < frames:
                            term = values[source] * weights[tap]
                            total = term if total is None else total + term
                    base = frame * width + first
                    rows = slice(base, base + 2 * SUBLANES)
                    swapped = slice(base + inputs, base + inputs + 2 * SUBLANES)
                    total = total.astype(jnp.bfloat16)
                    if part == 0:
                        windowed_ref[rows, lanes] = total
                        windowed_ref[swapped, upper] = -total
                    else:
                        windowed_ref[rows, upper] = total
                        windowed_ref[swapped, lanes] = total
        return carry

    lax.fori_loop(0, points // LANES, window, 0)
    keep = pltpu.make_async_copy(windowed_ref, windowed_hbm, sems.at[pieces + 1])
    keep.start()
    table_copy.wait()
    transformed(owners, frames, table_ref[...], windowed_ref, turned_ref)
    share = table_ref.shape[0] // owners
    main = share * frames
    extra = share * (taps - 1)
    for owner in range(owners):
        out_ref[owner, :main, :] = turned_ref[owner * main : (owner + 1) * main, :].astype(
            jnp.bfloat16
        )
        first = owners * main + owner * extra
        out_ref[owner, main : main + extra, :] = turned_ref[first : first + extra, :].astype(
            jnp.bfloat16
        )
    keep.wait()


def rows_copies(source, target, sems, first=0):
    size = target.shape[0] // sems.shape[0]
    return [
        pltpu.make_async_copy(
            source.at[pl.ds(first + i * size, size)], target.at[pl.ds(i * size, size)], sems.at[i]
        )
        for i in range(sems.shape[0])
    ]


def spill_kernel(first, start, windowed_hbm, table_hbm, out_ref, windowed_ref, table_ref, sems):
    copies = rows_copies(windowed_hbm, windowed_ref, sems.at[pl.ds(0, 1)], first)
    copies += rows_copies(table_hbm, table_ref, sems.at[pl.ds(1, 1)], start)
    for copy in copies:
        copy.start()
    for copy in copies:
        copy.wait()
    frames, _, width = out_ref.shape
    block = mxu(table_ref[...], windowed_ref[...], NT)
    for frame in range(frames):
        out_ref[frame] = block[:, frame * width : (frame + 1) * width].astype(jnp.bfloat16)


def filter_more_kernel(
    owners, start, windowed_hbm, table_hbm, turned_ref, windowed_ref, table_ref, sems
):
    frames = sems.shape[0] - 1
    copies = rows_copies(windowed_hbm, windowed_ref, sems.at[pl.ds(0, frames)])
    table_copies = rows_copies(table_hbm, table_ref, sems.at[pl.ds(frames, 1)], start)
    for copy in table_copies + copies:
        copy.start()
    for copy in table_copies:
        copy.wait()
    transformed(owners, frames, table_ref[...], windowed_ref, turned_ref, copies)


def added_kernel(turned_ref, added_ref, out_ref, total_ref):
    owners, main, _ = out_ref.shape
    nexts, rows, _ = added_ref.shape
    frames = turned_ref.shape[0] // rows
    total_ref[...] = turned_ref[...]
    for frame in range(nexts):
        here = pl.ds(frame, rows, stride=frames)
        total_ref[here, :] = turned_ref[here, :] + added_ref[frame].astype(jnp.float32)
    for owner in range(owners):
        out_ref[owner] = total_ref[owner * main : (owner + 1) * main, :].astype(jnp.bfloat16)


def filtered(samples, window_taps, kept_count, owners, shares):
    inputs, _, points, frames = samples.shape
    taps = window_taps.shape[0]
    width = 2 * inputs
    table = transform_rows(kept_count, points, owners, shares)
    by_frame = jnp.transpose(samples, (0, 1, 3, 2))
    by_frame = pltpu.with_memory_space_constraint(by_frame, pltpu.HBM)
    table = pltpu.with_memory_space_constraint(table, pltpu.HBM)
    window_taps = pltpu.with_memory_space_constraint(window_taps, pltpu.HBM)
    pieces = points // LANES
    anywhere = pl.BlockSpec(memory_space=pl.ANY)
    vmem = pl.BlockSpec(memory_space=pltpu.VMEM)
    windowed_shape = ((frames + taps - 1) * width, 2 * points)
    rows = owners * shares[0]
    windowed, first = pl.pallas_call(
        functools.partial(filter_kernel, owners),
        out_shape=[
            pltpu.HBM(windowed_shape, jnp.bfloat16),
            jax.ShapeDtypeStruct((owners, shares[0] * (frames + taps - 1), width), jnp.bfloat16),
        ],
        in_specs=[anywhere, anywhere, anywhere],
        out_specs=[anywhere, vmem],
        scratch_shapes=[
            pltpu.VMEM(by_frame.shape, jnp.bfloat16),
            pltpu.VMEM((rows, 2 * points), jnp.bfloat16),
            pltpu.VMEM(window_taps.shape, jnp.float32),
            pltpu.VMEM((2, pieces, inputs * frames, LANES), jnp.float32),
            pltpu.VMEM(windowed_shape, jnp.bfloat16),
            pltpu.VMEM((rows * (frames + taps - 1), width), jnp.float32),
            pltpu.SemaphoreType.DMA((7,)),
        ],
        compiler_params=pltpu.CompilerParams(vmem_limit_bytes=32 * MIB),
        name="filter",
    )(by_frame, window_taps, table)
    windowed = pltpu.with_memory_space_constraint(windowed, pltpu.HBM)

    def more(chunk, start):
        rows = owners * shares[chunk]
        spill = pl.pallas_call(
            functools.partial(spill_kernel, frames * width, start),
            out_shape=jax.ShapeDtypeStruct((taps - 1, rows, width), jnp.bfloat16),
            in_specs=[anywhere, anywhere],
            out_specs=vmem,
            scratch_shapes=[
                pltpu.VMEM(((taps - 1) * width, 2 * points), jnp.bfloat16),
                pltpu.VMEM((rows, 2 * points), jnp.bfloat16),
                pltpu.SemaphoreType.DMA((2,)),
            ],
            compiler_params=pltpu.CompilerParams(vmem_limit_bytes=24 * MIB),
            name="spill",
        )(windowed, table)
        added = from_behind(spill, "tm", 1)
        turned = pl.pallas_call(
            functools.partial(filter_more_kernel, owners, start),
            out_shape=jax.ShapeDtypeStruct((rows * frames, width), jnp.float32),
            in_specs=[anywhere, anywhere],
            out_specs=vmem,
            scratch_shapes=[
                pltpu.VMEM((frames * width, 2 * points), jnp.bfloat16),
                pltpu.VMEM((rows, 2 * points), jnp.bfloat16),
                pltpu.SemaphoreType.DMA((frames + 1,)),
            ],
            compiler_params=pltpu.CompilerParams(vmem_limit_bytes=24 * MIB),
            name="filter_more",
        )(windowed, table)
        return pl.pallas_call(
            added_kernel,
            out_shape=jax.ShapeDtypeStruct((owners, shares[chunk] * frames, width), jnp.bfloat16),
            in_specs=[vmem, vmem],
            out_specs=vmem,
            scratch_shapes=[pltpu.VMEM((rows * frames, width), jnp.float32)],
            compiler_params=pltpu.CompilerParams(vmem_limit_bytes=24 * MIB),
            name="added",
        )(turned, added)

    sent = [first]
    start = rows
    for chunk in range(1, len(shares)):
        sent.append(more(chunk, start))
        start += owners * shares[chunk]
    return sent


def gain_terms(real, imag, gains, flags):
    weights = flags.astype(jnp.float32)
    gain_real = gains[0:1] * weights
    gain_imag = gains[1:2] * weights
    turned_real = real * gain_real + imag * gain_imag
    turned_imag = imag * gain_real - real * gain_imag
    power = weights * (gains[0:1] * gains[0:1] + gains[1:2] * gains[1:2])
    return turned_real, turned_imag, power


def denominators(power, model_real, model_imag):
    model_power = model_real * model_real + model_imag * model_imag
    terms = model_power * jnp.broadcast_to(power.astype(jnp.bfloat16), model_power.shape)
    folded = terms[:, :LANES]
    for first in range(LANES, terms.shape[1], LANES):
        folded = folded + terms[:, first : first + LANES]
    return mxu(jnp.ones((SUBLANES, LANES), jnp.bfloat16), folded, NT)[0:1] + epsilon


def updated_gains(own, turned, model_real, model_imag, denom, older):
    real, imag = turned
    straight = jnp.concatenate([real, imag], axis=0).astype(jnp.bfloat16)
    crossed = jnp.concatenate([-imag, real], axis=0).astype(jnp.bfloat16)
    modelled = mxu(straight, model_real, NT) + mxu(crossed, model_imag, NT)
    frames = real.shape[0]
    modelled_real = modelled[:frames]
    modelled_imag = modelled[frames:]
    own_real, own_imag = own
    numer_real = jnp.sum(own_real * modelled_real + own_imag * modelled_imag, axis=0, keepdims=True)
    numer_imag = jnp.sum(own_imag * modelled_real - own_real * modelled_imag, axis=0, keepdims=True)
    numer = jnp.concatenate([numer_real, numer_imag], axis=0) / frames
    return damping * older + (1.0 - damping) * (numer / denom)


def own_half(values, core):
    half = values.shape[1] // 2
    return jnp.where(core == 0, values[:, :half], values[:, half:])


def model_kernel(base, own_hbm, model_hbm, model_ref, sem):
    del own_hbm
    count = min(MODEL_BLOCK, model_ref.shape[0])
    copy = pltpu.make_async_copy(
        model_hbm.at[pl.ds(base, count)], model_ref.at[pl.ds(0, count)], sem
    )
    copy.start()
    copy.wait()


def first_kernel(
    times, base, core_ref, own_ref, other_ref, model_hbm, gains_ref, flags_ref, here_ref, *refs
):
    del here_ref
    spectra_ref, updated_ref, model_ref, next_ref, sems = refs
    core = core_ref[0]
    share = spectra_ref.shape[0]
    sources, rows, width = own_ref.shape
    frames = spectra_ref.shape[1] // 2 // times
    nexts = rows // share - frames
    columns = sources // times
    lane = lax.broadcasted_iota(jnp.int32, (frames, width), 1)
    row = lax.broadcasted_iota(jnp.int32, (frames, width), 0)
    low = lane < width // 2
    count = BLOCK

    def copy(i):
        here = pl.ds(i * VIS_BLOCK, VIS_BLOCK)
        there = pl.ds(base + i * VIS_BLOCK, VIS_BLOCK)
        return pltpu.make_async_copy(model_hbm.at[there], model_ref.at[here], sems.at[i])

    groups = share // VIS_BLOCK
    there = min(MODEL_BLOCK, share) // VIS_BLOCK
    ahead = 4
    for i in range(there, min(there + ahead, groups)):
        copy(i).start()
    if nexts:
        for source in range(sources):
            for side, ref in enumerate((own_ref, other_ref)):
                next_ref[side, source] = ref[source, share * frames :, :].astype(jnp.float32)

    def assemble(i):
        main_rows = pl.ds(pl.multiple_of(i * (count * frames), count * frames), count * frames)

        def loaded(side, column, time):
            ref = (own_ref, other_ref)[side]
            source = column * times + time
            block = ref[source, main_rows, :].astype(jnp.float32)
            extra = []
            if time > 0:
                extra = [
                    next_ref[
                        side, source - 1, pl.ds(pl.multiple_of(share * k + i * count, count), count), :
                    ]
                    for k in range(nexts)
                ]
            return block, extra

        def one(value, c):
            block, extra = value
            block = block[c * frames : (c + 1) * frames]
            for k, more in enumerate(extra):
                block = block + jnp.where(row == k, more[c : c + 1], 0.0)
            return block

        blocks = {
            (column, time): (loaded(0, column, time), loaded(1, column, time))
            for column in range(columns)
            for time in range(times)
        }
        for c in range(count):
            real_rows = []
            imag_rows = []
            for time in range(times):
                reals = []
                imags = []
                for column in range(columns):
                    own, other = blocks[column, time]
                    own = one(own, c)
                    other = one(other, c)
                    first = jnp.where(core == 0, own, other)
                    second = jnp.where(core == 0, other, own)
                    reals.append(jnp.where(low, first, pltpu.roll(second, width // 2, 1)))
                    imags.append(jnp.where(low, pltpu.roll(first, width // 2, 1), second))
                real_rows.append(jnp.concatenate(reals, axis=1))
                imag_rows.append(jnp.concatenate(imags, axis=1))
            spectra = jnp.concatenate(real_rows + imag_rows, axis=0)
            spectra_ref[i * count + c] = spectra.astype(jnp.bfloat16)

    def update(i):
        for part in range(count // VIS_BLOCK):
            group = i * (count // VIS_BLOCK) + part

            @pl.when(group >= there)
            def _():
                copy(group).wait()

                @pl.when(group + ahead < groups)
                def _():
                    copy(group + ahead).start()

        for c in range(count):
            here = i * count + c
            values = spectra_ref[here].astype(jnp.float32)
            half = values.shape[0] // 2
            real = values[:half]
            imag = values[half:]
            gains = gains_ref[base + here]
            flags = flags_ref[pl.ds(base + here, 1), :]
            model_real = model_ref[here, 0]
            model_imag = model_ref[here, 1]
            turned_real, turned_imag, power = gain_terms(real, imag, gains, flags)
            updated_ref[here] = updated_gains(
                (own_half(real, core), own_half(imag, core)),
                (turned_real, turned_imag),
                model_real,
                model_imag,
                denominators(power, model_real, model_imag),
                own_half(gains, core),
            )

    def step(i, carry):
        update(i)
        assemble(i + 1)
        return carry

    last = share // count - 1
    assemble(0)
    lax.fori_loop(0, last, step, 0)
    update(last)


def second_kernel(
    base, core_ref, spectra_ref, model_ref, own_ref, other_ref, flags_ref, *refs
):
    visibilities_ref, updated_ref = refs[-2:]
    core = core_ref[0]
    count = visibilities_ref.shape[0]
    start = pl.program_id(0) * count
    for c in range(count):
        here = start + c
        spectra = spectra_ref[here]
        half = spectra.shape[0] // 2
        values = spectra.astype(jnp.float32)
        real = values[:half]
        imag = values[half:]
        own_real = own_half(real, core)
        own_imag = own_half(imag, core)
        paired = (jnp.concatenate([own_real, own_imag], axis=0) / half).astype(jnp.bfloat16)
        rotated = (jnp.concatenate([own_imag, -own_real], axis=0) / half).astype(jnp.bfloat16)
        visibilities_ref[c, 0] = mxu(paired, spectra, TN).astype(jnp.bfloat16)
        visibilities_ref[c, 1] = mxu(rotated, spectra, TN).astype(jnp.bfloat16)
        own = own_ref[here]
        other = other_ref[here]
        first = jnp.where(core == 0, own, other)
        second = jnp.where(core == 0, other, own)
        gains = jnp.concatenate([first, second], axis=1)
        turned_real, turned_imag, power = gain_terms(real, imag, gains, flags_ref[pl.ds(base + here, 1), :])
        model_real = model_ref[here, 0]
        model_imag = model_ref[here, 1]
        updated_ref[c] = updated_gains(
            (own_real, own_imag),
            (turned_real, turned_imag),
            model_real,
            model_imag,
            denominators(power, model_real, model_imag),
            own,
        )


def series_length(reach):
    terms = 1
    while reach**terms / math.factorial(terms) >= 2.0**-22:
        terms += 1
    return terms


def turns(count, period):
    quarter = period // 4
    quadrant = lax.shift_right_logical(count + period // 8, quarter.bit_length() - 1)
    angle = (count - quadrant * quarter).astype(jnp.float32) * (2.0 * math.pi / period)
    square = angle * angle
    sine_part = jnp.full_like(angle, 1.0 / math.factorial(9))
    cosine = jnp.full_like(angle, 1.0 / math.factorial(8))
    for power in (7, 5, 3, 1):
        sign = -1.0 if power % 4 == 3 else 1.0
        sine_part = sine_part * square + sign / math.factorial(power)
        cosine = cosine * square + sign / math.factorial(power - 1)
    sine_part = sine_part * angle
    odd = (quadrant & 1) == 1
    real = jnp.where(odd, sine_part, cosine)
    imag = jnp.where(odd, cosine, sine_part)
    real = jnp.where(((quadrant + 1) & 2) == 2, -real, real)
    imag = jnp.where((quadrant & 2) == 2, -imag, imag)
    return real, imag


def steering_tables(centre, steering_ref, table_ref, step, reach):
    inputs = table_ref.shape[1] // 2
    beams = table_ref.shape[2] // 2
    quarter = inputs // 4
    for column in range(4):
        for first in range(0, quarter, 4 * SUBLANES):
            shape = (4 * SUBLANES, beams)
            within = lax.broadcasted_iota(jnp.int32, shape, 0) + first
            phase_index = (steering_ref[0:1, :] * (column * 64) + steering_ref[1:2, :] * within) & 255
            cosine, sine_part = turns(phase_index * centre, round(4.0 * math.pi / step))
            offset = (phase_index - 128).astype(jnp.float32) * (reach * step)
            factor = None
            at = column * quarter + first
            rows = slice(at, at + shape[0])
            lower = slice(inputs + at, inputs + at + shape[0])
            for term in range(table_ref.shape[0]):
                real, imag = (
                    (cosine, sine_part),
                    (-sine_part, cosine),
                    (-cosine, -sine_part),
                    (sine_part, -cosine),
                )[term % 4]
                if term:
                    factor = offset if factor is None else factor * offset / term
                    real = factor * real
                    imag = factor * imag
                real = real.astype(jnp.bfloat16)
                imag = imag.astype(jnp.bfloat16)
                table_ref[term, rows, :beams] = real
                table_ref[term, rows, beams:] = imag
                table_ref[term, lower, :beams] = -imag
                table_ref[term, lower, beams:] = real


def beams_kernel(step, reach, base, centre_ref, spectra_ref, gains_ref, flags_ref, steering_ref, *refs):
    power_hbm, power_ref, left_ref, table_ref, sem = refs[-5:]
    steering_tables(centre_ref[0], steering_ref, table_ref, step, reach)
    count, doubled, inputs = spectra_ref.shape
    frames = doubled // 2
    scale = 1.0 / math.sqrt(inputs)
    middle = 0.5 * (count - 1)
    terms = table_ref.shape[0]
    for c in range(count):
        values = spectra_ref[c].astype(jnp.float32)
        real = values[:frames]
        imag = values[frames:]
        at = base + c
        weights = flags_ref[at : at + 1].astype(jnp.float32) * scale
        gain_real = gains_ref[at, 0:1] * weights
        gain_imag = gains_ref[at, 1:2] * weights
        lit_real = real * gain_real - imag * gain_imag
        lit_imag = real * gain_imag + imag * gain_real
        rows = slice(c * frames, (c + 1) * frames)
        for term in range(terms):
            power = ((c - middle) / max(middle, 0.5)) ** term
            left_ref[term, rows, :inputs] = (lit_real * power).astype(jnp.bfloat16)
            left_ref[term, rows, inputs:] = (lit_imag * power).astype(jnp.bfloat16)
    total = mxu(left_ref[0], table_ref[0], NN)
    for term in range(1, terms):
        total = total + mxu(left_ref[term], table_ref[term], NN)
    beams = total.shape[1] // 2
    real = total[:, :beams]
    imag = total[:, beams:]
    power_ref[...] = (real * real + imag * imag).reshape(count, frames, beams)
    copy = pltpu.make_async_copy(power_ref, power_hbm.at[pl.ds(base, count)], sem)
    copy.start()
    copy.wait()


def formed_beams(chunk, gains, flags, steering, step, earlier):
    base, centre, spectra = chunk
    share, doubled, input_count = spectra.shape
    frame_count = doubled // 2
    beams = steering.shape[1]
    earlier = [] if earlier is None else [earlier]
    reach = max(0.5 * (share - 1), 0.5)
    terms = series_length(128 * reach * step)
    vmem = pl.BlockSpec(memory_space=pltpu.VMEM)
    return pl.pallas_call(
        functools.partial(beams_kernel, step, reach, base),
        in_specs=[pl.BlockSpec(memory_space=pltpu.SMEM)] + [vmem] * 4
        + [pl.BlockSpec(memory_space=pl.ANY)] * len(earlier),
        out_specs=pl.BlockSpec(memory_space=pl.ANY),
        out_shape=jax.ShapeDtypeStruct((gains.shape[0], frame_count, beams), jnp.float32),
        input_output_aliases={5: 0} if earlier else {},
        scratch_shapes=[
            pltpu.VMEM((share, frame_count, beams), jnp.float32),
            pltpu.VMEM((terms, share * frame_count, 2 * input_count), jnp.bfloat16),
            pltpu.VMEM((terms, 2 * input_count, 2 * beams), jnp.bfloat16),
            pltpu.SemaphoreType.DMA,
        ],
        compiler_params=pltpu.CompilerParams(vmem_limit_bytes=UPDATE_LIMIT),
        name="beams",
    )(centre, spectra, gains, flags, steering, *earlier)


def chunk_shards(samples, window_taps, sky_model, prior_gains, beam_steering, input_flags):
    frames = samples.shape[3]
    chan_local, _, half_rows, input_count = sky_model.shape
    times = lax.axis_size("tm")
    owners = lax.axis_size("chan") * times
    core = lax.axis_index("beam").astype(jnp.int32).reshape(1)
    first_channel = (lax.axis_index("chan") * times + lax.axis_index("tm")) * chan_local
    kept_count = chan_local * owners
    frame_count = frames * times
    beams = beam_steering.shape[1]
    shares = chunk_shares(chan_local)
    bases = [sum(shares[:chunk]) for chunk in range(len(shares))]
    centres = [
        (2 * (kept_count + first_channel + base) + share - 1).astype(jnp.int32).reshape(1)
        for base, share in zip(bases, shares)
    ]
    sent = filtered(samples, window_taps, kept_count, owners, shares)
    swap = [(0, 1), (1, 0)]
    smem = pl.BlockSpec(memory_space=pltpu.SMEM)
    vmem = pl.BlockSpec(memory_space=pltpu.VMEM)
    anywhere = pl.BlockSpec(memory_space=pl.ANY)
    step = 2.0 * math.pi / (512 * kept_count)

    sent[0], gains, flags, steering, core, centres = lax.optimization_barrier(
        (sent[0], prior_gains, input_flags, beam_steering, core, centres)
    )
    visibilities = None
    beam_power = None
    gains_new = None
    before = None
    for chunk, (base, share) in enumerate(zip(bases, shares)):
        own = lax.all_to_all(sent[chunk], ("chan", "tm"), 0, 0, tiled=True)
        if before is not None:
            beam_power = formed_beams(before, gains, flags, steering, step, beam_power)
            own, gains_new, beam_power = lax.optimization_barrier((own, gains_new, beam_power))
        other = lax.ppermute(own, "beam", swap)
        model_shape = (share, *sky_model.shape[1:])
        model = pl.pallas_call(
            functools.partial(model_kernel, base),
            in_specs=[anywhere, anywhere],
            out_specs=vmem,
            out_shape=pltpu.VMEM(model_shape, sky_model.dtype),
            scratch_shapes=[pltpu.SemaphoreType.DMA],
            compiler_params=pltpu.CompilerParams(vmem_limit_bytes=UPDATE_LIMIT),
            name="model",
        )(own, sky_model)
        model = pltpu.with_memory_space_constraint(model, pltpu.VMEM)
        half_shape = jax.ShapeDtypeStruct((share, 2, half_rows), jnp.float32)
        spectra, gains_own, model = pl.pallas_call(
            functools.partial(first_kernel, times, base),
            in_specs=[smem, vmem, vmem, anywhere, vmem, vmem, vmem],
            out_specs=[vmem, vmem, vmem],
            out_shape=[
                jax.ShapeDtypeStruct((share, 2 * frame_count, input_count), jnp.bfloat16),
                half_shape,
                pltpu.VMEM(model_shape, sky_model.dtype),
            ],
            input_output_aliases={6: 2},
            scratch_shapes=[
                pltpu.VMEM((2, owners, max(own.shape[1] - share * frames, SUBLANES), own.shape[2]), jnp.float32),
                pltpu.SemaphoreType.DMA((share // VIS_BLOCK,)),
            ],
            compiler_params=pltpu.CompilerParams(vmem_limit_bytes=UPDATE_LIMIT),
            name="first_update",
        )(core, own, other, sky_model, gains, flags, model)
        model = pltpu.with_memory_space_constraint(model, pltpu.VMEM)
        gains_other = lax.ppermute(gains_own, "beam", swap)
        before = (base, centres[chunk], spectra)
        if chunk == len(shares) - 1:
            beam_power = formed_beams(before, gains, flags, steering, step, beam_power)
        earlier = [] if visibilities is None else [visibilities, gains_new]
        block = VIS_BLOCK
        block_spec = pl.BlockSpec(
            (block, 2, half_rows, input_count), lambda i, at=base // block: (at + i, 0, 0, 0)
        )
        visibilities, gains_new = pl.pallas_call(
            functools.partial(second_kernel, base),
            grid=(share // block,),
            in_specs=[smem, vmem, vmem, vmem, vmem, vmem] + [anywhere] * len(earlier),
            out_specs=[
                block_spec,
                pl.BlockSpec((block, 2, half_rows), lambda i, at=base // block: (at + i, 0, 0)),
            ],
            out_shape=[
                jax.ShapeDtypeStruct((chan_local, 2, half_rows, input_count), jnp.bfloat16),
                jax.ShapeDtypeStruct((chan_local, 2, half_rows), jnp.float32),
            ],
            input_output_aliases={6: 0, 7: 1} if earlier else {},
            compiler_params=pltpu.CompilerParams(vmem_limit_bytes=UPDATE_LIMIT),
            name="second_update",
        )(core, spectra, model, gains_own, gains_other, flags, *earlier)
    return (
        visibilities,
        gains_new,
        jnp.transpose(beam_power, (0, 2, 1)),
    )


BLOCK = 8
VIS_BLOCK = 4
MODEL_BLOCK = 8


def chunk_shares(chan_local):
    blocks = chan_local // BLOCK
    first = blocks * 3 // 8
    return [first * BLOCK, (blocks - first) * BLOCK]


def shards(samples, window_taps, sky_model, prior_gains, beam_steering, input_flags):
    inputs, _, points, frames = samples.shape
    chan_local, _, half_rows, input_count = sky_model.shape
    frame_count = frames * lax.axis_size("tm")
    owners = lax.axis_size("chan") * lax.axis_size("tm")
    fits = (
        ITERS == 2
        and 2 * inputs == LANES
        and points % LANES == 0
        and frames == SUBLANES
        and window_taps.shape[0] == NEXT_ROWS
        and lax.axis_size("beam") == 2
        and chan_local % (8 * BLOCK) == 0
        and half_rows % LANES == 0
        and frame_count & (frame_count - 1) == 0
        and chan_local * owners & (chan_local * owners - 1) == 0
        and half_rows % (4 * LANES // 2) == 0
        and beam_steering.shape[1] % LANES == 0
    )
    form = chunk_shards if fits else general_shards
    return form(samples, window_taps, sky_model, prior_gains, beam_steering, input_flags)


def solution(mesh):
    return jax.shard_map(
        shards,
        mesh=mesh,
        in_specs=(
            P(("group", "chan", "beam"), None, None, "tm"),
            P(),
            P(("group", "chan", "tm"), None, "beam", None),
            P(("group", "chan", "tm"), None, None),
            P(None, ("group", "beam")),
            P(("group", "chan", "tm"), None),
        ),
        out_specs=(
            P(("group", "chan", "tm"), None, "beam", None),
            P(("group", "chan", "tm"), None, "beam"),
            P(("group", "chan", "tm"), "beam", None),
        ),
        check_vma=False,
    )
```

```python
import functools
import math

import jax
import jax.numpy as jnp
import numpy as np
from jax import lax
from jax.experimental import pallas as pl
from jax.experimental.pallas import tpu as pltpu
from jax.sharding import PartitionSpec as P

NCH = 512
ITERS = 2


damping = 0.5
epsilon = 1e-06


def from_behind(block, axis, distance):
    devices = range(lax.axis_size(axis))
    route = [(i - distance, i) for i in devices if i - distance in devices]
    return lax.ppermute(block, axis, route)


def filter_bank(extended, window_taps, kept_count, frames):
    transform_count = window_taps.shape[1]
    tap_count = window_taps.shape[0]
    local_inputs = extended.shape[0]
    kept = jnp.arange(kept_count, dtype=jnp.int32)
    indices = jnp.arange(transform_count, dtype=jnp.int32)
    phases = (kept[:, None] * indices[None, :] % transform_count).astype(jnp.float32) * (
        2.0 * math.pi / transform_count
    )
    cosine = jnp.cos(phases)
    sine_part = jnp.sin(phases)
    real_in = extended[:, :transform_count]
    imag_in = extended[:, transform_count:]
    real_sum = jnp.zeros((local_inputs, kept_count, frames), jnp.float32)
    imag_sum = jnp.zeros((local_inputs, kept_count, frames), jnp.float32)
    for tap_index in range(tap_count):
        tap_row = window_taps[tap_index][None, :]
        cos_block = (cosine * tap_row / math.sqrt(transform_count)).astype(jnp.bfloat16)
        sin_block = (sine_part * tap_row / math.sqrt(transform_count)).astype(jnp.bfloat16)
        part_real = real_in[:, :, tap_index : tap_index + frames]
        part_imag = imag_in[:, :, tap_index : tap_index + frames]
        real_sum = (
            real_sum
            + jnp.einsum("kn,inf->ikf", cos_block, part_real, preferred_element_type=jnp.float32)
            + jnp.einsum("kn,inf->ikf", sin_block, part_imag, preferred_element_type=jnp.float32)
        )
        imag_sum = (
            imag_sum
            + jnp.einsum("kn,inf->ikf", cos_block, part_imag, preferred_element_type=jnp.float32)
            - jnp.einsum("kn,inf->ikf", sin_block, part_real, preferred_element_type=jnp.float32)
        )
    return jnp.stack([real_sum, imag_sum], axis=2).astype(jnp.bfloat16)


def steering_angles(beam_steering, channels, input_count, chan_total):
    positions = jnp.arange(input_count, dtype=jnp.int32)
    column = positions // (input_count // 4)
    within = positions % (input_count // 4)
    phase_index = (
        beam_steering[0][:, None] * column[None, :] * 64
        + beam_steering[1][:, None] * within[None, :]
    ) % 256
    scaled = phase_index[None] * (chan_total + channels)[:, None, None]
    return scaled.astype(jnp.float32) * (2.0 * math.pi / (512 * chan_total))


def cross_rows(owned_rows, all_rows):
    paired = owned_rows.reshape(owned_rows.shape[0], owned_rows.shape[1], -1)
    rotated = jnp.stack([owned_rows[:, :, 1], -owned_rows[:, :, 0]], axis=2).reshape(paired.shape)
    left = jnp.stack([paired, rotated], axis=1)
    columns = all_rows.reshape(all_rows.shape[0], all_rows.shape[1], -1)
    return jnp.einsum("isck,jck->csij", left, columns, preferred_element_type=jnp.float32)


def form_beams(whole_set, gains_part, weights, beam_steering, channels, chan_total):
    input_count = whole_set.shape[0]
    angles = steering_angles(beam_steering, channels, input_count, chan_total)
    cosine = jnp.cos(angles)
    sine_part = jnp.sin(angles)
    scale_factor = 1.0 / math.sqrt(input_count)
    gain_real = (gains_part[:, 0] * weights)[:, None, :]
    gain_imaginary = (gains_part[:, 1] * weights)[:, None, :]
    steering_real = ((gain_real * cosine - gain_imaginary * sine_part) * scale_factor).astype(
        jnp.bfloat16
    )
    steering_imaginary = ((gain_real * sine_part + gain_imaginary * cosine) * scale_factor).astype(
        jnp.bfloat16
    )
    spectrum_real = whole_set[:, :, 0]
    spectrum_imaginary = whole_set[:, :, 1]
    volt_real = jnp.einsum(
        "jan,njg->jag", steering_real, spectrum_real, preferred_element_type=jnp.float32
    ) - jnp.einsum(
        "jan,njg->jag", steering_imaginary, spectrum_imaginary, preferred_element_type=jnp.float32
    )
    volt_imag = jnp.einsum(
        "jan,njg->jag", steering_real, spectrum_imaginary, preferred_element_type=jnp.float32
    ) + jnp.einsum(
        "jan,njg->jag", steering_imaginary, spectrum_real, preferred_element_type=jnp.float32
    )
    return volt_real * volt_real + volt_imag * volt_imag


def matvec(matrix, vector):
    return jnp.einsum("crj,cj->cr", matrix, vector, precision=lax.Precision.HIGHEST)


def general_shards(samples, window_taps, sky_model, prior_gains, beam_steering, input_flags):
    local_inputs = samples.shape[0]
    transform_count = samples.shape[2]
    frames = samples.shape[3]
    tap_count = window_taps.shape[0]
    kept_count = NCH
    time_count = lax.axis_size("tm")
    beam_count = lax.axis_size("beam")
    time_index = lax.axis_index("tm")
    beam_index = lax.axis_index("beam")
    chan_index = lax.axis_index("chan")
    weights = input_flags.astype(jnp.float32)
    stacked = samples.reshape(local_inputs, 2 * transform_count, frames)
    previous = from_behind(stacked[:, :, frames - tap_count + 1 :], "tm", 1)
    extended = jnp.concatenate([previous, stacked], axis=2)
    spectra = filter_bank(extended, window_taps, kept_count, frames).reshape(
        1, local_inputs, kept_count, 2, 1, frames
    )
    mixed = lax.all_to_all(spectra, ("chan", "tm"), split_axis=2, concat_axis=0, tiled=True)
    blocks = mixed.reshape(
        mixed.shape[0] // time_count, time_count, local_inputs, mixed.shape[2], 2, frames
    )
    turned = jnp.transpose(blocks, (0, 2, 3, 4, 1, 5))
    joined = lax.all_gather(turned, "beam", axis=1, tiled=True)
    input_count = joined.shape[0] * joined.shape[1]
    chan_local = joined.shape[2]
    whole_set = joined.reshape(input_count, chan_local, 2, joined.shape[4] * frames)
    half_rows = input_count // beam_count
    owned_rows = lax.dynamic_slice_in_dim(whole_set, beam_index * half_rows, half_rows, 0)
    terms = cross_rows(owned_rows, whole_set)
    visibilities = (terms / whole_set.shape[3]).astype(jnp.bfloat16)
    channels = (chan_index * time_count + time_index) * chan_local + jnp.arange(
        chan_local, dtype=jnp.int32
    )
    beam_power = form_beams(whole_set, prior_gains, weights, beam_steering, channels, kept_count)
    vis_used = lax.optimization_barrier(visibilities).astype(jnp.float32)
    model_values = sky_model.astype(jnp.float32)
    weighted = jnp.stack(
        [
            vis_used[:, 0] * model_values[:, 0] + vis_used[:, 1] * model_values[:, 1],
            vis_used[:, 1] * model_values[:, 0] - vis_used[:, 0] * model_values[:, 1],
        ],
        axis=1,
    )
    model_power = model_values[:, 0] * model_values[:, 0] + model_values[:, 1] * model_values[:, 1]
    row_start = beam_index * half_rows
    current = prior_gains
    updated = lax.dynamic_slice_in_dim(current, row_start, half_rows, 2)
    for step_index in range(ITERS):
        masked_real = current[:, 0] * weights
        masked_imag = current[:, 1] * weights
        vectors = jnp.stack([masked_real, masked_imag], axis=2)
        products = jnp.einsum("csrj,cjv->csrv", weighted, vectors, precision=lax.Precision.HIGHEST)
        numer_real = products[:, 0, :, 0] - products[:, 1, :, 1]
        numer_imag = products[:, 0, :, 1] + products[:, 1, :, 0]
        denom = (
            matvec(
                model_power,
                weights * (current[:, 0] * current[:, 0] + current[:, 1] * current[:, 1]),
            )
            + epsilon
        )
        older = lax.dynamic_slice_in_dim(current, row_start, half_rows, 2)
        updated = damping * older + (1.0 - damping) * jnp.stack(
            [numer_real / denom, numer_imag / denom], axis=1
        )
        if step_index + 1 < ITERS:
            current = lax.all_gather(updated, "beam", axis=2, tiled=True)
    return (visibilities, updated, beam_power)


LANES = 128
SUBLANES = 8
NEXT_ROWS = 4
MIB = 2**20
UPDATE_LIMIT = 14 * MIB
NT = (((1,), (1,)), ((), ()))
TN = (((0,), (0,)), ((), ()))
NN = (((1,), (0,)), ((), ()))


def mxu(left, right, dims):
    return lax.dot_general(left, right, dims, preferred_element_type=jnp.float32)


def transform_rows(kept_count, transform_count, owners, shares):
    by_owner = np.arange(kept_count).reshape(owners, -1)
    ends = np.cumsum(shares)
    kept = np.concatenate(
        [by_owner[:, end - share : end].reshape(-1) for share, end in zip(shares, ends)]
    )
    phases = (kept[:, None] * np.arange(transform_count)[None, :] % transform_count) * (
        2.0 * math.pi / transform_count
    )
    table = np.concatenate([np.cos(phases), np.sin(phases)], axis=1) / math.sqrt(transform_count)
    return jnp.asarray(table.astype(jnp.bfloat16))


def transformed(owners, frames, table, windowed_ref, turned_ref, copies=()):
    rows = table.shape[0]
    width = turned_ref.shape[1]
    share = rows // owners
    total = windowed_ref.shape[0] // width
    step = 4
    for frame in range(0, total, step):
        some = min(step, total - frame)
        for copy in copies[frame : frame + some]:
            copy.wait()
        block = mxu(table, windowed_ref[frame * width : (frame + some) * width, :], NT)
        for i in range(some):
            at = frame + i
            part = block[:, i * width : (i + 1) * width]
            if at < frames:
                turned_ref[pl.ds(at, rows, stride=frames), :] = part
            else:
                first = rows * frames + (at - frames) * share
                for owner in range(owners):
                    turned_ref[pl.ds(first + owner * (total - frames) * share, share), :] = part[
                        owner * share : (owner + 1) * share
                    ]


def filter_kernel(
    owners,
    x_hbm,
    taps_hbm,
    table_hbm,
    windowed_hbm,
    out_ref,
    x_ref,
    table_ref,
    taps_ref,
    frames_ref,
    windowed_ref,
    turned_ref,
    sems,
):
    inputs, _, frames, points = x_ref.shape
    taps = taps_ref.shape[0]
    width = 2 * inputs
    pieces = sems.shape[0] - 3
    group = inputs // pieces
    table_copy = pltpu.make_async_copy(
        table_hbm.at[pl.ds(0, table_ref.shape[0])], table_ref, sems.at[pieces]
    )
    copies = [
        pltpu.make_async_copy(
            x_hbm.at[pl.ds(i * group, group)], x_ref.at[pl.ds(i * group, group)], sems.at[i]
        )
        for i in range(pieces)
    ]
    taps_copy = pltpu.make_async_copy(taps_hbm, taps_ref, sems.at[pieces + 2])
    taps_copy.start()
    for copy in copies:
        copy.start()
    taps_copy.wait()

    def spread(i, carry):
        for part in range(2):
            block = x_ref[i, part].astype(jnp.float32)
            for piece in range(points // LANES):
                here = pl.ds(pl.multiple_of(i * frames, frames), frames)
                frames_ref[part, piece, here, :] = block[:, piece * LANES : (piece + 1) * LANES]
        return carry

    for i, copy in enumerate(copies):
        copy.wait()
        lax.fori_loop(i * group, (i + 1) * group, spread, 0, unroll=4)

    table_copy.start()

    def window(piece, carry):
        lanes = pl.ds(pl.multiple_of(piece * LANES, LANES), LANES)
        upper = pl.ds(pl.multiple_of(points + piece * LANES, LANES), LANES)
        weights = taps_ref[:, lanes]
        weights = [
            jnp.broadcast_to(weights[tap : tap + 1], (2 * SUBLANES, LANES)) for tap in range(taps)
        ]
        for first in range(0, inputs, 2 * SUBLANES):
            for part in range(2):
                values = [
                    frames_ref[
                        part, piece, pl.ds(first * frames + frame, 2 * SUBLANES, stride=frames), :
                    ]
                    for frame in range(frames)
                ]
                for frame in range(frames + taps - 1):
                    total = None
                    for tap in range(taps):
                        source = frame + tap - (taps - 1)
                        if 0 <= source < frames:
                            term = values[source] * weights[tap]
                            total = term if total is None else total + term
                    base = frame * width + first
                    rows = slice(base, base + 2 * SUBLANES)
                    swapped = slice(base + inputs, base + inputs + 2 * SUBLANES)
                    total = total.astype(jnp.bfloat16)
                    if part == 0:
                        windowed_ref[rows, lanes] = total
                        windowed_ref[swapped, upper] = -total
                    else:
                        windowed_ref[rows, upper] = total
                        windowed_ref[swapped, lanes] = total
        return carry

    lax.fori_loop(0, points // LANES, window, 0)
    keep = pltpu.make_async_copy(windowed_ref, windowed_hbm, sems.at[pieces + 1])
    keep.start()
    table_copy.wait()
    transformed(owners, frames, table_ref[...], windowed_ref, turned_ref)
    share = table_ref.shape[0] // owners
    main = share * frames
    extra = share * (taps - 1)
    for owner in range(owners):
        out_ref[owner, :main, :] = turned_ref[owner * main : (owner + 1) * main, :].astype(
            jnp.bfloat16
        )
        first = owners * main + owner * extra
        out_ref[owner, main : main + extra, :] = turned_ref[first : first + extra, :].astype(
            jnp.bfloat16
        )
    keep.wait()


def rows_copies(source, target, sems, first=0):
    size = target.shape[0] // sems.shape[0]
    return [
        pltpu.make_async_copy(
            source.at[pl.ds(first + i * size, size)], target.at[pl.ds(i * size, size)], sems.at[i]
        )
        for i in range(sems.shape[0])
    ]


def spill_kernel(first, start, windowed_hbm, table_hbm, out_ref, windowed_ref, table_ref, sems):
    copies = rows_copies(windowed_hbm, windowed_ref, sems.at[pl.ds(0, 1)], first)
    copies += rows_copies(table_hbm, table_ref, sems.at[pl.ds(1, 1)], start)
    for copy in copies:
        copy.start()
    for copy in copies:
        copy.wait()
    frames, _, width = out_ref.shape
    block = mxu(table_ref[...], windowed_ref[...], NT)
    for frame in range(frames):
        out_ref[frame] = block[:, frame * width : (frame + 1) * width].astype(jnp.bfloat16)


def filter_more_kernel(
    owners, start, windowed_hbm, table_hbm, turned_ref, windowed_ref, table_ref, sems
):
    frames = sems.shape[0] - 1
    copies = rows_copies(windowed_hbm, windowed_ref, sems.at[pl.ds(0, frames)])
    table_copies = rows_copies(table_hbm, table_ref, sems.at[pl.ds(frames, 1)], start)
    for copy in table_copies + copies:
        copy.start()
    for copy in table_copies:
        copy.wait()
    transformed(owners, frames, table_ref[...], windowed_ref, turned_ref, copies)


def added_kernel(turned_ref, added_ref, out_ref, total_ref):
    owners, main, _ = out_ref.shape
    nexts, rows, _ = added_ref.shape
    frames = turned_ref.shape[0] // rows
    total_ref[...] = turned_ref[...]
    for frame in range(nexts):
        here = pl.ds(frame, rows, stride=frames)
        total_ref[here, :] = turned_ref[here, :] + added_ref[frame].astype(jnp.float32)
    for owner in range(owners):
        out_ref[owner] = total_ref[owner * main : (owner + 1) * main, :].astype(jnp.bfloat16)


def filtered(samples, window_taps, kept_count, owners, shares):
    inputs, _, points, frames = samples.shape
    taps = window_taps.shape[0]
    width = 2 * inputs
    table = transform_rows(kept_count, points, owners, shares)
    by_frame = jnp.transpose(samples, (0, 1, 3, 2))
    by_frame = pltpu.with_memory_space_constraint(by_frame, pltpu.HBM)
    table = pltpu.with_memory_space_constraint(table, pltpu.HBM)
    window_taps = pltpu.with_memory_space_constraint(window_taps, pltpu.HBM)
    pieces = points // LANES
    anywhere = pl.BlockSpec(memory_space=pl.ANY)
    vmem = pl.BlockSpec(memory_space=pltpu.VMEM)
    windowed_shape = ((frames + taps - 1) * width, 2 * points)
    rows = owners * shares[0]
    windowed, first = pl.pallas_call(
        functools.partial(filter_kernel, owners),
        out_shape=[
            pltpu.HBM(windowed_shape, jnp.bfloat16),
            jax.ShapeDtypeStruct((owners, shares[0] * (frames + taps - 1), width), jnp.bfloat16),
        ],
        in_specs=[anywhere, anywhere, anywhere],
        out_specs=[anywhere, vmem],
        scratch_shapes=[
            pltpu.VMEM(by_frame.shape, jnp.bfloat16),
            pltpu.VMEM((rows, 2 * points), jnp.bfloat16),
            pltpu.VMEM(window_taps.shape, jnp.float32),
            pltpu.VMEM((2, pieces, inputs * frames, LANES), jnp.float32),
            pltpu.VMEM(windowed_shape, jnp.bfloat16),
            pltpu.VMEM((rows * (frames + taps - 1), width), jnp.float32),
            pltpu.SemaphoreType.DMA((7,)),
        ],
        compiler_params=pltpu.CompilerParams(vmem_limit_bytes=32 * MIB),
        name="filter",
    )(by_frame, window_taps, table)
    windowed = pltpu.with_memory_space_constraint(windowed, pltpu.HBM)

    def more(chunk, start):
        rows = owners * shares[chunk]
        spill = pl.pallas_call(
            functools.partial(spill_kernel, frames * width, start),
            out_shape=jax.ShapeDtypeStruct((taps - 1, rows, width), jnp.bfloat16),
            in_specs=[anywhere, anywhere],
            out_specs=vmem,
            scratch_shapes=[
                pltpu.VMEM(((taps - 1) * width, 2 * points), jnp.bfloat16),
                pltpu.VMEM((rows, 2 * points), jnp.bfloat16),
                pltpu.SemaphoreType.DMA((2,)),
            ],
            compiler_params=pltpu.CompilerParams(vmem_limit_bytes=24 * MIB),
            name="spill",
        )(windowed, table)
        added = from_behind(spill, "tm", 1)
        turned = pl.pallas_call(
            functools.partial(filter_more_kernel, owners, start),
            out_shape=jax.ShapeDtypeStruct((rows * frames, width), jnp.float32),
            in_specs=[anywhere, anywhere],
            out_specs=vmem,
            scratch_shapes=[
                pltpu.VMEM((frames * width, 2 * points), jnp.bfloat16),
                pltpu.VMEM((rows, 2 * points), jnp.bfloat16),
                pltpu.SemaphoreType.DMA((frames + 1,)),
            ],
            compiler_params=pltpu.CompilerParams(vmem_limit_bytes=24 * MIB),
            name="filter_more",
        )(windowed, table)
        return pl.pallas_call(
            added_kernel,
            out_shape=jax.ShapeDtypeStruct((owners, shares[chunk] * frames, width), jnp.bfloat16),
            in_specs=[vmem, vmem],
            out_specs=vmem,
            scratch_shapes=[pltpu.VMEM((rows * frames, width), jnp.float32)],
            compiler_params=pltpu.CompilerParams(vmem_limit_bytes=24 * MIB),
            name="added",
        )(turned, added)

    sent = [first]
    start = rows
    for chunk in range(1, len(shares)):
        sent.append(more(chunk, start))
        start += owners * shares[chunk]
    return sent


def gain_terms(real, imag, gains, flags):
    weights = flags.astype(jnp.float32)
    gain_real = gains[0:1] * weights
    gain_imag = gains[1:2] * weights
    turned_real = real * gain_real + imag * gain_imag
    turned_imag = imag * gain_real - real * gain_imag
    power = weights * (gains[0:1] * gains[0:1] + gains[1:2] * gains[1:2])
    return turned_real, turned_imag, power


def denominators(power, model_real, model_imag):
    model_power = model_real * model_real + model_imag * model_imag
    terms = model_power * jnp.broadcast_to(power.astype(jnp.bfloat16), model_power.shape)
    folded = terms[:, :LANES]
    for first in range(LANES, terms.shape[1], LANES):
        folded = folded + terms[:, first : first + LANES]
    return mxu(jnp.ones((SUBLANES, LANES), jnp.bfloat16), folded, NT)[0:1] + epsilon


def updated_gains(own, turned, model_real, model_imag, denom, older):
    real, imag = turned
    straight = jnp.concatenate([real, imag], axis=0).astype(jnp.bfloat16)
    crossed = jnp.concatenate([-imag, real], axis=0).astype(jnp.bfloat16)
    modelled = mxu(straight, model_real, NT) + mxu(crossed, model_imag, NT)
    frames = real.shape[0]
    modelled_real = modelled[:frames]
    modelled_imag = modelled[frames:]
    own_real, own_imag = own
    numer_real = jnp.sum(own_real * modelled_real + own_imag * modelled_imag, axis=0, keepdims=True)
    numer_imag = jnp.sum(own_imag * modelled_real - own_real * modelled_imag, axis=0, keepdims=True)
    numer = jnp.concatenate([numer_real, numer_imag], axis=0) / frames
    return damping * older + (1.0 - damping) * (numer / denom)


def own_half(values, core):
    half = values.shape[1] // 2
    return jnp.where(core == 0, values[:, :half], values[:, half:])


def model_kernel(
    base, step, reach, own_hbm, model_hbm, centre_ref, steering_ref, model_ref, table_ref, sem
):
    del own_hbm
    count = min(MODEL_BLOCK, model_ref.shape[0])
    copy = pltpu.make_async_copy(
        model_hbm.at[pl.ds(base, count)], model_ref.at[pl.ds(0, count)], sem
    )
    copy.start()
    steering_tables(centre_ref[0], steering_ref, table_ref, step, reach)
    copy.wait()


def first_kernel(
    times, base, core_ref, own_ref, other_ref, model_hbm, gains_ref, flags_ref, here_ref, *refs
):
    del here_ref
    spectra_ref, updated_ref, model_ref, next_ref, sems = refs
    core = core_ref[0]
    share = spectra_ref.shape[0]
    sources, rows, width = own_ref.shape
    frames = spectra_ref.shape[1] // 2 // times
    nexts = rows // share - frames
    columns = sources // times
    lane = lax.broadcasted_iota(jnp.int32, (frames, width), 1)
    row = lax.broadcasted_iota(jnp.int32, (frames, width), 0)
    low = lane < width // 2
    count = BLOCK

    def copy(i):
        here = pl.ds(i * VIS_BLOCK, VIS_BLOCK)
        there = pl.ds(base + i * VIS_BLOCK, VIS_BLOCK)
        return pltpu.make_async_copy(model_hbm.at[there], model_ref.at[here], sems.at[i])

    groups = share // VIS_BLOCK
    there = min(MODEL_BLOCK, share) // VIS_BLOCK
    ahead = 3
    for i in range(there, min(there + ahead, groups)):
        copy(i).start()
    if nexts:
        for source in range(sources):
            for side, ref in enumerate((own_ref, other_ref)):
                next_ref[side, source] = ref[source, share * frames :, :].astype(jnp.float32)

    def assemble(i):
        main_rows = pl.ds(pl.multiple_of(i * (count * frames), count * frames), count * frames)

        def loaded(side, column, time):
            ref = (own_ref, other_ref)[side]
            source = column * times + time
            block = ref[source, main_rows, :].astype(jnp.float32)
            extra = []
            if time > 0:
                extra = [
                    next_ref[
                        side, source - 1, pl.ds(pl.multiple_of(share * k + i * count, count), count), :
                    ]
                    for k in range(nexts)
                ]
            return block, extra

        def one(value, c):
            block, extra = value
            block = block[c * frames : (c + 1) * frames]
            for k, more in enumerate(extra):
                block = block + jnp.where(row == k, more[c : c + 1], 0.0)
            return block

        blocks = {
            (column, time): (loaded(0, column, time), loaded(1, column, time))
            for column in range(columns)
            for time in range(times)
        }
        for c in range(count):
            real_rows = []
            imag_rows = []
            for time in range(times):
                reals = []
                imags = []
                for column in range(columns):
                    own, other = blocks[column, time]
                    own = one(own, c)
                    other = one(other, c)
                    first = jnp.where(core == 0, own, other)
                    second = jnp.where(core == 0, other, own)
                    reals.append(jnp.where(low, first, pltpu.roll(second, width // 2, 1)))
                    imags.append(jnp.where(low, pltpu.roll(first, width // 2, 1), second))
                real_rows.append(jnp.concatenate(reals, axis=1))
                imag_rows.append(jnp.concatenate(imags, axis=1))
            spectra = jnp.concatenate(real_rows + imag_rows, axis=0)
            spectra_ref[i * count + c] = spectra.astype(jnp.bfloat16)

    def update(i):
        for part in range(count // VIS_BLOCK):
            group = i * (count // VIS_BLOCK) + part

            @pl.when(group >= there)
            def _():
                copy(group).wait()

                @pl.when(group + ahead < groups)
                def _():
                    copy(group + ahead).start()

        for c in range(count):
            here = i * count + c
            values = spectra_ref[here].astype(jnp.float32)
            half = values.shape[0] // 2
            real = values[:half]
            imag = values[half:]
            gains = gains_ref[base + here]
            flags = flags_ref[pl.ds(base + here, 1), :]
            model_real = model_ref[here, 0]
            model_imag = model_ref[here, 1]
            turned_real, turned_imag, power = gain_terms(real, imag, gains, flags)
            updated_ref[here] = updated_gains(
                (own_half(real, core), own_half(imag, core)),
                (turned_real, turned_imag),
                model_real,
                model_imag,
                denominators(power, model_real, model_imag),
                own_half(gains, core),
            )

    def step(i, carry):
        update(i)
        assemble(i + 1)
        return carry

    last = share // count - 1
    assemble(0)
    lax.fori_loop(0, last, step, 0)
    update(last)


def second_kernel(
    base, core_ref, spectra_ref, model_ref, own_ref, other_ref, flags_ref, *refs
):
    visibilities_hbm, updated_hbm, ready_ref, updated_ref, sems, sem = refs[-6:]
    core = core_ref[0]
    share = spectra_ref.shape[0]
    slots, count = ready_ref.shape[:2]
    pieces = sems.shape[1]
    size = count // pieces
    steps = share // count

    def copy(i, slot, piece):
        return pltpu.make_async_copy(
            ready_ref.at[slot, pl.ds(piece * size, size)],
            visibilities_hbm.at[pl.ds(base + i * count + piece * size, size)],
            sems.at[slot, piece],
        )

    def step(i, carry):
        slot = lax.rem(i, slots)

        @pl.when(i >= slots)
        def _():
            for piece in range(pieces):
                copy(i - slots, slot, piece).wait()

        for c in range(count):
            here = i * count + c
            spectra = spectra_ref[here]
            half = spectra.shape[0] // 2
            values = spectra.astype(jnp.float32)
            real = values[:half]
            imag = values[half:]
            own_real = own_half(real, core)
            own_imag = own_half(imag, core)
            paired = (jnp.concatenate([own_real, own_imag], axis=0) / half).astype(jnp.bfloat16)
            rotated = (jnp.concatenate([own_imag, -own_real], axis=0) / half).astype(jnp.bfloat16)
            ready_ref[slot, c, 0] = mxu(paired, spectra, TN).astype(jnp.bfloat16)
            ready_ref[slot, c, 1] = mxu(rotated, spectra, TN).astype(jnp.bfloat16)
            if c % size == size - 1:
                copy(i, slot, c // size).start()
            own = own_ref[here]
            other = other_ref[here]
            first = jnp.where(core == 0, own, other)
            second = jnp.where(core == 0, other, own)
            gains = jnp.concatenate([first, second], axis=1)
            flags = flags_ref[pl.ds(base + here, 1), :]
            turned_real, turned_imag, power = gain_terms(real, imag, gains, flags)
            model_real = model_ref[here, 0]
            model_imag = model_ref[here, 1]
            updated_ref[here] = updated_gains(
                (own_real, own_imag),
                (turned_real, turned_imag),
                model_real,
                model_imag,
                denominators(power, model_real, model_imag),
                own,
            )
        return carry

    lax.fori_loop(0, steps, step, 0)
    last = pltpu.make_async_copy(updated_ref, updated_hbm.at[pl.ds(base, share)], sem)
    last.start()
    for i in range(max(0, steps - slots), steps):
        for piece in range(pieces):
            copy(i, i % slots, piece).wait()
    last.wait()


def series_length(reach):
    terms = 1
    while 2.0 * (0.5 * reach) ** terms / math.factorial(terms) >= 2.0**-22:
        terms += 1
    return terms


def bessel(order, x, reach):
    count = 1
    while (0.5 * reach) ** (2 * count) / math.factorial(count) ** 2 >= 2.0**-26:
        count += 1
    square = x * x * -0.25
    total = jnp.full_like(x, 1.0 / (math.factorial(count - 1) * math.factorial(count - 1 + order)))
    for m in reversed(range(count - 1)):
        total = total * square + 1.0 / (math.factorial(m) * math.factorial(m + order))
    for _ in range(order):
        total = total * (0.5 * x)
    return total


def turns(count, period):
    quarter = period // 4
    quadrant = lax.shift_right_logical(count + period // 8, quarter.bit_length() - 1)
    angle = (count - quadrant * quarter).astype(jnp.float32) * (2.0 * math.pi / period)
    square = angle * angle
    sine_part = jnp.full_like(angle, 1.0 / math.factorial(9))
    cosine = jnp.full_like(angle, 1.0 / math.factorial(8))
    for power in (7, 5, 3, 1):
        sign = -1.0 if power % 4 == 3 else 1.0
        sine_part = sine_part * square + sign / math.factorial(power)
        cosine = cosine * square + sign / math.factorial(power - 1)
    sine_part = sine_part * angle
    odd = (quadrant & 1) == 1
    real = jnp.where(odd, sine_part, cosine)
    imag = jnp.where(odd, cosine, sine_part)
    real = jnp.where(((quadrant + 1) & 2) == 2, -real, real)
    imag = jnp.where((quadrant & 2) == 2, -imag, imag)
    return real, imag


def steering_tables(centre, steering_ref, table_ref, step, reach):
    inputs = table_ref.shape[1] // 2
    beams = table_ref.shape[2] // 2
    quarter = inputs // 4
    for column in range(4):
        for first in range(0, quarter, 4 * SUBLANES):
            shape = (4 * SUBLANES, beams)
            within = lax.broadcasted_iota(jnp.int32, shape, 0) + first
            phase_index = (steering_ref[0:1, :] * (column * 64) + steering_ref[1:2, :] * within) & 255
            cosine, sine_part = turns(phase_index * centre, round(4.0 * math.pi / step))
            offset = (phase_index - 128).astype(jnp.float32) * (reach * step)
            at = column * quarter + first
            rows = slice(at, at + shape[0])
            lower = slice(inputs + at, inputs + at + shape[0])
            for term in range(table_ref.shape[0]):
                real, imag = (
                    (cosine, sine_part),
                    (-sine_part, cosine),
                    (-cosine, -sine_part),
                    (sine_part, -cosine),
                )[term % 4]
                factor = bessel(term, offset, 128 * reach * step) * (2.0 if term else 1.0)
                real = factor * real
                imag = factor * imag
                real = real.astype(jnp.bfloat16)
                imag = imag.astype(jnp.bfloat16)
                table_ref[term, rows, :beams] = real
                table_ref[term, rows, beams:] = imag
                table_ref[term, lower, :beams] = -imag
                table_ref[term, lower, beams:] = real


def beams_kernel(base, spectra_ref, gains_ref, flags_ref, table_ref, *refs):
    power_hbm, power_ref, left_ref, sem = refs[-4:]
    count, doubled, inputs = spectra_ref.shape
    frames = doubled // 2
    scale = 1.0 / math.sqrt(inputs)
    middle = 0.5 * (count - 1)
    terms = table_ref.shape[0]
    for c in range(count):
        values = spectra_ref[c].astype(jnp.float32)
        real = values[:frames]
        imag = values[frames:]
        at = base + c
        weights = flags_ref[at : at + 1].astype(jnp.float32) * scale
        gain_real = gains_ref[at, 0:1] * weights
        gain_imag = gains_ref[at, 1:2] * weights
        lit_real = real * gain_real - imag * gain_imag
        lit_imag = real * gain_imag + imag * gain_real
        rows = slice(c * frames, (c + 1) * frames)
        for term in range(terms):
            power = math.cos(term * math.acos((c - middle) / max(middle, 0.5)))
            left_ref[term, rows, :inputs] = (lit_real * power).astype(jnp.bfloat16)
            left_ref[term, rows, inputs:] = (lit_imag * power).astype(jnp.bfloat16)
    total = mxu(left_ref[0], table_ref[0], NN)
    for term in range(1, terms):
        total = total + mxu(left_ref[term], table_ref[term], NN)
    beams = total.shape[1] // 2
    real = total[:, :beams]
    imag = total[:, beams:]
    power_ref[...] = (real * real + imag * imag).reshape(count, frames, beams)
    copy = pltpu.make_async_copy(power_ref, power_hbm.at[pl.ds(base, count)], sem)
    copy.start()
    copy.wait()


def formed_beams(chunk, gains, flags, earlier):
    base, table, spectra = chunk
    share, doubled, input_count = spectra.shape
    frame_count = doubled // 2
    beams = table.shape[2] // 2
    earlier = [] if earlier is None else [earlier]
    vmem = pl.BlockSpec(memory_space=pltpu.VMEM)
    return pl.pallas_call(
        functools.partial(beams_kernel, base),
        in_specs=[vmem] * 4 + [pl.BlockSpec(memory_space=pl.ANY)] * len(earlier),
        out_specs=pl.BlockSpec(memory_space=pl.ANY),
        out_shape=jax.ShapeDtypeStruct((gains.shape[0], frame_count, beams), jnp.float32),
        input_output_aliases={4: 0} if earlier else {},
        scratch_shapes=[
            pltpu.VMEM((share, frame_count, beams), jnp.float32),
            pltpu.VMEM((table.shape[0], share * frame_count, 2 * input_count), jnp.bfloat16),
            pltpu.SemaphoreType.DMA,
        ],
        compiler_params=pltpu.CompilerParams(vmem_limit_bytes=UPDATE_LIMIT),
        name="beams",
    )(spectra, gains, flags, table, *earlier)


def chunk_shards(samples, window_taps, sky_model, prior_gains, beam_steering, input_flags):
    frames = samples.shape[3]
    chan_local, _, half_rows, input_count = sky_model.shape
    times = lax.axis_size("tm")
    owners = lax.axis_size("chan") * times
    core = lax.axis_index("beam").astype(jnp.int32).reshape(1)
    first_channel = (lax.axis_index("chan") * times + lax.axis_index("tm")) * chan_local
    kept_count = chan_local * owners
    frame_count = frames * times
    beams = beam_steering.shape[1]
    shares = chunk_shares(chan_local)
    bases = [sum(shares[:chunk]) for chunk in range(len(shares))]
    centres = [
        (2 * (kept_count + first_channel + base) + share - 1).astype(jnp.int32).reshape(1)
        for base, share in zip(bases, shares)
    ]
    sent = filtered(samples, window_taps, kept_count, owners, shares)
    swap = [(0, 1), (1, 0)]
    smem = pl.BlockSpec(memory_space=pltpu.SMEM)
    vmem = pl.BlockSpec(memory_space=pltpu.VMEM)
    anywhere = pl.BlockSpec(memory_space=pl.ANY)
    step = 2.0 * math.pi / (512 * kept_count)

    sent[0], gains, flags, steering, core, centres = lax.optimization_barrier(
        (sent[0], prior_gains, input_flags, beam_steering, core, centres)
    )
    visibilities = None
    beam_power = None
    gains_new = None
    before = None
    for chunk, (base, share) in enumerate(zip(bases, shares)):
        own = lax.all_to_all(sent[chunk], ("chan", "tm"), 0, 0, tiled=True)
        if before is not None:
            beam_power = formed_beams(before, gains, flags, beam_power)
            own, gains_new, beam_power = lax.optimization_barrier((own, gains_new, beam_power))
        other = lax.ppermute(own, "beam", swap)
        model_shape = (share, *sky_model.shape[1:])
        reach = max(0.5 * (share - 1), 0.5)
        table_shape = (series_length(128 * reach * step), 2 * input_count, 2 * beams)
        model, table = pl.pallas_call(
            functools.partial(model_kernel, base, step, reach),
            in_specs=[anywhere, anywhere, smem, vmem],
            out_specs=[vmem, vmem],
            out_shape=[
                pltpu.VMEM(model_shape, sky_model.dtype),
                jax.ShapeDtypeStruct(table_shape, jnp.bfloat16),
            ],
            scratch_shapes=[pltpu.SemaphoreType.DMA],
            compiler_params=pltpu.CompilerParams(vmem_limit_bytes=UPDATE_LIMIT),
            name="model",
        )(own, sky_model, centres[chunk], steering)
        model = pltpu.with_memory_space_constraint(model, pltpu.VMEM)
        half_shape = jax.ShapeDtypeStruct((share, 2, half_rows), jnp.float32)
        spectra, gains_own, model = pl.pallas_call(
            functools.partial(first_kernel, times, base),
            in_specs=[smem, vmem, vmem, anywhere, vmem, vmem, vmem],
            out_specs=[vmem, vmem, vmem],
            out_shape=[
                jax.ShapeDtypeStruct((share, 2 * frame_count, input_count), jnp.bfloat16),
                half_shape,
                pltpu.VMEM(model_shape, sky_model.dtype),
            ],
            input_output_aliases={6: 2},
            scratch_shapes=[
                pltpu.VMEM((2, owners, max(own.shape[1] - share * frames, SUBLANES), own.shape[2]), jnp.float32),
                pltpu.SemaphoreType.DMA((share // VIS_BLOCK,)),
            ],
            compiler_params=pltpu.CompilerParams(vmem_limit_bytes=UPDATE_LIMIT),
            name="first_update",
        )(core, own, other, sky_model, gains, flags, model)
        model = pltpu.with_memory_space_constraint(model, pltpu.VMEM)
        gains_other = lax.ppermute(gains_own, "beam", swap)
        before = (base, table, spectra)
        if chunk == len(shares) - 1:
            beam_power = formed_beams(before, gains, flags, beam_power)
        earlier = [] if visibilities is None else [visibilities, gains_new]
        visibilities, gains_new = pl.pallas_call(
            functools.partial(second_kernel, base),
            in_specs=[smem] + [vmem] * 5 + [anywhere] * len(earlier),
            out_specs=[anywhere, anywhere],
            out_shape=[
                jax.ShapeDtypeStruct(sky_model.shape, jnp.bfloat16),
                jax.ShapeDtypeStruct((chan_local, 2, half_rows), jnp.float32),
            ],
            scratch_shapes=[
                pltpu.VMEM((2, BLOCK, 2, half_rows, input_count), jnp.bfloat16),
                pltpu.VMEM((share, 2, half_rows), jnp.float32),
                pltpu.SemaphoreType.DMA((2, 4)),
                pltpu.SemaphoreType.DMA,
            ],
            input_output_aliases={6: 0, 7: 1} if earlier else {},
            compiler_params=pltpu.CompilerParams(vmem_limit_bytes=UPDATE_LIMIT),
            name="second_update",
        )(core, spectra, model, gains_own, gains_other, flags, *earlier)
    return (
        visibilities,
        gains_new,
        jnp.transpose(beam_power, (0, 2, 1)),
    )


BLOCK = 8
VIS_BLOCK = 4
MODEL_BLOCK = 8


def chunk_shares(chan_local):
    blocks = chan_local // BLOCK
    first = blocks * 3 // 8
    return [first * BLOCK, (blocks - first) * BLOCK]


def shards(samples, window_taps, sky_model, prior_gains, beam_steering, input_flags):
    inputs, _, points, frames = samples.shape
    chan_local, _, half_rows, input_count = sky_model.shape
    frame_count = frames * lax.axis_size("tm")
    owners = lax.axis_size("chan") * lax.axis_size("tm")
    fits = (
        ITERS == 2
        and 2 * inputs == LANES
        and points % LANES == 0
        and frames == SUBLANES
        and window_taps.shape[0] == NEXT_ROWS
        and lax.axis_size("beam") == 2
        and chan_local % (8 * BLOCK) == 0
        and half_rows % LANES == 0
        and frame_count & (frame_count - 1) == 0
        and chan_local * owners & (chan_local * owners - 1) == 0
        and half_rows % (4 * LANES // 2) == 0
        and beam_steering.shape[1] % LANES == 0
    )
    form = chunk_shards if fits else general_shards
    return form(samples, window_taps, sky_model, prior_gains, beam_steering, input_flags)


def solution(mesh):
    return jax.shard_map(
        shards,
        mesh=mesh,
        in_specs=(
            P(("group", "chan", "beam"), None, None, "tm"),
            P(),
            P(("group", "chan", "tm"), None, "beam", None),
            P(("group", "chan", "tm"), None, None),
            P(None, ("group", "beam")),
            P(("group", "chan", "tm"), None),
        ),
        out_specs=(
            P(("group", "chan", "tm"), None, "beam", None),
            P(("group", "chan", "tm"), None, "beam"),
            P(("group", "chan", "tm"), "beam", None),
        ),
        check_vma=False,
    )
```

```python
import functools
import math

import jax
import jax.numpy as jnp
import numpy as np
from jax import lax
from jax.experimental import pallas as pl
from jax.experimental.pallas import tpu as pltpu
from jax.sharding import PartitionSpec as P

NCH = 512
ITERS = 2


damping = 0.5
epsilon = 1e-06


def from_behind(block, axis, distance):
    devices = range(lax.axis_size(axis))
    route = [(i - distance, i) for i in devices if i - distance in devices]
    return lax.ppermute(block, axis, route)


def filter_bank(extended, window_taps, kept_count, frames):
    transform_count = window_taps.shape[1]
    tap_count = window_taps.shape[0]
    local_inputs = extended.shape[0]
    kept = jnp.arange(kept_count, dtype=jnp.int32)
    indices = jnp.arange(transform_count, dtype=jnp.int32)
    phases = (kept[:, None] * indices[None, :] % transform_count).astype(jnp.float32) * (
        2.0 * math.pi / transform_count
    )
    cosine = jnp.cos(phases)
    sine_part = jnp.sin(phases)
    real_in = extended[:, :transform_count]
    imag_in = extended[:, transform_count:]
    real_sum = jnp.zeros((local_inputs, kept_count, frames), jnp.float32)
    imag_sum = jnp.zeros((local_inputs, kept_count, frames), jnp.float32)
    for tap_index in range(tap_count):
        tap_row = window_taps[tap_index][None, :]
        cos_block = (cosine * tap_row / math.sqrt(transform_count)).astype(jnp.bfloat16)
        sin_block = (sine_part * tap_row / math.sqrt(transform_count)).astype(jnp.bfloat16)
        part_real = real_in[:, :, tap_index : tap_index + frames]
        part_imag = imag_in[:, :, tap_index : tap_index + frames]
        real_sum = (
            real_sum
            + jnp.einsum("kn,inf->ikf", cos_block, part_real, preferred_element_type=jnp.float32)
            + jnp.einsum("kn,inf->ikf", sin_block, part_imag, preferred_element_type=jnp.float32)
        )
        imag_sum = (
            imag_sum
            + jnp.einsum("kn,inf->ikf", cos_block, part_imag, preferred_element_type=jnp.float32)
            - jnp.einsum("kn,inf->ikf", sin_block, part_real, preferred_element_type=jnp.float32)
        )
    return jnp.stack([real_sum, imag_sum], axis=2).astype(jnp.bfloat16)


def steering_angles(beam_steering, channels, input_count, chan_total):
    positions = jnp.arange(input_count, dtype=jnp.int32)
    column = positions // (input_count // 4)
    within = positions % (input_count // 4)
    phase_index = (
        beam_steering[0][:, None] * column[None, :] * 64
        + beam_steering[1][:, None] * within[None, :]
    ) % 256
    scaled = phase_index[None] * (chan_total + channels)[:, None, None]
    return scaled.astype(jnp.float32) * (2.0 * math.pi / (512 * chan_total))


def cross_rows(owned_rows, all_rows):
    paired = owned_rows.reshape(owned_rows.shape[0], owned_rows.shape[1], -1)
    rotated = jnp.stack([owned_rows[:, :, 1], -owned_rows[:, :, 0]], axis=2).reshape(paired.shape)
    left = jnp.stack([paired, rotated], axis=1)
    columns = all_rows.reshape(all_rows.shape[0], all_rows.shape[1], -1)
    return jnp.einsum("isck,jck->csij", left, columns, preferred_element_type=jnp.float32)


def form_beams(whole_set, gains_part, weights, beam_steering, channels, chan_total):
    input_count = whole_set.shape[0]
    angles = steering_angles(beam_steering, channels, input_count, chan_total)
    cosine = jnp.cos(angles)
    sine_part = jnp.sin(angles)
    scale_factor = 1.0 / math.sqrt(input_count)
    gain_real = (gains_part[:, 0] * weights)[:, None, :]
    gain_imaginary = (gains_part[:, 1] * weights)[:, None, :]
    steering_real = ((gain_real * cosine - gain_imaginary * sine_part) * scale_factor).astype(
        jnp.bfloat16
    )
    steering_imaginary = ((gain_real * sine_part + gain_imaginary * cosine) * scale_factor).astype(
        jnp.bfloat16
    )
    spectrum_real = whole_set[:, :, 0]
    spectrum_imaginary = whole_set[:, :, 1]
    volt_real = jnp.einsum(
        "jan,njg->jag", steering_real, spectrum_real, preferred_element_type=jnp.float32
    ) - jnp.einsum(
        "jan,njg->jag", steering_imaginary, spectrum_imaginary, preferred_element_type=jnp.float32
    )
    volt_imag = jnp.einsum(
        "jan,njg->jag", steering_real, spectrum_imaginary, preferred_element_type=jnp.float32
    ) + jnp.einsum(
        "jan,njg->jag", steering_imaginary, spectrum_real, preferred_element_type=jnp.float32
    )
    return volt_real * volt_real + volt_imag * volt_imag


def matvec(matrix, vector):
    return jnp.einsum("crj,cj->cr", matrix, vector, precision=lax.Precision.HIGHEST)


def general_shards(samples, window_taps, sky_model, prior_gains, beam_steering, input_flags):
    local_inputs = samples.shape[0]
    transform_count = samples.shape[2]
    frames = samples.shape[3]
    tap_count = window_taps.shape[0]
    kept_count = NCH
    time_count = lax.axis_size("tm")
    beam_count = lax.axis_size("beam")
    time_index = lax.axis_index("tm")
    beam_index = lax.axis_index("beam")
    chan_index = lax.axis_index("chan")
    weights = input_flags.astype(jnp.float32)
    stacked = samples.reshape(local_inputs, 2 * transform_count, frames)
    previous = from_behind(stacked[:, :, frames - tap_count + 1 :], "tm", 1)
    extended = jnp.concatenate([previous, stacked], axis=2)
    spectra = filter_bank(extended, window_taps, kept_count, frames).reshape(
        1, local_inputs, kept_count, 2, 1, frames
    )
    mixed = lax.all_to_all(spectra, ("chan", "tm"), split_axis=2, concat_axis=0, tiled=True)
    blocks = mixed.reshape(
        mixed.shape[0] // time_count, time_count, local_inputs, mixed.shape[2], 2, frames
    )
    turned = jnp.transpose(blocks, (0, 2, 3, 4, 1, 5))
    joined = lax.all_gather(turned, "beam", axis=1, tiled=True)
    input_count = joined.shape[0] * joined.shape[1]
    chan_local = joined.shape[2]
    whole_set = joined.reshape(input_count, chan_local, 2, joined.shape[4] * frames)
    half_rows = input_count // beam_count
    owned_rows = lax.dynamic_slice_in_dim(whole_set, beam_index * half_rows, half_rows, 0)
    terms = cross_rows(owned_rows, whole_set)
    visibilities = (terms / whole_set.shape[3]).astype(jnp.bfloat16)
    channels = (chan_index * time_count + time_index) * chan_local + jnp.arange(
        chan_local, dtype=jnp.int32
    )
    beam_power = form_beams(whole_set, prior_gains, weights, beam_steering, channels, kept_count)
    vis_used = lax.optimization_barrier(visibilities).astype(jnp.float32)
    model_values = sky_model.astype(jnp.float32)
    weighted = jnp.stack(
        [
            vis_used[:, 0] * model_values[:, 0] + vis_used[:, 1] * model_values[:, 1],
            vis_used[:, 1] * model_values[:, 0] - vis_used[:, 0] * model_values[:, 1],
        ],
        axis=1,
    )
    model_power = model_values[:, 0] * model_values[:, 0] + model_values[:, 1] * model_values[:, 1]
    row_start = beam_index * half_rows
    current = prior_gains
    updated = lax.dynamic_slice_in_dim(current, row_start, half_rows, 2)
    for step_index in range(ITERS):
        masked_real = current[:, 0] * weights
        masked_imag = current[:, 1] * weights
        vectors = jnp.stack([masked_real, masked_imag], axis=2)
        products = jnp.einsum("csrj,cjv->csrv", weighted, vectors, precision=lax.Precision.HIGHEST)
        numer_real = products[:, 0, :, 0] - products[:, 1, :, 1]
        numer_imag = products[:, 0, :, 1] + products[:, 1, :, 0]
        denom = (
            matvec(
                model_power,
                weights * (current[:, 0] * current[:, 0] + current[:, 1] * current[:, 1]),
            )
            + epsilon
        )
        older = lax.dynamic_slice_in_dim(current, row_start, half_rows, 2)
        updated = damping * older + (1.0 - damping) * jnp.stack(
            [numer_real / denom, numer_imag / denom], axis=1
        )
        if step_index + 1 < ITERS:
            current = lax.all_gather(updated, "beam", axis=2, tiled=True)
    return (visibilities, updated, beam_power)


LANES = 128
SUBLANES = 8
NEXT_ROWS = 4
MIB = 2**20
UPDATE_LIMIT = 14 * MIB
NT = (((1,), (1,)), ((), ()))
TN = (((0,), (0,)), ((), ()))
NN = (((1,), (0,)), ((), ()))


def mxu(left, right, dims):
    return lax.dot_general(left, right, dims, preferred_element_type=jnp.float32)


def transform_rows(kept_count, transform_count, owners, shares):
    by_owner = np.arange(kept_count).reshape(owners, -1)
    ends = np.cumsum(shares)
    kept = np.concatenate(
        [by_owner[:, end - share : end].reshape(-1) for share, end in zip(shares, ends)]
    )
    phases = (kept[:, None] * np.arange(transform_count)[None, :] % transform_count) * (
        2.0 * math.pi / transform_count
    )
    table = np.concatenate([np.cos(phases), np.sin(phases)], axis=1) / math.sqrt(transform_count)
    return jnp.asarray(table.astype(jnp.bfloat16))


def transformed(owners, frames, table, windowed_ref, turned_ref, copies=()):
    rows = table.shape[0]
    width = turned_ref.shape[1]
    share = rows // owners
    total = windowed_ref.shape[0] // width
    step = 4
    for frame in range(0, total, step):
        some = min(step, total - frame)
        for copy in copies[frame : frame + some]:
            copy.wait()
        block = mxu(table, windowed_ref[frame * width : (frame + some) * width, :], NT)
        for i in range(some):
            at = frame + i
            part = block[:, i * width : (i + 1) * width]
            if at < frames:
                turned_ref[pl.ds(at, rows, stride=frames), :] = part
            else:
                first = rows * frames + (at - frames) * share
                for owner in range(owners):
                    turned_ref[pl.ds(first + owner * (total - frames) * share, share), :] = part[
                        owner * share : (owner + 1) * share
                    ]


def filter_kernel(
    owners,
    x_hbm,
    taps_hbm,
    table_hbm,
    windowed_hbm,
    out_ref,
    x_ref,
    table_ref,
    taps_ref,
    frames_ref,
    windowed_ref,
    turned_ref,
    sems,
    keep_sems,
):
    inputs, _, frames, points = x_ref.shape
    taps = taps_ref.shape[0]
    width = 2 * inputs
    pieces = sems.shape[0] - 2
    group = inputs // pieces
    table_copy = pltpu.make_async_copy(
        table_hbm.at[pl.ds(0, table_ref.shape[0])], table_ref, sems.at[pieces]
    )
    copies = [
        pltpu.make_async_copy(
            x_hbm.at[pl.ds(i * group, group)], x_ref.at[pl.ds(i * group, group)], sems.at[i]
        )
        for i in range(pieces)
    ]
    taps_copy = pltpu.make_async_copy(taps_hbm, taps_ref, sems.at[pieces + 1])
    taps_copy.start()
    for copy in copies:
        copy.start()
    taps_copy.wait()

    def spread(i, carry):
        for part in range(2):
            block = x_ref[i, part].astype(jnp.float32)
            for piece in range(points // LANES):
                here = pl.ds(pl.multiple_of(i * frames, frames), frames)
                frames_ref[part, piece, here, :] = block[:, piece * LANES : (piece + 1) * LANES]
        return carry

    for i, copy in enumerate(copies):
        copy.wait()
        lax.fori_loop(i * group, (i + 1) * group, spread, 0, unroll=8)

    table_copy.start()

    def keep(piece, half):
        here = pl.ds(pl.multiple_of(half * points + piece * LANES, LANES), LANES)
        return pltpu.make_async_copy(
            windowed_ref.at[:, here], windowed_hbm.at[:, here], keep_sems.at[half, piece]
        )

    def window(piece, carry):
        lanes = pl.ds(pl.multiple_of(piece * LANES, LANES), LANES)
        upper = pl.ds(pl.multiple_of(points + piece * LANES, LANES), LANES)
        weights = taps_ref[:, lanes]
        weights = [
            jnp.broadcast_to(weights[tap : tap + 1], (2 * SUBLANES, LANES)) for tap in range(taps)
        ]
        for first in range(0, inputs, 2 * SUBLANES):
            for part in range(2):
                values = [
                    frames_ref[
                        part, piece, pl.ds(first * frames + frame, 2 * SUBLANES, stride=frames), :
                    ]
                    for frame in range(frames)
                ]
                for frame in range(frames + taps - 1):
                    total = None
                    for tap in range(taps):
                        source = frame + tap - (taps - 1)
                        if 0 <= source < frames:
                            term = values[source] * weights[tap]
                            total = term if total is None else total + term
                    base = frame * width + first
                    rows = slice(base, base + 2 * SUBLANES)
                    swapped = slice(base + inputs, base + inputs + 2 * SUBLANES)
                    total = total.astype(jnp.bfloat16)
                    if part == 0:
                        windowed_ref[rows, lanes] = total
                        windowed_ref[swapped, upper] = -total
                    else:
                        windowed_ref[rows, upper] = total
                        windowed_ref[swapped, lanes] = total
        keep(piece, 0).start()
        keep(piece, 1).start()
        return carry

    lax.fori_loop(0, points // LANES, window, 0, unroll=2)
    table_copy.wait()
    transformed(owners, frames, table_ref[...], windowed_ref, turned_ref)
    share = table_ref.shape[0] // owners
    main = share * frames
    extra = share * (taps - 1)
    for owner in range(owners):
        out_ref[owner, :main, :] = turned_ref[owner * main : (owner + 1) * main, :].astype(
            jnp.bfloat16
        )
        first = owners * main + owner * extra
        out_ref[owner, main : main + extra, :] = turned_ref[first : first + extra, :].astype(
            jnp.bfloat16
        )
    for piece in range(points // LANES):
        keep(piece, 0).wait()
        keep(piece, 1).wait()


def rows_copies(source, target, sems, first=0):
    size = target.shape[0] // sems.shape[0]
    return [
        pltpu.make_async_copy(
            source.at[pl.ds(first + i * size, size)], target.at[pl.ds(i * size, size)], sems.at[i]
        )
        for i in range(sems.shape[0])
    ]


def spill_kernel(first, start, windowed_hbm, table_hbm, out_ref, windowed_ref, table_ref, sems):
    copies = rows_copies(windowed_hbm, windowed_ref, sems.at[pl.ds(0, 1)], first)
    copies += rows_copies(table_hbm, table_ref, sems.at[pl.ds(1, 1)], start)
    for copy in copies:
        copy.start()
    for copy in copies:
        copy.wait()
    frames, _, width = out_ref.shape
    block = mxu(table_ref[...], windowed_ref[...], NT)
    for frame in range(frames):
        out_ref[frame] = block[:, frame * width : (frame + 1) * width].astype(jnp.bfloat16)


def filter_more_kernel(
    owners, start, windowed_hbm, table_hbm, turned_ref, windowed_ref, table_ref, sems
):
    frames = sems.shape[0] - 1
    copies = rows_copies(windowed_hbm, windowed_ref, sems.at[pl.ds(0, frames)])
    table_copies = rows_copies(table_hbm, table_ref, sems.at[pl.ds(frames, 1)], start)
    for copy in table_copies + copies:
        copy.start()
    for copy in table_copies:
        copy.wait()
    transformed(owners, frames, table_ref[...], windowed_ref, turned_ref, copies)


def added_kernel(turned_ref, added_ref, out_ref, total_ref):
    owners, main, _ = out_ref.shape
    nexts, rows, _ = added_ref.shape
    frames = turned_ref.shape[0] // rows
    total_ref[...] = turned_ref[...]
    for frame in range(nexts):
        here = pl.ds(frame, rows, stride=frames)
        total_ref[here, :] = turned_ref[here, :] + added_ref[frame].astype(jnp.float32)
    for owner in range(owners):
        out_ref[owner] = total_ref[owner * main : (owner + 1) * main, :].astype(jnp.bfloat16)


def filtered(samples, window_taps, kept_count, owners, shares):
    inputs, _, points, frames = samples.shape
    taps = window_taps.shape[0]
    width = 2 * inputs
    table = transform_rows(kept_count, points, owners, shares)
    by_frame = jnp.transpose(samples, (0, 1, 3, 2))
    by_frame = pltpu.with_memory_space_constraint(by_frame, pltpu.HBM)
    table = pltpu.with_memory_space_constraint(table, pltpu.HBM)
    window_taps = pltpu.with_memory_space_constraint(window_taps, pltpu.HBM)
    pieces = points // LANES
    anywhere = pl.BlockSpec(memory_space=pl.ANY)
    vmem = pl.BlockSpec(memory_space=pltpu.VMEM)
    windowed_shape = ((frames + taps - 1) * width, 2 * points)
    rows = owners * shares[0]
    windowed, first = pl.pallas_call(
        functools.partial(filter_kernel, owners),
        out_shape=[
            pltpu.HBM(windowed_shape, jnp.bfloat16),
            jax.ShapeDtypeStruct((owners, shares[0] * (frames + taps - 1), width), jnp.bfloat16),
        ],
        in_specs=[anywhere, anywhere, anywhere],
        out_specs=[anywhere, vmem],
        scratch_shapes=[
            pltpu.VMEM(by_frame.shape, jnp.bfloat16),
            pltpu.VMEM((rows, 2 * points), jnp.bfloat16),
            pltpu.VMEM(window_taps.shape, jnp.float32),
            pltpu.VMEM((2, pieces, inputs * frames, LANES), jnp.float32),
            pltpu.VMEM(windowed_shape, jnp.bfloat16),
            pltpu.VMEM((rows * (frames + taps - 1), width), jnp.float32),
            pltpu.SemaphoreType.DMA((6,)),
            pltpu.SemaphoreType.DMA((2, pieces)),
        ],
        compiler_params=pltpu.CompilerParams(vmem_limit_bytes=32 * MIB),
        name="filter",
    )(by_frame, window_taps, table)
    windowed = pltpu.with_memory_space_constraint(windowed, pltpu.HBM)

    def more(chunk, start):
        rows = owners * shares[chunk]
        spill = pl.pallas_call(
            functools.partial(spill_kernel, frames * width, start),
            out_shape=jax.ShapeDtypeStruct((taps - 1, rows, width), jnp.bfloat16),
            in_specs=[anywhere, anywhere],
            out_specs=vmem,
            scratch_shapes=[
                pltpu.VMEM(((taps - 1) * width, 2 * points), jnp.bfloat16),
                pltpu.VMEM((rows, 2 * points), jnp.bfloat16),
                pltpu.SemaphoreType.DMA((2,)),
            ],
            compiler_params=pltpu.CompilerParams(vmem_limit_bytes=24 * MIB),
            name="spill",
        )(windowed, table)
        added = from_behind(spill, "tm", 1)
        turned = pl.pallas_call(
            functools.partial(filter_more_kernel, owners, start),
            out_shape=jax.ShapeDtypeStruct((rows * frames, width), jnp.float32),
            in_specs=[anywhere, anywhere],
            out_specs=vmem,
            scratch_shapes=[
                pltpu.VMEM((frames * width, 2 * points), jnp.bfloat16),
                pltpu.VMEM((rows, 2 * points), jnp.bfloat16),
                pltpu.SemaphoreType.DMA((frames + 1,)),
            ],
            compiler_params=pltpu.CompilerParams(vmem_limit_bytes=24 * MIB),
            name="filter_more",
        )(windowed, table)
        return pl.pallas_call(
            added_kernel,
            out_shape=jax.ShapeDtypeStruct((owners, shares[chunk] * frames, width), jnp.bfloat16),
            in_specs=[vmem, vmem],
            out_specs=vmem,
            scratch_shapes=[pltpu.VMEM((rows * frames, width), jnp.float32)],
            compiler_params=pltpu.CompilerParams(vmem_limit_bytes=24 * MIB),
            name="added",
        )(turned, added)

    sent = [first]
    start = rows
    for chunk in range(1, len(shares)):
        sent.append(more(chunk, start))
        start += owners * shares[chunk]
    return sent


def gain_terms(real, imag, gains, flags):
    weights = flags.astype(jnp.float32)
    gain_real = gains[0:1] * weights
    gain_imag = gains[1:2] * weights
    turned_real = real * gain_real + imag * gain_imag
    turned_imag = imag * gain_real - real * gain_imag
    power = weights * (gains[0:1] * gains[0:1] + gains[1:2] * gains[1:2])
    return turned_real, turned_imag, power


def denominators(power, model_real, model_imag):
    model_power = model_real * model_real + model_imag * model_imag
    terms = model_power * jnp.broadcast_to(power.astype(jnp.bfloat16), model_power.shape)
    folded = terms[:, :LANES]
    for first in range(LANES, terms.shape[1], LANES):
        folded = folded + terms[:, first : first + LANES]
    return mxu(jnp.ones((SUBLANES, LANES), jnp.bfloat16), folded, NT)[0:1] + epsilon


def put_turned(turned_ref, at, real, imag, gains, flags):
    turned_real, turned_imag, power = gain_terms(real, imag, gains, flags)
    frames = real.shape[0]
    turned_real = turned_real.astype(jnp.bfloat16)
    turned_imag = turned_imag.astype(jnp.bfloat16)
    turned_ref[at, 0, :frames] = turned_real
    turned_ref[at, 0, frames:] = turned_imag
    turned_ref[at, 1, :frames] = -turned_imag
    turned_ref[at, 1, frames:] = turned_real
    return power


def modelled(turned_ref, at, model_real, model_imag):
    return mxu(turned_ref[at, 0], model_real, NT) + mxu(turned_ref[at, 1], model_imag, NT)


def updated_gains(own, products, denom, older):
    own_real, own_imag = own
    frames = own_real.shape[0]
    real = products[:frames]
    imag = products[frames:]
    numer_real = jnp.sum(own_real * real + own_imag * imag, axis=0, keepdims=True)
    numer_imag = jnp.sum(own_imag * real - own_real * imag, axis=0, keepdims=True)
    numer = jnp.concatenate([numer_real, numer_imag], axis=0) / frames
    return damping * older + (1.0 - damping) * (numer / denom)


def own_half(values, core):
    half = values.shape[1] // 2
    return jnp.where(core == 0, values[:, :half], values[:, half:])


def model_kernel(
    base, step, reach, own_hbm, model_hbm, centre_ref, steering_ref, model_ref, table_ref, sem
):
    del own_hbm
    count = min(MODEL_BLOCK, model_ref.shape[0])
    copy = pltpu.make_async_copy(
        model_hbm.at[pl.ds(base, count)], model_ref.at[pl.ds(0, count)], sem
    )
    copy.start()
    steering_tables(centre_ref[0], steering_ref, table_ref, step, reach)
    copy.wait()


def first_kernel(
    times, base, core_ref, own_ref, other_ref, model_hbm, gains_ref, flags_ref, here_ref, *refs
):
    del here_ref
    spectra_ref, updated_ref, model_ref, next_ref, turned_ref, products_ref, power_ref, denom_ref, sems = refs
    core = core_ref[0]
    share = spectra_ref.shape[0]
    sources, rows, width = own_ref.shape
    frames = spectra_ref.shape[1] // 2 // times
    nexts = rows // share - frames
    columns = sources // times
    lane = lax.broadcasted_iota(jnp.int32, (frames, width), 1)
    row = lax.broadcasted_iota(jnp.int32, (frames, width), 0)
    low = lane < width // 2
    count = BLOCK

    def copy(i):
        here = pl.ds(i * VIS_BLOCK, VIS_BLOCK)
        there = pl.ds(base + i * VIS_BLOCK, VIS_BLOCK)
        return pltpu.make_async_copy(model_hbm.at[there], model_ref.at[here], sems.at[i])

    groups = share // VIS_BLOCK
    there = min(MODEL_BLOCK, share) // VIS_BLOCK
    ahead = 3
    for i in range(there, min(there + ahead, groups)):
        copy(i).start()
    if nexts:
        for source in range(sources):
            for side, ref in enumerate((own_ref, other_ref)):
                next_ref[side, source] = ref[source, share * frames :, :].astype(jnp.float32)

    def assemble(i):
        main_rows = pl.ds(pl.multiple_of(i * (count * frames), count * frames), count * frames)

        def loaded(side, column, time):
            ref = (own_ref, other_ref)[side]
            source = column * times + time
            block = ref[source, main_rows, :].astype(jnp.float32)
            extra = []
            if time > 0:
                extra = [
                    next_ref[
                        side, source - 1, pl.ds(pl.multiple_of(share * k + i * count, count), count), :
                    ]
                    for k in range(nexts)
                ]
            return block, extra

        def one(value, c):
            block, extra = value
            block = block[c * frames : (c + 1) * frames]
            for k, more in enumerate(extra):
                block = block + jnp.where(row == k, more[c : c + 1], 0.0)
            return block

        blocks = {
            (column, time): (loaded(0, column, time), loaded(1, column, time))
            for column in range(columns)
            for time in range(times)
        }
        for c in range(count):
            real_rows = []
            imag_rows = []
            for time in range(times):
                reals = []
                imags = []
                for column in range(columns):
                    own, other = blocks[column, time]
                    own = one(own, c)
                    other = one(other, c)
                    first = jnp.where(core == 0, own, other)
                    second = jnp.where(core == 0, other, own)
                    reals.append(jnp.where(low, first, pltpu.roll(second, width // 2, 1)))
                    imags.append(jnp.where(low, pltpu.roll(first, width // 2, 1), second))
                real_rows.append(jnp.concatenate(reals, axis=1))
                imag_rows.append(jnp.concatenate(imags, axis=1))
            spectra = jnp.concatenate(real_rows + imag_rows, axis=0)
            spectra_ref[i * count + c] = spectra.astype(jnp.bfloat16)

    def update(i):
        for part in range(count // VIS_BLOCK):
            group = i * (count // VIS_BLOCK) + part

            @pl.when(group >= there)
            def _():
                copy(group).wait()

                @pl.when(group + ahead < groups)
                def _():
                    copy(group + ahead).start()

        channels = [i * count + c for c in range(count)]

        def parts(here):
            values = spectra_ref[here].astype(jnp.float32)
            half = values.shape[0] // 2
            return values[:half], values[half:]

        for c, here in enumerate(channels):
            real, imag = parts(here)
            flags = flags_ref[pl.ds(base + here, 1), :]
            power_ref[c] = put_turned(turned_ref, c, real, imag, gains_ref[base + here], flags)
        for c, here in enumerate(channels):
            model_real = model_ref[here, 0]
            model_imag = model_ref[here, 1]
            products_ref[c] = modelled(turned_ref, c, model_real, model_imag)
            denom_ref[c] = denominators(power_ref[c], model_real, model_imag)
        for c, here in enumerate(channels):
            real, imag = parts(here)
            updated_ref[here] = updated_gains(
                (own_half(real, core), own_half(imag, core)),
                products_ref[c],
                denom_ref[c],
                own_half(gains_ref[base + here], core),
            )

    def step(i, carry):
        update(i)
        assemble(i + 1)
        return carry

    last = share // count - 1
    assemble(0)
    lax.fori_loop(0, last, step, 0)
    update(last)


def second_kernel(
    base, core_ref, spectra_ref, model_ref, own_ref, other_ref, flags_ref, *refs
):
    visibilities_hbm, updated_hbm, ready_ref, updated_ref = refs[-10:-6]
    turned_ref, products_ref, power_ref, denom_ref, sems, sem = refs[-6:]
    core = core_ref[0]
    share = spectra_ref.shape[0]
    slots, count = ready_ref.shape[:2]
    pieces = sems.shape[1]
    size = count // pieces
    steps = share // count

    def copy(i, slot, piece):
        return pltpu.make_async_copy(
            ready_ref.at[slot, pl.ds(piece * size, size)],
            visibilities_hbm.at[pl.ds(base + i * count + piece * size, size)],
            sems.at[slot, piece],
        )

    def step(i, carry):
        slot = lax.rem(i, slots)

        @pl.when(i >= slots)
        def _():
            for piece in range(pieces):
                copy(i - slots, slot, piece).wait()

        channels = [i * count + c for c in range(count)]

        def parts(here):
            values = spectra_ref[here].astype(jnp.float32)
            half = values.shape[0] // 2
            return values[:half], values[half:]

        for c, here in enumerate(channels):
            real, imag = parts(here)
            own = own_ref[here]
            other = other_ref[here]
            first = jnp.where(core == 0, own, other)
            second = jnp.where(core == 0, other, own)
            gains = jnp.concatenate([first, second], axis=1)
            flags = flags_ref[pl.ds(base + here, 1), :]
            power_ref[c] = put_turned(turned_ref, c, real, imag, gains, flags)
        for c, here in enumerate(channels):
            real, imag = parts(here)
            frames = real.shape[0]
            own_real = own_half(real, core)
            own_imag = own_half(imag, core)
            paired = jnp.concatenate([own_real, own_imag], axis=0) / frames
            rotated = jnp.concatenate([own_imag, -own_real], axis=0) / frames
            spectra = spectra_ref[here]
            ready_ref[slot, c, 0] = mxu(paired.astype(jnp.bfloat16), spectra, TN).astype(jnp.bfloat16)
            ready_ref[slot, c, 1] = mxu(rotated.astype(jnp.bfloat16), spectra, TN).astype(jnp.bfloat16)
            if c % size == size - 1:
                copy(i, slot, c // size).start()
            model_real = model_ref[here, 0]
            model_imag = model_ref[here, 1]
            products_ref[c] = modelled(turned_ref, c, model_real, model_imag)
            denom_ref[c] = denominators(power_ref[c], model_real, model_imag)
        for c, here in enumerate(channels):
            real, imag = parts(here)
            updated_ref[here] = updated_gains(
                (own_half(real, core), own_half(imag, core)),
                products_ref[c],
                denom_ref[c],
                own_ref[here],
            )
        return carry

    lax.fori_loop(0, steps, step, 0)
    last = pltpu.make_async_copy(updated_ref, updated_hbm.at[pl.ds(base, share)], sem)
    last.start()
    for i in range(max(0, steps - slots), steps):
        for piece in range(pieces):
            copy(i, i % slots, piece).wait()
    last.wait()


def series_length(reach):
    terms = 1
    while 2.0 * (0.5 * reach) ** terms / math.factorial(terms) >= 2.0**-22:
        terms += 1
    return terms


def bessel(order, x, reach):
    count = 1
    while (0.5 * reach) ** (2 * count) / math.factorial(count) ** 2 >= 2.0**-26:
        count += 1
    square = x * x * -0.25
    total = jnp.full_like(x, 1.0 / (math.factorial(count - 1) * math.factorial(count - 1 + order)))
    for m in reversed(range(count - 1)):
        total = total * square + 1.0 / (math.factorial(m) * math.factorial(m + order))
    for _ in range(order):
        total = total * (0.5 * x)
    return total


def turns(count, period):
    quarter = period // 4
    quadrant = lax.shift_right_logical(count + period // 8, quarter.bit_length() - 1)
    angle = (count - quadrant * quarter).astype(jnp.float32) * (2.0 * math.pi / period)
    square = angle * angle
    sine_part = jnp.full_like(angle, 1.0 / math.factorial(9))
    cosine = jnp.full_like(angle, 1.0 / math.factorial(8))
    for power in (7, 5, 3, 1):
        sign = -1.0 if power % 4 == 3 else 1.0
        sine_part = sine_part * square + sign / math.factorial(power)
        cosine = cosine * square + sign / math.factorial(power - 1)
    sine_part = sine_part * angle
    odd = (quadrant & 1) == 1
    real = jnp.where(odd, sine_part, cosine)
    imag = jnp.where(odd, cosine, sine_part)
    real = jnp.where(((quadrant + 1) & 2) == 2, -real, real)
    imag = jnp.where((quadrant & 2) == 2, -imag, imag)
    return real, imag


def steering_tables(centre, steering_ref, table_ref, step, reach):
    inputs = table_ref.shape[1] // 2
    beams = table_ref.shape[2] // 2
    quarter = inputs // 4
    for column in range(4):
        for first in range(0, quarter, 4 * SUBLANES):
            shape = (4 * SUBLANES, beams)
            within = lax.broadcasted_iota(jnp.int32, shape, 0) + first
            phase_index = (steering_ref[0:1, :] * (column * 64) + steering_ref[1:2, :] * within) & 255
            cosine, sine_part = turns(phase_index * centre, round(4.0 * math.pi / step))
            offset = (phase_index - 128).astype(jnp.float32) * (reach * step)
            at = column * quarter + first
            rows = slice(at, at + shape[0])
            lower = slice(inputs + at, inputs + at + shape[0])
            for term in range(table_ref.shape[0]):
                real, imag = (
                    (cosine, sine_part),
                    (-sine_part, cosine),
                    (-cosine, -sine_part),
                    (sine_part, -cosine),
                )[term % 4]
                factor = bessel(term, offset, 128 * reach * step) * (2.0 if term else 1.0)
                real = factor * real
                imag = factor * imag
                real = real.astype(jnp.bfloat16)
                imag = imag.astype(jnp.bfloat16)
                table_ref[term, rows, :beams] = real
                table_ref[term, rows, beams:] = imag
                table_ref[term, lower, :beams] = -imag
                table_ref[term, lower, beams:] = real


def beams_kernel(base, spectra_ref, gains_ref, flags_ref, table_ref, *refs):
    power_hbm, power_ref, left_ref, sem = refs[-4:]
    count, doubled, inputs = spectra_ref.shape
    frames = doubled // 2
    scale = 1.0 / math.sqrt(inputs)
    middle = 0.5 * (count - 1)
    terms = table_ref.shape[0]
    for c in range(count):
        values = spectra_ref[c].astype(jnp.float32)
        real = values[:frames]
        imag = values[frames:]
        at = base + c
        weights = flags_ref[at : at + 1].astype(jnp.float32) * scale
        gain_real = gains_ref[at, 0:1] * weights
        gain_imag = gains_ref[at, 1:2] * weights
        lit_real = real * gain_real - imag * gain_imag
        lit_imag = real * gain_imag + imag * gain_real
        rows = slice(c * frames, (c + 1) * frames)
        for term in range(terms):
            power = math.cos(term * math.acos((c - middle) / max(middle, 0.5)))
            left_ref[term, rows, :inputs] = (lit_real * power).astype(jnp.bfloat16)
            left_ref[term, rows, inputs:] = (lit_imag * power).astype(jnp.bfloat16)
    total = mxu(left_ref[0], table_ref[0], NN)
    for term in range(1, terms):
        total = total + mxu(left_ref[term], table_ref[term], NN)
    beams = total.shape[1] // 2
    real = total[:, :beams]
    imag = total[:, beams:]
    power_ref[...] = (real * real + imag * imag).reshape(count, frames, beams)
    copy = pltpu.make_async_copy(power_ref, power_hbm.at[pl.ds(base, count)], sem)
    copy.start()
    copy.wait()


def formed_beams(chunk, gains, flags, earlier):
    base, table, spectra = chunk
    share, doubled, input_count = spectra.shape
    frame_count = doubled // 2
    beams = table.shape[2] // 2
    earlier = [] if earlier is None else [earlier]
    vmem = pl.BlockSpec(memory_space=pltpu.VMEM)
    return pl.pallas_call(
        functools.partial(beams_kernel, base),
        in_specs=[vmem] * 4 + [pl.BlockSpec(memory_space=pl.ANY)] * len(earlier),
        out_specs=pl.BlockSpec(memory_space=pl.ANY),
        out_shape=jax.ShapeDtypeStruct((gains.shape[0], frame_count, beams), jnp.float32),
        input_output_aliases={4: 0} if earlier else {},
        scratch_shapes=[
            pltpu.VMEM((share, frame_count, beams), jnp.float32),
            pltpu.VMEM((table.shape[0], share * frame_count, 2 * input_count), jnp.bfloat16),
            pltpu.SemaphoreType.DMA,
        ],
        compiler_params=pltpu.CompilerParams(vmem_limit_bytes=UPDATE_LIMIT),
        name="beams",
    )(spectra, gains, flags, table, *earlier)


def chunk_shards(samples, window_taps, sky_model, prior_gains, beam_steering, input_flags):
    frames = samples.shape[3]
    chan_local, _, half_rows, input_count = sky_model.shape
    times = lax.axis_size("tm")
    owners = lax.axis_size("chan") * times
    core = lax.axis_index("beam").astype(jnp.int32).reshape(1)
    first_channel = (lax.axis_index("chan") * times + lax.axis_index("tm")) * chan_local
    kept_count = chan_local * owners
    frame_count = frames * times
    beams = beam_steering.shape[1]
    shares = chunk_shares(chan_local)
    bases = [sum(shares[:chunk]) for chunk in range(len(shares))]
    centres = [
        (2 * (kept_count + first_channel + base) + share - 1).astype(jnp.int32).reshape(1)
        for base, share in zip(bases, shares)
    ]
    sent = filtered(samples, window_taps, kept_count, owners, shares)
    swap = [(0, 1), (1, 0)]
    smem = pl.BlockSpec(memory_space=pltpu.SMEM)
    vmem = pl.BlockSpec(memory_space=pltpu.VMEM)
    anywhere = pl.BlockSpec(memory_space=pl.ANY)
    step = 2.0 * math.pi / (512 * kept_count)

    sent[0], gains, flags, steering, core, centres = lax.optimization_barrier(
        (sent[0], prior_gains, input_flags, beam_steering, core, centres)
    )
    visibilities = None
    beam_power = None
    gains_new = None
    before = None
    for chunk, (base, share) in enumerate(zip(bases, shares)):
        own = lax.all_to_all(sent[chunk], ("chan", "tm"), 0, 0, tiled=True)
        if before is not None:
            beam_power = formed_beams(before, gains, flags, beam_power)
            own, gains_new, beam_power = lax.optimization_barrier((own, gains_new, beam_power))
        other = lax.ppermute(own, "beam", swap)
        model_shape = (share, *sky_model.shape[1:])
        reach = max(0.5 * (share - 1), 0.5)
        table_shape = (series_length(128 * reach * step), 2 * input_count, 2 * beams)
        model, table = pl.pallas_call(
            functools.partial(model_kernel, base, step, reach),
            in_specs=[anywhere, anywhere, smem, vmem],
            out_specs=[vmem, vmem],
            out_shape=[
                pltpu.VMEM(model_shape, sky_model.dtype),
                jax.ShapeDtypeStruct(table_shape, jnp.bfloat16),
            ],
            scratch_shapes=[pltpu.SemaphoreType.DMA],
            compiler_params=pltpu.CompilerParams(vmem_limit_bytes=UPDATE_LIMIT),
            name="model",
        )(own, sky_model, centres[chunk], steering)
        model = pltpu.with_memory_space_constraint(model, pltpu.VMEM)
        half_shape = jax.ShapeDtypeStruct((share, 2, half_rows), jnp.float32)
        spectra, gains_own, model = pl.pallas_call(
            functools.partial(first_kernel, times, base),
            in_specs=[smem, vmem, vmem, anywhere, vmem, vmem, vmem],
            out_specs=[vmem, vmem, vmem],
            out_shape=[
                jax.ShapeDtypeStruct((share, 2 * frame_count, input_count), jnp.bfloat16),
                half_shape,
                pltpu.VMEM(model_shape, sky_model.dtype),
            ],
            input_output_aliases={6: 2},
            scratch_shapes=[
                pltpu.VMEM((2, owners, max(own.shape[1] - share * frames, SUBLANES), own.shape[2]), jnp.float32),
                pltpu.VMEM((BLOCK, 2, 2 * frame_count, input_count), jnp.bfloat16),
                pltpu.VMEM((BLOCK, 2 * frame_count, half_rows), jnp.float32),
                pltpu.VMEM((BLOCK, 1, input_count), jnp.float32),
                pltpu.VMEM((BLOCK, 1, half_rows), jnp.float32),
                pltpu.SemaphoreType.DMA((share // VIS_BLOCK,)),
            ],
            compiler_params=pltpu.CompilerParams(vmem_limit_bytes=UPDATE_LIMIT),
            name="first_update",
        )(core, own, other, sky_model, gains, flags, model)
        model = pltpu.with_memory_space_constraint(model, pltpu.VMEM)
        gains_other = lax.ppermute(gains_own, "beam", swap)
        before = (base, table, spectra)
        if chunk == len(shares) - 1:
            beam_power = formed_beams(before, gains, flags, beam_power)
        earlier = [] if visibilities is None else [visibilities, gains_new]
        visibilities, gains_new = pl.pallas_call(
            functools.partial(second_kernel, base),
            in_specs=[smem] + [vmem] * 5 + [anywhere] * len(earlier),
            out_specs=[anywhere, anywhere],
            out_shape=[
                jax.ShapeDtypeStruct(sky_model.shape, jnp.bfloat16),
                jax.ShapeDtypeStruct((chan_local, 2, half_rows), jnp.float32),
            ],
            scratch_shapes=[
                pltpu.VMEM((2, BLOCK, 2, half_rows, input_count), jnp.bfloat16),
                pltpu.VMEM((share, 2, half_rows), jnp.float32),
                pltpu.VMEM((BLOCK, 2, 2 * frame_count, input_count), jnp.bfloat16),
                pltpu.VMEM((BLOCK, 2 * frame_count, half_rows), jnp.float32),
                pltpu.VMEM((BLOCK, 1, input_count), jnp.float32),
                pltpu.VMEM((BLOCK, 1, half_rows), jnp.float32),
                pltpu.SemaphoreType.DMA((2, 4)),
                pltpu.SemaphoreType.DMA,
            ],
            input_output_aliases={6: 0, 7: 1} if earlier else {},
            compiler_params=pltpu.CompilerParams(vmem_limit_bytes=UPDATE_LIMIT),
            name="second_update",
        )(core, spectra, model, gains_own, gains_other, flags, *earlier)
    return (
        visibilities,
        gains_new,
        jnp.transpose(beam_power, (0, 2, 1)),
    )


BLOCK = 8
VIS_BLOCK = 4
MODEL_BLOCK = 8


def chunk_shares(chan_local):
    blocks = chan_local // BLOCK
    first = blocks * 3 // 8
    return [first * BLOCK, (blocks - first) * BLOCK]


def shards(samples, window_taps, sky_model, prior_gains, beam_steering, input_flags):
    inputs, _, points, frames = samples.shape
    chan_local, _, half_rows, input_count = sky_model.shape
    frame_count = frames * lax.axis_size("tm")
    owners = lax.axis_size("chan") * lax.axis_size("tm")
    fits = (
        ITERS == 2
        and 2 * inputs == LANES
        and points % LANES == 0
        and frames == SUBLANES
        and window_taps.shape[0] == NEXT_ROWS
        and lax.axis_size("beam") == 2
        and chan_local % (8 * BLOCK) == 0
        and half_rows % LANES == 0
        and frame_count & (frame_count - 1) == 0
        and chan_local * owners & (chan_local * owners - 1) == 0
        and half_rows % (4 * LANES // 2) == 0
        and beam_steering.shape[1] % LANES == 0
    )
    form = chunk_shards if fits else general_shards
    return form(samples, window_taps, sky_model, prior_gains, beam_steering, input_flags)


def solution(mesh):
    return jax.shard_map(
        shards,
        mesh=mesh,
        in_specs=(
            P(("group", "chan", "beam"), None, None, "tm"),
            P(),
            P(("group", "chan", "tm"), None, "beam", None),
            P(("group", "chan", "tm"), None, None),
            P(None, ("group", "beam")),
            P(("group", "chan", "tm"), None),
        ),
        out_specs=(
            P(("group", "chan", "tm"), None, "beam", None),
            P(("group", "chan", "tm"), None, "beam"),
            P(("group", "chan", "tm"), "beam", None),
        ),
        check_vma=False,
    )
```

```python
import functools
import math

import jax
import jax.numpy as jnp
import numpy as np
from jax import lax
from jax.experimental import pallas as pl
from jax.experimental.pallas import tpu as pltpu
from jax.sharding import PartitionSpec as P

NCH = 512
ITERS = 2


damping = 0.5
epsilon = 1e-06


def from_behind(block, axis, distance):
    devices = range(lax.axis_size(axis))
    route = [(i - distance, i) for i in devices if i - distance in devices]
    return lax.ppermute(block, axis, route)


def filter_bank(extended, window_taps, kept_count, frames):
    transform_count = window_taps.shape[1]
    tap_count = window_taps.shape[0]
    local_inputs = extended.shape[0]
    kept = jnp.arange(kept_count, dtype=jnp.int32)
    indices = jnp.arange(transform_count, dtype=jnp.int32)
    phases = (kept[:, None] * indices[None, :] % transform_count).astype(jnp.float32) * (
        2.0 * math.pi / transform_count
    )
    cosine = jnp.cos(phases)
    sine_part = jnp.sin(phases)
    real_in = extended[:, :transform_count]
    imag_in = extended[:, transform_count:]
    real_sum = jnp.zeros((local_inputs, kept_count, frames), jnp.float32)
    imag_sum = jnp.zeros((local_inputs, kept_count, frames), jnp.float32)
    for tap_index in range(tap_count):
        tap_row = window_taps[tap_index][None, :]
        cos_block = (cosine * tap_row / math.sqrt(transform_count)).astype(jnp.bfloat16)
        sin_block = (sine_part * tap_row / math.sqrt(transform_count)).astype(jnp.bfloat16)
        part_real = real_in[:, :, tap_index : tap_index + frames]
        part_imag = imag_in[:, :, tap_index : tap_index + frames]
        real_sum = (
            real_sum
            + jnp.einsum("kn,inf->ikf", cos_block, part_real, preferred_element_type=jnp.float32)
            + jnp.einsum("kn,inf->ikf", sin_block, part_imag, preferred_element_type=jnp.float32)
        )
        imag_sum = (
            imag_sum
            + jnp.einsum("kn,inf->ikf", cos_block, part_imag, preferred_element_type=jnp.float32)
            - jnp.einsum("kn,inf->ikf", sin_block, part_real, preferred_element_type=jnp.float32)
        )
    return jnp.stack([real_sum, imag_sum], axis=2).astype(jnp.bfloat16)


def steering_angles(beam_steering, channels, input_count, chan_total):
    positions = jnp.arange(input_count, dtype=jnp.int32)
    column = positions // (input_count // 4)
    within = positions % (input_count // 4)
    phase_index = (
        beam_steering[0][:, None] * column[None, :] * 64
        + beam_steering[1][:, None] * within[None, :]
    ) % 256
    scaled = phase_index[None] * (chan_total + channels)[:, None, None]
    return scaled.astype(jnp.float32) * (2.0 * math.pi / (512 * chan_total))


def cross_rows(owned_rows, all_rows):
    paired = owned_rows.reshape(owned_rows.shape[0], owned_rows.shape[1], -1)
    rotated = jnp.stack([owned_rows[:, :, 1], -owned_rows[:, :, 0]], axis=2).reshape(paired.shape)
    left = jnp.stack([paired, rotated], axis=1)
    columns = all_rows.reshape(all_rows.shape[0], all_rows.shape[1], -1)
    return jnp.einsum("isck,jck->csij", left, columns, preferred_element_type=jnp.float32)


def form_beams(whole_set, gains_part, weights, beam_steering, channels, chan_total):
    input_count = whole_set.shape[0]
    angles = steering_angles(beam_steering, channels, input_count, chan_total)
    cosine = jnp.cos(angles)
    sine_part = jnp.sin(angles)
    scale_factor = 1.0 / math.sqrt(input_count)
    gain_real = (gains_part[:, 0] * weights)[:, None, :]
    gain_imaginary = (gains_part[:, 1] * weights)[:, None, :]
    steering_real = ((gain_real * cosine - gain_imaginary * sine_part) * scale_factor).astype(
        jnp.bfloat16
    )
    steering_imaginary = ((gain_real * sine_part + gain_imaginary * cosine) * scale_factor).astype(
        jnp.bfloat16
    )
    spectrum_real = whole_set[:, :, 0]
    spectrum_imaginary = whole_set[:, :, 1]
    volt_real = jnp.einsum(
        "jan,njg->jag", steering_real, spectrum_real, preferred_element_type=jnp.float32
    ) - jnp.einsum(
        "jan,njg->jag", steering_imaginary, spectrum_imaginary, preferred_element_type=jnp.float32
    )
    volt_imag = jnp.einsum(
        "jan,njg->jag", steering_real, spectrum_imaginary, preferred_element_type=jnp.float32
    ) + jnp.einsum(
        "jan,njg->jag", steering_imaginary, spectrum_real, preferred_element_type=jnp.float32
    )
    return volt_real * volt_real + volt_imag * volt_imag


def matvec(matrix, vector):
    return jnp.einsum("crj,cj->cr", matrix, vector, precision=lax.Precision.HIGHEST)


def general_shards(samples, window_taps, sky_model, prior_gains, beam_steering, input_flags):
    local_inputs = samples.shape[0]
    transform_count = samples.shape[2]
    frames = samples.shape[3]
    tap_count = window_taps.shape[0]
    kept_count = NCH
    time_count = lax.axis_size("tm")
    beam_count = lax.axis_size("beam")
    time_index = lax.axis_index("tm")
    beam_index = lax.axis_index("beam")
    chan_index = lax.axis_index("chan")
    weights = input_flags.astype(jnp.float32)
    stacked = samples.reshape(local_inputs, 2 * transform_count, frames)
    previous = from_behind(stacked[:, :, frames - tap_count + 1 :], "tm", 1)
    extended = jnp.concatenate([previous, stacked], axis=2)
    spectra = filter_bank(extended, window_taps, kept_count, frames).reshape(
        1, local_inputs, kept_count, 2, 1, frames
    )
    mixed = lax.all_to_all(spectra, ("chan", "tm"), split_axis=2, concat_axis=0, tiled=True)
    blocks = mixed.reshape(
        mixed.shape[0] // time_count, time_count, local_inputs, mixed.shape[2], 2, frames
    )
    turned = jnp.transpose(blocks, (0, 2, 3, 4, 1, 5))
    joined = lax.all_gather(turned, "beam", axis=1, tiled=True)
    input_count = joined.shape[0] * joined.shape[1]
    chan_local = joined.shape[2]
    whole_set = joined.reshape(input_count, chan_local, 2, joined.shape[4] * frames)
    half_rows = input_count // beam_count
    owned_rows = lax.dynamic_slice_in_dim(whole_set, beam_index * half_rows, half_rows, 0)
    terms = cross_rows(owned_rows, whole_set)
    visibilities = (terms / whole_set.shape[3]).astype(jnp.bfloat16)
    channels = (chan_index * time_count + time_index) * chan_local + jnp.arange(
        chan_local, dtype=jnp.int32
    )
    beam_power = form_beams(whole_set, prior_gains, weights, beam_steering, channels, kept_count)
    vis_used = lax.optimization_barrier(visibilities).astype(jnp.float32)
    model_values = sky_model.astype(jnp.float32)
    weighted = jnp.stack(
        [
            vis_used[:, 0] * model_values[:, 0] + vis_used[:, 1] * model_values[:, 1],
            vis_used[:, 1] * model_values[:, 0] - vis_used[:, 0] * model_values[:, 1],
        ],
        axis=1,
    )
    model_power = model_values[:, 0] * model_values[:, 0] + model_values[:, 1] * model_values[:, 1]
    row_start = beam_index * half_rows
    current = prior_gains
    updated = lax.dynamic_slice_in_dim(current, row_start, half_rows, 2)
    for step_index in range(ITERS):
        masked_real = current[:, 0] * weights
        masked_imag = current[:, 1] * weights
        vectors = jnp.stack([masked_real, masked_imag], axis=2)
        products = jnp.einsum("csrj,cjv->csrv", weighted, vectors, precision=lax.Precision.HIGHEST)
        numer_real = products[:, 0, :, 0] - products[:, 1, :, 1]
        numer_imag = products[:, 0, :, 1] + products[:, 1, :, 0]
        denom = (
            matvec(
                model_power,
                weights * (current[:, 0] * current[:, 0] + current[:, 1] * current[:, 1]),
            )
            + epsilon
        )
        older = lax.dynamic_slice_in_dim(current, row_start, half_rows, 2)
        updated = damping * older + (1.0 - damping) * jnp.stack(
            [numer_real / denom, numer_imag / denom], axis=1
        )
        if step_index + 1 < ITERS:
            current = lax.all_gather(updated, "beam", axis=2, tiled=True)
    return (visibilities, updated, beam_power)


LANES = 128
SUBLANES = 8
NEXT_ROWS = 4
MIB = 2**20
UPDATE_LIMIT = 14 * MIB
NT = (((1,), (1,)), ((), ()))
TN = (((0,), (0,)), ((), ()))
NN = (((1,), (0,)), ((), ()))


def mxu(left, right, dims):
    return lax.dot_general(left, right, dims, preferred_element_type=jnp.float32)


def transform_rows(kept_count, transform_count, owners, shares):
    by_owner = np.arange(kept_count).reshape(owners, -1)
    ends = np.cumsum(shares)
    kept = np.concatenate(
        [by_owner[:, end - share : end].reshape(-1) for share, end in zip(shares, ends)]
    )
    phases = (kept[:, None] * np.arange(transform_count)[None, :] % transform_count) * (
        2.0 * math.pi / transform_count
    )
    table = np.concatenate([np.cos(phases), np.sin(phases)], axis=1) / math.sqrt(transform_count)
    return jnp.asarray(table.astype(jnp.bfloat16))


def transformed(owners, frames, table, windowed_ref, turned_ref, copies=()):
    rows = table.shape[0]
    width = turned_ref.shape[1]
    share = rows // owners
    total = windowed_ref.shape[0] // width
    step = 4
    for frame in range(0, total, step):
        some = min(step, total - frame)
        for copy in copies[frame : frame + some]:
            copy.wait()
        block = mxu(table, windowed_ref[frame * width : (frame + some) * width, :], NT)
        for i in range(some):
            at = frame + i
            part = block[:, i * width : (i + 1) * width]
            if at < frames:
                turned_ref[pl.ds(at, rows, stride=frames), :] = part
            else:
                first = rows * frames + (at - frames) * share
                for owner in range(owners):
                    turned_ref[pl.ds(first + owner * (total - frames) * share, share), :] = part[
                        owner * share : (owner + 1) * share
                    ]


def filter_kernel(
    owners,
    x_hbm,
    taps_hbm,
    table_hbm,
    windowed_hbm,
    out_ref,
    x_ref,
    table_ref,
    taps_ref,
    frames_ref,
    windowed_ref,
    turned_ref,
    sems,
    keep_sems,
):
    inputs, _, frames, points = x_ref.shape
    taps = taps_ref.shape[0]
    width = 2 * inputs
    pieces = sems.shape[0] - 2
    group = inputs // pieces
    table_copy = pltpu.make_async_copy(
        table_hbm.at[pl.ds(0, table_ref.shape[0])], table_ref, sems.at[pieces]
    )
    copies = [
        pltpu.make_async_copy(
            x_hbm.at[pl.ds(i * group, group)], x_ref.at[pl.ds(i * group, group)], sems.at[i]
        )
        for i in range(pieces)
    ]
    taps_copy = pltpu.make_async_copy(taps_hbm, taps_ref, sems.at[pieces + 1])
    taps_copy.start()
    for copy in copies:
        copy.start()
    taps_copy.wait()

    def spread(i, carry):
        for part in range(2):
            block = x_ref[i, part].astype(jnp.float32)
            for piece in range(points // LANES):
                here = pl.ds(pl.multiple_of(i * frames, frames), frames)
                frames_ref[part, piece, here, :] = block[:, piece * LANES : (piece + 1) * LANES]
        return carry

    for i, copy in enumerate(copies):
        copy.wait()
        lax.fori_loop(i * group, (i + 1) * group, spread, 0, unroll=8)

    table_copy.start()

    def keep(piece, half):
        here = pl.ds(pl.multiple_of(half * points + piece * LANES, LANES), LANES)
        return pltpu.make_async_copy(
            windowed_ref.at[:, here], windowed_hbm.at[:, here], keep_sems.at[half, piece]
        )

    def window(piece, carry):
        lanes = pl.ds(pl.multiple_of(piece * LANES, LANES), LANES)
        upper = pl.ds(pl.multiple_of(points + piece * LANES, LANES), LANES)
        weights = taps_ref[:, lanes]
        weights = [
            jnp.broadcast_to(weights[tap : tap + 1], (2 * SUBLANES, LANES)) for tap in range(taps)
        ]
        for first in range(0, inputs, 2 * SUBLANES):
            for part in range(2):
                values = [
                    frames_ref[
                        part, piece, pl.ds(first * frames + frame, 2 * SUBLANES, stride=frames), :
                    ]
                    for frame in range(frames)
                ]
                for frame in range(frames + taps - 1):
                    total = None
                    for tap in range(taps):
                        source = frame + tap - (taps - 1)
                        if 0 <= source < frames:
                            term = values[source] * weights[tap]
                            total = term if total is None else total + term
                    base = frame * width + first
                    rows = slice(base, base + 2 * SUBLANES)
                    swapped = slice(base + inputs, base + inputs + 2 * SUBLANES)
                    total = total.astype(jnp.bfloat16)
                    if part == 0:
                        windowed_ref[rows, lanes] = total
                        windowed_ref[swapped, upper] = -total
                    else:
                        windowed_ref[rows, upper] = total
                        windowed_ref[swapped, lanes] = total
        keep(piece, 0).start()
        keep(piece, 1).start()
        return carry

    lax.fori_loop(0, points // LANES, window, 0, unroll=2)
    table_copy.wait()
    transformed(owners, frames, table_ref[...], windowed_ref, turned_ref)
    share = table_ref.shape[0] // owners
    main = share * frames
    extra = share * (taps - 1)
    for owner in range(owners):
        out_ref[owner, :main, :] = turned_ref[owner * main : (owner + 1) * main, :].astype(
            jnp.bfloat16
        )
        first = owners * main + owner * extra
        out_ref[owner, main : main + extra, :] = turned_ref[first : first + extra, :].astype(
            jnp.bfloat16
        )
    for piece in range(points // LANES):
        keep(piece, 0).wait()
        keep(piece, 1).wait()


def rows_copies(source, target, sems, first=0):
    size = target.shape[0] // sems.shape[0]
    return [
        pltpu.make_async_copy(
            source.at[pl.ds(first + i * size, size)], target.at[pl.ds(i * size, size)], sems.at[i]
        )
        for i in range(sems.shape[0])
    ]


def spill_kernel(first, start, windowed_hbm, table_hbm, out_ref, windowed_ref, table_ref, sems):
    copies = rows_copies(windowed_hbm, windowed_ref, sems.at[pl.ds(0, 1)], first)
    copies += rows_copies(table_hbm, table_ref, sems.at[pl.ds(1, 1)], start)
    for copy in copies:
        copy.start()
    for copy in copies:
        copy.wait()
    frames, _, width = out_ref.shape
    block = mxu(table_ref[...], windowed_ref[...], NT)
    for frame in range(frames):
        out_ref[frame] = block[:, frame * width : (frame + 1) * width].astype(jnp.bfloat16)


def filter_more_kernel(
    owners, start, windowed_hbm, table_hbm, turned_ref, windowed_ref, table_ref, sems
):
    frames = sems.shape[0] - 1
    copies = rows_copies(windowed_hbm, windowed_ref, sems.at[pl.ds(0, frames)])
    table_copies = rows_copies(table_hbm, table_ref, sems.at[pl.ds(frames, 1)], start)
    for copy in table_copies + copies:
        copy.start()
    for copy in table_copies:
        copy.wait()
    transformed(owners, frames, table_ref[...], windowed_ref, turned_ref, copies)


def added_kernel(turned_ref, added_ref, out_ref, total_ref):
    owners, main, _ = out_ref.shape
    nexts, rows, _ = added_ref.shape
    frames = turned_ref.shape[0] // rows
    total_ref[...] = turned_ref[...]
    for frame in range(nexts):
        here = pl.ds(frame, rows, stride=frames)
        total_ref[here, :] = turned_ref[here, :] + added_ref[frame].astype(jnp.float32)
    for owner in range(owners):
        out_ref[owner] = total_ref[owner * main : (owner + 1) * main, :].astype(jnp.bfloat16)


def filtered(samples, window_taps, kept_count, owners, shares):
    inputs, _, points, frames = samples.shape
    taps = window_taps.shape[0]
    width = 2 * inputs
    table = transform_rows(kept_count, points, owners, shares)
    by_frame = jnp.transpose(samples, (0, 1, 3, 2))
    by_frame = pltpu.with_memory_space_constraint(by_frame, pltpu.HBM)
    table = pltpu.with_memory_space_constraint(table, pltpu.HBM)
    window_taps = pltpu.with_memory_space_constraint(window_taps, pltpu.HBM)
    pieces = points // LANES
    anywhere = pl.BlockSpec(memory_space=pl.ANY)
    vmem = pl.BlockSpec(memory_space=pltpu.VMEM)
    windowed_shape = ((frames + taps - 1) * width, 2 * points)
    rows = owners * shares[0]
    windowed, first = pl.pallas_call(
        functools.partial(filter_kernel, owners),
        out_shape=[
            pltpu.HBM(windowed_shape, jnp.bfloat16),
            jax.ShapeDtypeStruct((owners, shares[0] * (frames + taps - 1), width), jnp.bfloat16),
        ],
        in_specs=[anywhere, anywhere, anywhere],
        out_specs=[anywhere, vmem],
        scratch_shapes=[
            pltpu.VMEM(by_frame.shape, jnp.bfloat16),
            pltpu.VMEM((rows, 2 * points), jnp.bfloat16),
            pltpu.VMEM(window_taps.shape, jnp.float32),
            pltpu.VMEM((2, pieces, inputs * frames, LANES), jnp.float32),
            pltpu.VMEM(windowed_shape, jnp.bfloat16),
            pltpu.VMEM((rows * (frames + taps - 1), width), jnp.float32),
            pltpu.SemaphoreType.DMA((6,)),
            pltpu.SemaphoreType.DMA((2, pieces)),
        ],
        compiler_params=pltpu.CompilerParams(vmem_limit_bytes=32 * MIB),
        name="filter",
    )(by_frame, window_taps, table)
    windowed = pltpu.with_memory_space_constraint(windowed, pltpu.HBM)

    def more(chunk, start):
        rows = owners * shares[chunk]
        spill = pl.pallas_call(
            functools.partial(spill_kernel, frames * width, start),
            out_shape=jax.ShapeDtypeStruct((taps - 1, rows, width), jnp.bfloat16),
            in_specs=[anywhere, anywhere],
            out_specs=vmem,
            scratch_shapes=[
                pltpu.VMEM(((taps - 1) * width, 2 * points), jnp.bfloat16),
                pltpu.VMEM((rows, 2 * points), jnp.bfloat16),
                pltpu.SemaphoreType.DMA((2,)),
            ],
            compiler_params=pltpu.CompilerParams(vmem_limit_bytes=24 * MIB),
            name="spill",
        )(windowed, table)
        added = from_behind(spill, "tm", 1)
        turned = pl.pallas_call(
            functools.partial(filter_more_kernel, owners, start),
            out_shape=jax.ShapeDtypeStruct((rows * frames, width), jnp.float32),
            in_specs=[anywhere, anywhere],
            out_specs=vmem,
            scratch_shapes=[
                pltpu.VMEM((frames * width, 2 * points), jnp.bfloat16),
                pltpu.VMEM((rows, 2 * points), jnp.bfloat16),
                pltpu.SemaphoreType.DMA((frames + 1,)),
            ],
            compiler_params=pltpu.CompilerParams(vmem_limit_bytes=24 * MIB),
            name="filter_more",
        )(windowed, table)
        return pl.pallas_call(
            added_kernel,
            out_shape=jax.ShapeDtypeStruct((owners, shares[chunk] * frames, width), jnp.bfloat16),
            in_specs=[vmem, vmem],
            out_specs=vmem,
            scratch_shapes=[pltpu.VMEM((rows * frames, width), jnp.float32)],
            compiler_params=pltpu.CompilerParams(vmem_limit_bytes=24 * MIB),
            name="added",
        )(turned, added)

    sent = [first]
    start = rows
    for chunk in range(1, len(shares)):
        sent.append(more(chunk, start))
        start += owners * shares[chunk]
    return sent


def gain_terms(real, imag, gains, flags):
    weights = flags.astype(jnp.float32)
    gain_real = gains[0:1] * weights
    gain_imag = gains[1:2] * weights
    turned_real = real * gain_real + imag * gain_imag
    turned_imag = imag * gain_real - real * gain_imag
    power = weights * (gains[0:1] * gains[0:1] + gains[1:2] * gains[1:2])
    return turned_real, turned_imag, power


def denominators(power, model_real, model_imag):
    model_power = model_real * model_real + model_imag * model_imag
    terms = model_power * jnp.broadcast_to(power.astype(jnp.bfloat16), model_power.shape)
    folded = terms[:, :LANES]
    for first in range(LANES, terms.shape[1], LANES):
        folded = folded + terms[:, first : first + LANES]
    return mxu(jnp.ones((SUBLANES, LANES), jnp.bfloat16), folded, NT)[0:1] + epsilon


def put_turned(turned_ref, at, real, imag, gains, flags):
    turned_real, turned_imag, power = gain_terms(real, imag, gains, flags)
    frames = real.shape[0]
    turned_real = turned_real.astype(jnp.bfloat16)
    turned_imag = turned_imag.astype(jnp.bfloat16)
    turned_ref[at, 0, :frames] = turned_real
    turned_ref[at, 0, frames:] = turned_imag
    turned_ref[at, 1, :frames] = -turned_imag
    turned_ref[at, 1, frames:] = turned_real
    return power


def modelled(turned_ref, at, model_real, model_imag):
    return mxu(turned_ref[at, 0], model_real, NT) + mxu(turned_ref[at, 1], model_imag, NT)


def updated_gains(own, products, denom, older):
    own_real, own_imag = own
    frames = own_real.shape[0]
    real = products[:frames]
    imag = products[frames:]
    numer_real = jnp.sum(own_real * real + own_imag * imag, axis=0, keepdims=True)
    numer_imag = jnp.sum(own_imag * real - own_real * imag, axis=0, keepdims=True)
    numer = jnp.concatenate([numer_real, numer_imag], axis=0) / frames
    return damping * older + (1.0 - damping) * (numer / denom)


def own_half(values, core):
    half = values.shape[1] // 2
    return jnp.where(core == 0, values[:, :half], values[:, half:])


def model_kernel(
    base, step, reach, own_hbm, model_hbm, centre_ref, steering_ref, model_ref, table_ref, sem
):
    del own_hbm
    count = min(MODEL_BLOCK, model_ref.shape[0])
    copy = pltpu.make_async_copy(
        model_hbm.at[pl.ds(base, count)], model_ref.at[pl.ds(0, count)], sem
    )
    copy.start()
    steering_tables(centre_ref[0], steering_ref, table_ref, step, reach)
    copy.wait()


def first_kernel(
    times, base, core_ref, own_ref, other_ref, model_hbm, gains_ref, flags_ref, here_ref, *refs
):
    del here_ref
    spectra_ref, updated_ref, model_ref, next_ref, turned_ref, products_ref, power_ref, denom_ref, sems = refs
    core = core_ref[0]
    share = spectra_ref.shape[0]
    sources, rows, width = own_ref.shape
    frames = spectra_ref.shape[1] // 2 // times
    nexts = rows // share - frames
    columns = sources // times
    lane = lax.broadcasted_iota(jnp.int32, (frames, width), 1)
    row = lax.broadcasted_iota(jnp.int32, (frames, width), 0)
    low = lane < width // 2
    count = BLOCK

    def copy(i):
        here = pl.ds(i * VIS_BLOCK, VIS_BLOCK)
        there = pl.ds(base + i * VIS_BLOCK, VIS_BLOCK)
        return pltpu.make_async_copy(model_hbm.at[there], model_ref.at[here], sems.at[i])

    groups = share // VIS_BLOCK
    there = min(MODEL_BLOCK, share) // VIS_BLOCK
    ahead = 3
    for i in range(there, min(there + ahead, groups)):
        copy(i).start()
    if nexts:
        for source in range(sources):
            for side, ref in enumerate((own_ref, other_ref)):
                next_ref[side, source] = ref[source, share * frames :, :].astype(jnp.float32)

    def assemble(i):
        main_rows = pl.ds(pl.multiple_of(i * (count * frames), count * frames), count * frames)

        def loaded(side, column, time):
            ref = (own_ref, other_ref)[side]
            source = column * times + time
            block = ref[source, main_rows, :].astype(jnp.float32)
            extra = []
            if time > 0:
                extra = [
                    next_ref[
                        side, source - 1, pl.ds(pl.multiple_of(share * k + i * count, count), count), :
                    ]
                    for k in range(nexts)
                ]
            return block, extra

        def one(value, c):
            block, extra = value
            block = block[c * frames : (c + 1) * frames]
            for k, more in enumerate(extra):
                block = block + jnp.where(row == k, more[c : c + 1], 0.0)
            return block

        blocks = {
            (column, time): (loaded(0, column, time), loaded(1, column, time))
            for column in range(columns)
            for time in range(times)
        }
        for c in range(count):
            real_rows = []
            imag_rows = []
            for time in range(times):
                reals = []
                imags = []
                for column in range(columns):
                    own, other = blocks[column, time]
                    own = one(own, c)
                    other = one(other, c)
                    first = jnp.where(core == 0, own, other)
                    second = jnp.where(core == 0, other, own)
                    reals.append(jnp.where(low, first, pltpu.roll(second, width // 2, 1)))
                    imags.append(jnp.where(low, pltpu.roll(first, width // 2, 1), second))
                real_rows.append(jnp.concatenate(reals, axis=1))
                imag_rows.append(jnp.concatenate(imags, axis=1))
            spectra = jnp.concatenate(real_rows + imag_rows, axis=0)
            spectra_ref[i * count + c] = spectra.astype(jnp.bfloat16)

    def update(i):
        for part in range(count // VIS_BLOCK):
            group = i * (count // VIS_BLOCK) + part

            @pl.when(group >= there)
            def _():
                copy(group).wait()

                @pl.when(group + ahead < groups)
                def _():
                    copy(group + ahead).start()

        channels = [i * count + c for c in range(count)]

        def parts(here):
            values = spectra_ref[here].astype(jnp.float32)
            half = values.shape[0] // 2
            return values[:half], values[half:]

        for c, here in enumerate(channels):
            real, imag = parts(here)
            flags = flags_ref[pl.ds(base + here, 1), :]
            power_ref[c] = put_turned(turned_ref, c, real, imag, gains_ref[base + here], flags)
        for c, here in enumerate(channels):
            model_real = model_ref[here, 0]
            model_imag = model_ref[here, 1]
            products_ref[c] = modelled(turned_ref, c, model_real, model_imag)
            denom_ref[c] = denominators(power_ref[c], model_real, model_imag)
        for c, here in enumerate(channels):
            real, imag = parts(here)
            updated_ref[here] = updated_gains(
                (own_half(real, core), own_half(imag, core)),
                products_ref[c],
                denom_ref[c],
                own_half(gains_ref[base + here], core),
            )

    def step(i, carry):
        update(i)
        assemble(i + 1)
        return carry

    last = share // count - 1
    assemble(0)
    lax.fori_loop(0, last, step, 0)
    update(last)


def second_kernel(
    base, core_ref, spectra_ref, model_ref, own_ref, other_ref, flags_ref, beams_ref, *refs
):
    visibilities_hbm, updated_hbm, beams_hbm, ready_ref, updated_ref = refs[-11:-6]
    turned_ref, products_ref, power_ref, denom_ref, sems, sem = refs[-6:]
    core = core_ref[0]
    share = spectra_ref.shape[0]
    slots, count = ready_ref.shape[:2]
    pieces = sems.shape[1]
    size = count // pieces
    steps = share // count
    beams_copy = pltpu.make_async_copy(beams_ref, beams_hbm.at[pl.ds(base, share)], sem.at[0])
    beams_copy.start()

    def copy(i, slot, piece):
        return pltpu.make_async_copy(
            ready_ref.at[slot, pl.ds(piece * size, size)],
            visibilities_hbm.at[pl.ds(base + i * count + piece * size, size)],
            sems.at[slot, piece],
        )

    def step(i, carry):
        slot = lax.rem(i, slots)

        @pl.when(i >= slots)
        def _():
            for piece in range(pieces):
                copy(i - slots, slot, piece).wait()

        channels = [i * count + c for c in range(count)]

        def parts(here):
            values = spectra_ref[here].astype(jnp.float32)
            half = values.shape[0] // 2
            return values[:half], values[half:]

        for c, here in enumerate(channels):
            real, imag = parts(here)
            own = own_ref[here]
            other = other_ref[here]
            first = jnp.where(core == 0, own, other)
            second = jnp.where(core == 0, other, own)
            gains = jnp.concatenate([first, second], axis=1)
            flags = flags_ref[pl.ds(base + here, 1), :]
            power_ref[c] = put_turned(turned_ref, c, real, imag, gains, flags)
        for c, here in enumerate(channels):
            real, imag = parts(here)
            frames = real.shape[0]
            own_real = own_half(real, core)
            own_imag = own_half(imag, core)
            paired = jnp.concatenate([own_real, own_imag], axis=0) / frames
            rotated = jnp.concatenate([own_imag, -own_real], axis=0) / frames
            spectra = spectra_ref[here]
            ready_ref[slot, c, 0] = mxu(paired.astype(jnp.bfloat16), spectra, TN).astype(jnp.bfloat16)
            ready_ref[slot, c, 1] = mxu(rotated.astype(jnp.bfloat16), spectra, TN).astype(jnp.bfloat16)
            if c % size == size - 1:
                copy(i, slot, c // size).start()
            model_real = model_ref[here, 0]
            model_imag = model_ref[here, 1]
            products_ref[c] = modelled(turned_ref, c, model_real, model_imag)
            denom_ref[c] = denominators(power_ref[c], model_real, model_imag)
        for c, here in enumerate(channels):
            real, imag = parts(here)
            updated_ref[here] = updated_gains(
                (own_half(real, core), own_half(imag, core)),
                products_ref[c],
                denom_ref[c],
                own_ref[here],
            )
        return carry

    lax.fori_loop(0, steps, step, 0)
    last = pltpu.make_async_copy(updated_ref, updated_hbm.at[pl.ds(base, share)], sem.at[1])
    last.start()
    for i in range(max(0, steps - slots), steps):
        for piece in range(pieces):
            copy(i, i % slots, piece).wait()
    last.wait()
    beams_copy.wait()


def series_length(reach):
    terms = 1
    while 2.0 * (0.5 * reach) ** terms / math.factorial(terms) >= 2.0**-22:
        terms += 1
    return terms


def bessel(order, x, reach):
    count = 1
    while (0.5 * reach) ** (2 * count) / math.factorial(count) ** 2 >= 2.0**-26:
        count += 1
    square = x * x * -0.25
    total = jnp.full_like(x, 1.0 / (math.factorial(count - 1) * math.factorial(count - 1 + order)))
    for m in reversed(range(count - 1)):
        total = total * square + 1.0 / (math.factorial(m) * math.factorial(m + order))
    for _ in range(order):
        total = total * (0.5 * x)
    return total


def turns(count, period):
    quarter = period // 4
    quadrant = lax.shift_right_logical(count + period // 8, quarter.bit_length() - 1)
    angle = (count - quadrant * quarter).astype(jnp.float32) * (2.0 * math.pi / period)
    square = angle * angle
    sine_part = jnp.full_like(angle, 1.0 / math.factorial(9))
    cosine = jnp.full_like(angle, 1.0 / math.factorial(8))
    for power in (7, 5, 3, 1):
        sign = -1.0 if power % 4 == 3 else 1.0
        sine_part = sine_part * square + sign / math.factorial(power)
        cosine = cosine * square + sign / math.factorial(power - 1)
    sine_part = sine_part * angle
    odd = (quadrant & 1) == 1
    real = jnp.where(odd, sine_part, cosine)
    imag = jnp.where(odd, cosine, sine_part)
    real = jnp.where(((quadrant + 1) & 2) == 2, -real, real)
    imag = jnp.where((quadrant & 2) == 2, -imag, imag)
    return real, imag


def steering_tables(centre, steering_ref, table_ref, step, reach):
    inputs = table_ref.shape[1] // 2
    beams = table_ref.shape[2] // 2
    quarter = inputs // 4
    for column in range(4):
        for first in range(0, quarter, 4 * SUBLANES):
            shape = (4 * SUBLANES, beams)
            within = lax.broadcasted_iota(jnp.int32, shape, 0) + first
            phase_index = (steering_ref[0:1, :] * (column * 64) + steering_ref[1:2, :] * within) & 255
            cosine, sine_part = turns(phase_index * centre, round(4.0 * math.pi / step))
            offset = (phase_index - 128).astype(jnp.float32) * (reach * step)
            at = column * quarter + first
            rows = slice(at, at + shape[0])
            lower = slice(inputs + at, inputs + at + shape[0])
            for term in range(table_ref.shape[0]):
                real, imag = (
                    (cosine, sine_part),
                    (-sine_part, cosine),
                    (-cosine, -sine_part),
                    (sine_part, -cosine),
                )[term % 4]
                factor = bessel(term, offset, 128 * reach * step) * (2.0 if term else 1.0)
                real = factor * real
                imag = factor * imag
                real = real.astype(jnp.bfloat16)
                imag = imag.astype(jnp.bfloat16)
                table_ref[term, rows, :beams] = real
                table_ref[term, rows, beams:] = imag
                table_ref[term, lower, :beams] = -imag
                table_ref[term, lower, beams:] = real


def beams_kernel(base, spectra_ref, gains_ref, flags_ref, table_ref, *refs):
    power_ref, left_ref = refs
    count, doubled, inputs = spectra_ref.shape
    frames = doubled // 2
    scale = 1.0 / math.sqrt(inputs)
    middle = 0.5 * (count - 1)
    terms = table_ref.shape[0]
    for c in range(count):
        values = spectra_ref[c].astype(jnp.float32)
        real = values[:frames]
        imag = values[frames:]
        at = base + c
        weights = flags_ref[at : at + 1].astype(jnp.float32) * scale
        gain_real = gains_ref[at, 0:1] * weights
        gain_imag = gains_ref[at, 1:2] * weights
        lit_real = real * gain_real - imag * gain_imag
        lit_imag = real * gain_imag + imag * gain_real
        rows = slice(c * frames, (c + 1) * frames)
        for term in range(terms):
            power = math.cos(term * math.acos((c - middle) / max(middle, 0.5)))
            left_ref[term, rows, :inputs] = (lit_real * power).astype(jnp.bfloat16)
            left_ref[term, rows, inputs:] = (lit_imag * power).astype(jnp.bfloat16)
    total = mxu(left_ref[0], table_ref[0], NN)
    for term in range(1, terms):
        total = total + mxu(left_ref[term], table_ref[term], NN)
    beams = total.shape[1] // 2
    real = total[:, :beams]
    imag = total[:, beams:]
    power_ref[...] = (real * real + imag * imag).reshape(count, frames, beams)


def formed_beams(base, spectra, table, gains, flags):
    share, doubled, input_count = spectra.shape
    frame_count = doubled // 2
    vmem = pl.BlockSpec(memory_space=pltpu.VMEM)
    return pl.pallas_call(
        functools.partial(beams_kernel, base),
        in_specs=[vmem] * 4,
        out_specs=vmem,
        out_shape=jax.ShapeDtypeStruct((share, frame_count, table.shape[2] // 2), jnp.float32),
        scratch_shapes=[
            pltpu.VMEM((table.shape[0], share * frame_count, 2 * input_count), jnp.bfloat16),
        ],
        compiler_params=pltpu.CompilerParams(vmem_limit_bytes=UPDATE_LIMIT),
        name="beams",
    )(spectra, gains, flags, table)


def chunk_shards(samples, window_taps, sky_model, prior_gains, beam_steering, input_flags):
    frames = samples.shape[3]
    chan_local, _, half_rows, input_count = sky_model.shape
    times = lax.axis_size("tm")
    owners = lax.axis_size("chan") * times
    core = lax.axis_index("beam").astype(jnp.int32).reshape(1)
    first_channel = (lax.axis_index("chan") * times + lax.axis_index("tm")) * chan_local
    kept_count = chan_local * owners
    frame_count = frames * times
    beams = beam_steering.shape[1]
    shares = chunk_shares(chan_local)
    bases = [sum(shares[:chunk]) for chunk in range(len(shares))]
    centres = [
        (2 * (kept_count + first_channel + base) + share - 1).astype(jnp.int32).reshape(1)
        for base, share in zip(bases, shares)
    ]
    sent = filtered(samples, window_taps, kept_count, owners, shares)
    swap = [(0, 1), (1, 0)]
    smem = pl.BlockSpec(memory_space=pltpu.SMEM)
    vmem = pl.BlockSpec(memory_space=pltpu.VMEM)
    anywhere = pl.BlockSpec(memory_space=pl.ANY)
    step = 2.0 * math.pi / (512 * kept_count)

    sent[0], gains, flags, steering, core, centres = lax.optimization_barrier(
        (sent[0], prior_gains, input_flags, beam_steering, core, centres)
    )
    visibilities = None
    beam_power = None
    gains_new = None
    for chunk, (base, share) in enumerate(zip(bases, shares)):
        own = lax.all_to_all(sent[chunk], ("chan", "tm"), 0, 0, tiled=True)
        if gains_new is not None:
            own, gains_new = lax.optimization_barrier((own, gains_new))
        other = lax.ppermute(own, "beam", swap)
        model_shape = (share, *sky_model.shape[1:])
        reach = max(0.5 * (share - 1), 0.5)
        table_shape = (series_length(128 * reach * step), 2 * input_count, 2 * beams)
        model, table = pl.pallas_call(
            functools.partial(model_kernel, base, step, reach),
            in_specs=[anywhere, anywhere, smem, vmem],
            out_specs=[vmem, vmem],
            out_shape=[
                pltpu.VMEM(model_shape, sky_model.dtype),
                jax.ShapeDtypeStruct(table_shape, jnp.bfloat16),
            ],
            scratch_shapes=[pltpu.SemaphoreType.DMA],
            compiler_params=pltpu.CompilerParams(vmem_limit_bytes=UPDATE_LIMIT),
            name="model",
        )(own, sky_model, centres[chunk], steering)
        model = pltpu.with_memory_space_constraint(model, pltpu.VMEM)
        half_shape = jax.ShapeDtypeStruct((share, 2, half_rows), jnp.float32)
        spectra, gains_own, model = pl.pallas_call(
            functools.partial(first_kernel, times, base),
            in_specs=[smem, vmem, vmem, anywhere, vmem, vmem, vmem],
            out_specs=[vmem, vmem, vmem],
            out_shape=[
                jax.ShapeDtypeStruct((share, 2 * frame_count, input_count), jnp.bfloat16),
                half_shape,
                pltpu.VMEM(model_shape, sky_model.dtype),
            ],
            input_output_aliases={6: 2},
            scratch_shapes=[
                pltpu.VMEM((2, owners, max(own.shape[1] - share * frames, SUBLANES), own.shape[2]), jnp.float32),
                pltpu.VMEM((BLOCK, 2, 2 * frame_count, input_count), jnp.bfloat16),
                pltpu.VMEM((BLOCK, 2 * frame_count, half_rows), jnp.float32),
                pltpu.VMEM((BLOCK, 1, input_count), jnp.float32),
                pltpu.VMEM((BLOCK, 1, half_rows), jnp.float32),
                pltpu.SemaphoreType.DMA((share // VIS_BLOCK,)),
            ],
            compiler_params=pltpu.CompilerParams(vmem_limit_bytes=UPDATE_LIMIT),
            name="first_update",
        )(core, own, other, sky_model, gains, flags, model)
        model = pltpu.with_memory_space_constraint(model, pltpu.VMEM)
        gains_other = lax.ppermute(gains_own, "beam", swap)
        powers = formed_beams(base, spectra, table, gains, flags)
        earlier = [] if visibilities is None else [visibilities, gains_new, beam_power]
        visibilities, gains_new, beam_power = pl.pallas_call(
            functools.partial(second_kernel, base),
            in_specs=[smem] + [vmem] * 6 + [anywhere] * len(earlier),
            out_specs=[anywhere] * 3,
            out_shape=[
                jax.ShapeDtypeStruct(sky_model.shape, jnp.bfloat16),
                jax.ShapeDtypeStruct((chan_local, 2, half_rows), jnp.float32),
                jax.ShapeDtypeStruct((chan_local, frame_count, beams), jnp.float32),
            ],
            scratch_shapes=[
                pltpu.VMEM((2, BLOCK, 2, half_rows, input_count), jnp.bfloat16),
                pltpu.VMEM((share, 2, half_rows), jnp.float32),
                pltpu.VMEM((BLOCK, 2, 2 * frame_count, input_count), jnp.bfloat16),
                pltpu.VMEM((BLOCK, 2 * frame_count, half_rows), jnp.float32),
                pltpu.VMEM((BLOCK, 1, input_count), jnp.float32),
                pltpu.VMEM((BLOCK, 1, half_rows), jnp.float32),
                pltpu.SemaphoreType.DMA((2, 4)),
                pltpu.SemaphoreType.DMA((2,)),
            ],
            input_output_aliases={7: 0, 8: 1, 9: 2} if earlier else {},
            compiler_params=pltpu.CompilerParams(vmem_limit_bytes=UPDATE_LIMIT),
            name="second_update",
        )(core, spectra, model, gains_own, gains_other, flags, powers, *earlier)
    return (
        visibilities,
        gains_new,
        jnp.transpose(beam_power, (0, 2, 1)),
    )


BLOCK = 8
VIS_BLOCK = 4
MODEL_BLOCK = 8


def chunk_shares(chan_local):
    blocks = chan_local // BLOCK
    first = blocks * 3 // 8
    return [first * BLOCK, (blocks - first) * BLOCK]


def shards(samples, window_taps, sky_model, prior_gains, beam_steering, input_flags):
    inputs, _, points, frames = samples.shape
    chan_local, _, half_rows, input_count = sky_model.shape
    frame_count = frames * lax.axis_size("tm")
    owners = lax.axis_size("chan") * lax.axis_size("tm")
    fits = (
        ITERS == 2
        and 2 * inputs == LANES
        and points % LANES == 0
        and frames == SUBLANES
        and window_taps.shape[0] == NEXT_ROWS
        and lax.axis_size("beam") == 2
        and chan_local % (8 * BLOCK) == 0
        and half_rows % LANES == 0
        and frame_count & (frame_count - 1) == 0
        and chan_local * owners & (chan_local * owners - 1) == 0
        and half_rows % (4 * LANES // 2) == 0
        and beam_steering.shape[1] % LANES == 0
    )
    form = chunk_shards if fits else general_shards
    return form(samples, window_taps, sky_model, prior_gains, beam_steering, input_flags)


def solution(mesh):
    return jax.shard_map(
        shards,
        mesh=mesh,
        in_specs=(
            P(("group", "chan", "beam"), None, None, "tm"),
            P(),
            P(("group", "chan", "tm"), None, "beam", None),
            P(("group", "chan", "tm"), None, None),
            P(None, ("group", "beam")),
            P(("group", "chan", "tm"), None),
        ),
        out_specs=(
            P(("group", "chan", "tm"), None, "beam", None),
            P(("group", "chan", "tm"), None, "beam"),
            P(("group", "chan", "tm"), "beam", None),
        ),
        check_vma=False,
    )
```
